32 devices in a mesh: space: 16 (over z, y, x), sub: 2 (over core).
Axes of the slice: x: 2, y: 2, z: 4, core: 2. Of those that a mesh axis runs over, the one named last changes fastest.
Arguments:
- fluid_state: float32 [8, 65536], P(None, 'space'), may hold values from 0 to 1
- sphere_state: float32 [7, 65536], P(None, 'space'), may hold values from 0 to 1
- sphere_offset: float32 [3, 65536], P(None, 'space'), may hold values from -1 to 1
- tile_list: int32 [4096, 2], P(('space', 'sub')), may hold values from 0 to 31, as said below
- tile_count: int32 [32], P(('space', 'sub')), may hold values from 32 to 128, as said below
- clump_ids: int32 [65536], P('space'), may hold values from 0 to 127, as said below
- clump_state: float32 [6, 2048], P(None, 'space'), may hold values from -6 to 6
- clump_inverse: float32 [4, 2048], P(None, 'space'), may hold values from 0.02 to 0.2
Outputs:
- clump_velocity: float32 [6, 2048], P(None, 'space')
- sphere_velocity: float32 [3, 65536], P(None, 'space')
The draws below stay inside these ranges and needn't reach their ends.
Inputs may be any that keep to these rules, and one draw needn't show every extreme that they name: `tile_list`: within a domain the 256 slots of its two devices name distinct pairs; the first entry is below 32, the second below 32. `tile_count`: some device's list is full in every draw. `clump_ids`: among the spheres sent to one owner from all domains, each clump id names exactly 32 spheres.
All inputs are finite; a program needn't handle non-finite values.
Results may differ from the reference program's by a relative error of at most 0.0003.
Values sent between devices are 32-bit elements; how exact they have to be, the bound alone decides.
No kernel may reach another device: no remote copies, remote signals or barrier semaphores. Data moves between devices by JAX's collectives and lax.ppermute only.
A program may use at most 64 MiB of HBM per device.

```python
import math
import jax
import jax.numpy as jnp
from jax import lax

TILE = 128
SPC = 32
SLOT = 256
FLUID_DEV = 4096
TILES = 128
SPH_DEV = 4096
CL_DEV = 128
SPHERES = 65536
CLUMPS = 2048
FLUID = 65536
N_SPACE = 16
N_SUB = 2


def draw_tile_list(key, part):
    fluid_tiles = FLUID_DEV // TILE
    pair_count = SPH_DEV // TILE * fluid_tiles

    def one_domain(domain):
        domain_key = jax.random.fold_in(key, domain)
        middle = 1 + jax.random.permutation(jax.random.fold_in(domain_key, 1), pair_count - 2)[:N_SUB * TILES - 2]
        chosen = jnp.concatenate([jnp.array([0, pair_count - 1], jnp.int32), middle.astype(jnp.int32)])
        chosen = chosen[jax.random.permutation(jax.random.fold_in(domain_key, 2), N_SUB * TILES)]
        return jnp.stack([chosen // fluid_tiles, chosen % fluid_tiles], axis=1)
    domain_lists = jax.vmap(one_domain)(jnp.arange(N_SPACE))
    return domain_lists.reshape(N_SPACE * N_SUB * TILES, 2).astype(jnp.int32)


def draw_tile_count(key, part):
    first_draw = jax.random.randint(jax.random.fold_in(key, 1), (N_SPACE * N_SUB,), 0, TILES * 3 // 4)
    second_draw = jax.random.randint(jax.random.fold_in(key, 2), (N_SPACE * N_SUB,), 0, TILES * 3 // 4)
    counts_drawn = TILES // 4 + first_draw * second_draw // TILES
    busiest = jax.random.randint(jax.random.fold_in(key, 3), (), 0, N_SPACE * N_SUB)
    return jnp.where(jnp.arange(N_SPACE * N_SUB) == busiest, TILES, counts_drawn).astype(jnp.int32)


def draw_clump_ids(key, part):

    def one_owner(owner):
        return jax.random.permutation(jax.random.fold_in(key, owner), SPH_DEV) // SPC
    owner_table = jax.vmap(one_owner)(jnp.arange(N_SPACE))
    return owner_table.reshape(N_SPACE, N_SPACE, SLOT).transpose(1, 0, 2).reshape(SPHERES).astype(jnp.int32)


def shard_levels(key, shape, shards, low, largest):
    gain, own = 1.0, jax.random.fold_in(key, 6)
    for position, shards_of in shards:
        draws = jnp.exp(jax.random.uniform(jax.random.fold_in(own, position), (shards_of,), jnp.float32, low / len(shards), largest / len(shards)))
        gain = gain * jnp.repeat(draws, shape[position] // shards_of).reshape([-1 if axis == position else 1 for axis in range(len(shape))])
    return gain


def noise(key, dims, width, limit, split=(), kind=jnp.bfloat16):
    values = width * jax.random.normal(key, dims, jnp.float32)
    if split:
        values = values * shard_levels(key, dims, split, -0.22, 0.18)
    return jnp.clip(values, -limit, limit).astype(kind)


def setup_inputs(seed: int = 0) -> dict:
    keys = jax.random.split(jax.random.key(seed), 9)
    fluid_state = jnp.clip(1.0 * jax.random.uniform(keys[0], (8, FLUID), jnp.float32) ** shard_levels(keys[0], (8, FLUID), ((1, 16),), -0.2, 0.2), 0.0, 1.0)
    sphere_state = jnp.clip(1.0 * jax.random.uniform(keys[1], (7, SPHERES), jnp.float32) ** shard_levels(keys[1], (7, SPHERES), ((1, 16),), -0.2, 0.2), 0.0, 1.0)
    sphere_offset = jnp.clip(jax.random.uniform(keys[2], (3, SPHERES), jnp.float32, -1.0, 1.0) * shard_levels(keys[2], (3, SPHERES), ((1, 16),), -0.4, 0.0), -1.0, 1.0)
    tile_list = draw_tile_list(jax.random.fold_in(keys[8], 71), 0)
    tile_count = draw_tile_count(jax.random.fold_in(keys[8], 71), 0)
    clump_ids = draw_clump_ids(jax.random.fold_in(keys[8], 71), 0)
    clump_state = noise(keys[6], (6, CLUMPS), 1.0, 6.0, ((1, 16),), jnp.float32)
    clump_inverse = jnp.clip(jnp.exp(math.log(0.2) - 2.3025851 * jax.random.uniform(keys[7], (4, CLUMPS), jnp.float32) ** shard_levels(keys[7], (4, CLUMPS), ((1, 16),), -0.2, 0.2)), 0.02, 0.2)
    return {"fluid_state": fluid_state, "sphere_state": sphere_state, "sphere_offset": sphere_offset, "tile_list": tile_list, "tile_count": tile_count, "clump_ids": clump_ids, "clump_state": clump_state, "clump_inverse": clump_inverse}


support_radius = 0.5
press_coef = 4.0
visc_coef = 1.0
gravity_step = 0.1

def cross_rows(left, right):
    return jnp.stack([left[1] * right[2] - left[2] * right[1], left[2] * right[0] - left[0] * right[2], left[0] * right[1] - left[1] * right[0]], axis=0)

def tile_force(fluid_state, sphere_state, sphere_tile, fluid_tile, tile_width):
    spheres = lax.dynamic_slice_in_dim(sphere_state, (sphere_tile * tile_width).astype(jnp.int32), tile_width, 1)
    fluid = lax.dynamic_slice_in_dim(fluid_state, (fluid_tile * tile_width).astype(jnp.int32), tile_width, 1)
    separation = spheres[0:3, :, None] - fluid[0:3, None, :]
    distance = jnp.sqrt(lax.optimization_barrier(jnp.sum(separation * separation, axis=0)))
    falloff = jnp.maximum(1.0 - distance / support_radius, 0.0)
    weight = falloff * falloff * falloff * fluid[7][None, :]
    pressure = press_coef * (spheres[6][:, None] + fluid[6][None, :]) * weight
    repulsion = lax.optimization_barrier(jnp.sum(pressure[None, :, :] * separation, axis=2))
    drag = lax.optimization_barrier(jnp.sum(weight[None, :, :] * (fluid[3:6, None, :] - spheres[3:6, :, None]), axis=2))
    return repulsion + visc_coef * drag

def add_tile(forces, fluid_state, sphere_state, pair, tile_width):
    term = tile_force(fluid_state, sphere_state, pair[0], pair[1], tile_width)
    first_col = (pair[0] * tile_width).astype(jnp.int32)
    current = lax.dynamic_slice_in_dim(forces, first_col, tile_width, 1)
    return lax.dynamic_update_slice_in_dim(forces, current + term, first_col, 1)

def domain_forces(fluid_state, sphere_state, tile_list, tile_count):
    forces = jnp.zeros((3, SPH_DEV), jnp.float32)
    for sub_core in range(N_SUB):

        def accumulate(entry_number, forces, sub_core=sub_core):
            return add_tile(forces, fluid_state, sphere_state, tile_list[sub_core * TILES + entry_number], TILE)
        forces = lax.fori_loop(0, tile_count[sub_core], accumulate, forces)
    return forces

def reference(fluid_state, sphere_state, sphere_offset, tile_list, tile_count, clump_ids, clump_state, clump_inverse):
    fluid_blocks = fluid_state.reshape(8, N_SPACE, FLUID_DEV).transpose(1, 0, 2)
    sphere_blocks = sphere_state.reshape(7, N_SPACE, SPH_DEV).transpose(1, 0, 2)
    list_blocks = tile_list.reshape(N_SPACE, N_SUB * TILES, 2)
    count_blocks = tile_count.reshape(N_SPACE, N_SUB)
    forces = lax.map(lambda group: domain_forces(group[0], group[1], group[2], group[3]), (fluid_blocks, sphere_blocks, list_blocks, count_blocks))
    forces = forces.transpose(1, 0, 2).reshape(3, SPHERES)
    sphere_loads = jnp.concatenate([forces, cross_rows(sphere_offset, forces)], axis=0)
    owner = jnp.arange(SPHERES, dtype=jnp.int32) // SLOT % N_SPACE
    global_ids = (owner * CL_DEV + clump_ids).astype(jnp.int32)
    totals = jax.ops.segment_sum(sphere_loads.T, global_ids, num_segments=CLUMPS).T
    gravity_pull = jnp.array([0.0, 0.0, -gravity_step], jnp.float32)[:, None]
    linear = clump_state[0:3] + clump_inverse[0:1] * totals[0:3] + gravity_pull
    angular = clump_state[3:6] + clump_inverse[1:4] * totals[3:6]
    clump_velocity = jnp.concatenate([linear, angular], axis=0)
    picked = jnp.take(clump_velocity, global_ids, axis=1)
    sphere_velocity = picked[0:3] + cross_rows(picked[3:6], sphere_offset)
    return (clump_velocity, sphere_velocity)
```

```python
import functools
import math

import jax
import jax.numpy as jnp
from jax import lax
from jax.experimental import pallas as pl
from jax.experimental.pallas import tpu as pltpu
from jax.sharding import PartitionSpec as P

TILE = 128
SLOT = 256
UNROLL = 4

support_radius = 0.5
press_coef = 4.0
visc_coef = 1.0
gravity_step = 0.1

f32 = jnp.float32
bf16 = jnp.bfloat16


def split_two(value):
    high = value.astype(bf16)
    return high, (value - high.astype(f32)).astype(bf16)


def cross(left, right):
    return [
        left[1] * right[2] - left[2] * right[1],
        left[2] * right[0] - left[0] * right[2],
        left[0] * right[1] - left[1] * right[0],
    ]


def group_of(owners):
    return math.gcd(owners, 16)


def loads_kernel(
    count_ref, list_ref, fluid_ref, sphere_ref, offset_ref, ids_ref, out_ref,
    place_ref, wide_ref, terms_ref, weight_ref, acc_ref,
):
    fluid_tiles = fluid_ref.shape[1] // TILE
    spheres = sphere_ref.shape[1]
    clumps = out_ref.shape[1]
    owners = out_ref.shape[0] // 6

    place_ref[...] = sphere_ref[0:3, :] * (1.0 / support_radius) - 1.0
    acc_ref[...] = jnp.zeros_like(acc_ref)
    weight_ref[...] = jnp.zeros_like(weight_ref)

    @pl.loop(0, fluid_tiles)
    def _(tile):
        cols = pl.ds(pl.multiple_of(tile * TILE, TILE), TILE)
        state = fluid_ref[:, cols]
        row = lax.broadcasted_iota(jnp.int32, state.shape, 0)
        state = jnp.where(row < 3, state * (1.0 / support_radius) - 1.0, state)
        mass = state[7:8]
        first = jnp.where(row < 7, state * mass, state)
        second = jnp.where(row < 3, state * (mass * state[6:7]), 0.0)
        high, low = split_two(jnp.concatenate([first, second], axis=0))
        both = jnp.concatenate([high, low], axis=0)
        terms_ref[tile] = jnp.concatenate([both, both], axis=1)
        turned = state.T
        for k in range(3):
            wide_ref[k, cols, :] = jnp.broadcast_to(turned[:, k : k + 1], (TILE, TILE))

    def pair_weights(slot, part):
        a = list_ref[0, slot]
        b = list_ref[1, slot]
        cols = pl.ds(pl.multiple_of(a * TILE, TILE), TILE)
        rows = pl.ds(pl.multiple_of(b * TILE, TILE), TILE)
        dx = place_ref[0:1, cols] - wide_ref[0, rows, :]
        dy = place_ref[1:2, cols] - wide_ref[1, rows, :]
        dz = place_ref[2:3, cols] - wide_ref[2, rows, :]
        square = jnp.maximum(dx * dx + dy * dy + dz * dz, 1e-30)
        falloff = jnp.maximum(1.0 - square * lax.rsqrt(square), 0.0)
        high, low = split_two(falloff * falloff * falloff)
        weight_ref[part, 0:TILE, :] = high
        weight_ref[part, TILE:, :] = low

    def add_sums(slot, part, live):
        a = list_ref[0, slot]
        b = list_ref[1, slot]
        cols = pl.ds(pl.multiple_of(a * TILE, TILE), TILE)
        sums = jnp.dot(terms_ref[b], weight_ref[part], preferred_element_type=f32)
        acc_ref[:, cols] += live * (sums[0:16] + sums[16:32])

    count = count_ref[0]
    trips = (count + UNROLL - 1) // UNROLL

    @pl.loop(0, trips + 1)
    def _(trip):
        for part in range(UNROLL):
            slot = (trip - 1) * UNROLL + part
            live = jnp.where((slot >= 0) & (slot < count), 1.0, 0.0).astype(f32)
            add_sums(jnp.maximum(slot, 0), part, live)
        for part in range(UNROLL):
            slot = jnp.minimum(trip * UNROLL + part, list_ref.shape[1] - 1)
            pair_weights(slot, part)

    group = group_of(owners)
    width = group * SLOT

    @pl.loop(0, owners // group)
    def _(block):
        cols = pl.ds(pl.multiple_of(block * width, width), width)
        acc = acc_ref[:, cols]
        place = place_ref[:, cols]
        sphere = sphere_ref[:, cols]
        offset = offset_ref[:, cols]
        total = acc[7:8]
        pull = total * place - acc[0:3]
        press = acc[6:7] * place - acc[8:11]
        scale = press_coef * support_radius
        force = scale * (sphere[6:7] * pull + press) + visc_coef * (acc[3:6] - total * sphere[3:6])
        force = [force[k : k + 1] for k in range(3)]
        turn = cross([offset[k : k + 1] for k in range(3)], force)
        loads = jnp.concatenate(force + turn + [jnp.zeros_like(force[0])] * 2, axis=0)
        high, low = split_two(loads)
        both = jnp.concatenate([high, low], axis=0)
        column = lax.broadcasted_iota(jnp.int32, (clumps, SLOT), 0)
        results = []
        for k in range(group):
            here = pl.ds(pl.multiple_of(block * width + k * SLOT, SLOT), SLOT)
            one_hot = jnp.where(column == ids_ref[:, here], 1.0, 0.0).astype(bf16)
            sums = lax.dot_general(
                both[:, k * SLOT : (k + 1) * SLOT], one_hot, (((1,), (1,)), ((), ())),
                preferred_element_type=f32,
            )
            results.append((sums[0:8] + sums[8:16])[0:6])
        start = pl.multiple_of(block * (6 * group), math.gcd(6 * group, 8))
        out_ref[pl.ds(start, 6 * group), :] = jnp.concatenate(results, axis=0)


def velocity_kernel(totals_ref, state_ref, inverse_ref, offset_ref, ids_ref, clump_ref, sphere_ref, own_ref):
    owners, _, clumps = state_ref.shape
    group = group_of(owners)
    row = lax.broadcasted_iota(jnp.int32, (6, clumps), 0)
    gravity = jnp.where(row == 2, -gravity_step, 0.0)
    me = lax.axis_index("space")

    @pl.loop(0, owners // group)
    def _(block):
        start = pl.multiple_of(block * (6 * group), math.gcd(6 * group, 8))
        totals = totals_ref[pl.ds(start, 6 * group), :]
        for k in range(group):
            owner = block * group + k
            inverse = inverse_ref[owner]
            factor = jnp.concatenate([inverse[0:1]] * 3 + [inverse[1:4]], axis=0)
            velocity = state_ref[owner] + factor * totals[6 * k : 6 * k + 6] + gravity
            own_ref[owner] = velocity
            high, low = split_two(jnp.concatenate([velocity, jnp.zeros((2, clumps), f32)], axis=0))
            both = jnp.concatenate([high, low], axis=0)
            here = pl.ds(pl.multiple_of(owner * SLOT, SLOT), SLOT)
            column = lax.broadcasted_iota(jnp.int32, (clumps, SLOT), 0)
            one_hot = jnp.where(column == ids_ref[:, here], 1.0, 0.0).astype(bf16)
            picked = jnp.dot(both, one_hot, preferred_element_type=f32)
            picked = picked[0:8] + picked[8:16]
            offset = offset_ref[:, here]
            turn = cross([picked[3 + i : 4 + i] for i in range(3)], [offset[i : i + 1] for i in range(3)])
            sphere_ref[:, here] = picked[0:3] + jnp.concatenate(turn, axis=0)

    clump_ref[...] = own_ref[me]


def per_device(
    fluid_state, sphere_state, sphere_offset, tile_list, tile_count, clump_ids, clump_state, clump_inverse
):
    owners = lax.axis_size("space")
    spheres = sphere_state.shape[1]
    fluid = fluid_state.shape[1]
    clumps = clump_state.shape[1]
    ids = clump_ids.reshape(1, spheres)
    vmem = pl.BlockSpec(memory_space=pltpu.VMEM)
    smem = pl.BlockSpec(memory_space=pltpu.SMEM)

    all_state = lax.all_gather(clump_state, "space", axis=0)
    all_inverse = lax.all_gather(clump_inverse, "space", axis=0)

    partial = pl.pallas_call(
        loads_kernel,
        out_shape=jax.ShapeDtypeStruct((owners * 6, clumps), f32),
        in_specs=[smem, smem, vmem, vmem, vmem, vmem],
        out_specs=vmem,
        scratch_shapes=[
            pltpu.VMEM((3, spheres), f32),
            pltpu.VMEM((3, fluid, TILE), f32),
            pltpu.VMEM((fluid // TILE, 32, 2 * TILE), bf16),
            pltpu.VMEM((UNROLL, 2 * TILE, TILE), bf16),
            pltpu.VMEM((16, spheres), f32),
        ],
        compiler_params=pltpu.CompilerParams(vmem_limit_bytes=48 * 1024 * 1024),
        name="clump_loads",
    )(tile_count, tile_list.T, fluid_state, sphere_state, sphere_offset, ids)

    totals = lax.psum(partial, ("space", "sub"))

    velocity, sphere_velocity = pl.pallas_call(
        velocity_kernel,
        out_shape=(
            jax.ShapeDtypeStruct((6, clumps), f32),
            jax.ShapeDtypeStruct((3, spheres), f32),
        ),
        in_specs=[vmem] * 5,
        out_specs=(vmem, vmem),
        scratch_shapes=[pltpu.VMEM((owners, 6, clumps), f32)],
        compiler_params=pltpu.CompilerParams(vmem_limit_bytes=48 * 1024 * 1024),
        name="velocities",
    )(totals, all_state, all_inverse, sphere_offset, ids)
    return velocity, sphere_velocity


def solution(mesh):
    in_specs = (
        P(None, "space"),
        P(None, "space"),
        P(None, "space"),
        P(("space", "sub"), None),
        P(("space", "sub")),
        P("space"),
        P(None, "space"),
        P(None, "space"),
    )
    out_specs = (P(None, "space"), P(None, "space"))
    return jax.shard_map(
        per_device, mesh=mesh, in_specs=in_specs, out_specs=out_specs, check_vma=False
    )
```

```python
import functools
import math

import jax
import jax.numpy as jnp
from jax import lax
from jax.experimental import pallas as pl
from jax.experimental.pallas import tpu as pltpu
from jax.sharding import PartitionSpec as P

TILE = 128
SLOT = 256
UNROLL = 4

support_radius = 0.5
press_coef = 4.0
visc_coef = 1.0
gravity_step = 0.1

f32 = jnp.float32
bf16 = jnp.bfloat16


def split_two(value):
    high = value.astype(bf16)
    return high, (value - high.astype(f32)).astype(bf16)


def cross(left, right):
    return [
        left[1] * right[2] - left[2] * right[1],
        left[2] * right[0] - left[0] * right[2],
        left[0] * right[1] - left[1] * right[0],
    ]


def group_of(owners):
    return math.gcd(owners, 16)


def loads_kernel(
    count_hbm, list_hbm, fluid_hbm, sphere_hbm, offset_hbm, ids_hbm, out_ref,
    count_ref, list_ref, fluid_ref, sphere_ref, offset_ref, ids_ref, arrived,
    place_ref, wide_ref, terms_ref, weight_ref, acc_ref,
):
    fluid_tiles = fluid_ref.shape[1] // TILE
    clumps = out_ref.shape[2]
    owners = out_ref.shape[0] // 2

    pairs = (
        (fluid_hbm, fluid_ref),
        (sphere_hbm, sphere_ref),
        (list_hbm, list_ref),
        (count_hbm, count_ref),
        (offset_hbm, offset_ref),
        (ids_hbm, ids_ref),
    )
    copies = [
        pltpu.make_async_copy(source, target, arrived.at[k]) for k, (source, target) in enumerate(pairs)
    ]
    for copy in copies:
        copy.start()

    acc_ref[...] = jnp.zeros_like(acc_ref)
    weight_ref[...] = jnp.zeros_like(weight_ref)
    copies[0].wait()

    @pl.loop(0, fluid_tiles, unroll=8)
    def _(tile):
        cols = pl.ds(pl.multiple_of(tile * TILE, TILE), TILE)
        state = fluid_ref[:, cols]
        row = lax.broadcasted_iota(jnp.int32, state.shape, 0)
        state = jnp.where(row < 3, state * (1.0 / support_radius) - 1.0, state)
        mass = state[7:8]
        first = jnp.where(row < 7, state * mass, state)
        second = jnp.where(row < 3, state * (mass * state[6:7]), 0.0)
        high, low = split_two(jnp.concatenate([first, second], axis=0))
        both = jnp.concatenate([high, low], axis=0)
        terms_ref[tile] = jnp.concatenate([both, both], axis=1)
        turned = state.T
        for k in range(3):
            wide_ref[k, cols, :] = jnp.broadcast_to(turned[:, k : k + 1], (TILE, TILE))

    copies[1].wait()
    place_ref[...] = sphere_ref[0:3, :] * (1.0 / support_radius) - 1.0
    copies[2].wait()
    copies[3].wait()

    def pair_weights(slot, part):
        a = list_ref[0, slot]
        b = list_ref[1, slot]
        cols = pl.ds(pl.multiple_of(a * TILE, TILE), TILE)
        rows = pl.ds(pl.multiple_of(b * TILE, TILE), TILE)
        dx = place_ref[0:1, cols] - wide_ref[0, rows, :]
        dy = place_ref[1:2, cols] - wide_ref[1, rows, :]
        dz = place_ref[2:3, cols] - wide_ref[2, rows, :]
        square = jnp.maximum(dx * dx + dy * dy + dz * dz, 1e-30)
        falloff = jnp.maximum(1.0 - square * lax.rsqrt(square), 0.0)
        high, low = split_two(falloff * falloff * falloff)
        weight_ref[part, 0:TILE, :] = high
        weight_ref[part, TILE:, :] = low

    def add_sums(slot, part, live):
        a = list_ref[0, slot]
        b = list_ref[1, slot]
        cols = pl.ds(pl.multiple_of(a * TILE, TILE), TILE)
        sums = jnp.dot(terms_ref[b], weight_ref[part], preferred_element_type=f32)
        acc_ref[:, cols] += live * (sums[0:16] + sums[16:32])

    count = count_ref[0]
    trips = (count + UNROLL - 1) // UNROLL

    @pl.loop(0, trips + 1)
    def _(trip):
        for part in range(UNROLL):
            slot = (trip - 1) * UNROLL + part
            live = jnp.where((slot >= 0) & (slot < count), 1.0, 0.0).astype(f32)
            add_sums(jnp.maximum(slot, 0), part, live)
        for part in range(UNROLL):
            slot = jnp.minimum(trip * UNROLL + part, list_ref.shape[1] - 1)
            pair_weights(slot, part)

    copies[4].wait()
    copies[5].wait()
    group = group_of(owners)
    width = group * SLOT

    @pl.loop(0, owners // group)
    def _(block):
        cols = pl.ds(pl.multiple_of(block * width, width), width)
        acc = acc_ref[:, cols]
        place = place_ref[:, cols]
        sphere = sphere_ref[:, cols]
        offset = offset_ref[:, cols]
        total = acc[7:8]
        pull = total * place - acc[0:3]
        press = acc[6:7] * place - acc[8:11]
        scale = press_coef * support_radius
        force = scale * (sphere[6:7] * pull + press) + visc_coef * (acc[3:6] - total * sphere[3:6])
        force = [force[k : k + 1] for k in range(3)]
        turn = cross([offset[k : k + 1] for k in range(3)], force)
        loads = jnp.concatenate(force + turn + [jnp.zeros_like(force[0])] * 2, axis=0)
        high, low = split_two(loads)
        both = jnp.concatenate([high, low], axis=0)
        column = lax.broadcasted_iota(jnp.int32, (clumps, SLOT), 0)
        for k in range(group):
            here = pl.ds(pl.multiple_of(block * width + k * SLOT, SLOT), SLOT)
            one_hot = jnp.where(column == ids_ref[:, here], 1.0, 0.0).astype(bf16)
            sums = lax.dot_general(
                both[:, k * SLOT : (k + 1) * SLOT], one_hot, (((1,), (1,)), ((), ())),
                preferred_element_type=f32,
            )
            sums = sums[0:8] + sums[8:16]
            out_ref[2 * (block * group + k)] = sums[0:3]
            out_ref[2 * (block * group + k) + 1] = sums[3:6]


def update_kernel(arrived_ref, state_ref, inverse_ref, out_ref):
    totals = jnp.sum(arrived_ref[...], axis=0)
    state = state_ref[...]
    inverse = inverse_ref[...]
    row = lax.broadcasted_iota(jnp.int32, totals.shape, 0)
    linear = state[0:3] + inverse[0:1] * totals + jnp.where(row == 2, -gravity_step, 0.0)
    angular = state[3:6] + inverse[1:4] * totals
    rows = jnp.where(lax.axis_index("sub") == 0, linear, angular)
    out_ref[...] = jnp.broadcast_to(rows[None], out_ref.shape)


def velocity_kernel(velocity_ref, offset_ref, ids_ref, clump_ref, sphere_ref):
    owners = velocity_ref.shape[0] // 2
    clumps = velocity_ref.shape[2]
    group = group_of(owners)
    me = lax.axis_index("space")

    @pl.loop(0, owners // group)
    def _(block):
        for k in range(group):
            owner = block * group + k
            rows = [velocity_ref[2 * owner], velocity_ref[2 * owner + 1], jnp.zeros((2, clumps), f32)]
            high, low = split_two(jnp.concatenate(rows, axis=0))
            both = jnp.concatenate([high, low], axis=0)
            here = pl.ds(pl.multiple_of(owner * SLOT, SLOT), SLOT)
            column = lax.broadcasted_iota(jnp.int32, (clumps, SLOT), 0)
            one_hot = jnp.where(column == ids_ref[:, here], 1.0, 0.0).astype(bf16)
            picked = jnp.dot(both, one_hot, preferred_element_type=f32)
            picked = picked[0:8] + picked[8:16]
            offset = offset_ref[:, here]
            turn = cross([picked[3 + i : 4 + i] for i in range(3)], [offset[i : i + 1] for i in range(3)])
            sphere_ref[:, here] = picked[0:3] + jnp.concatenate(turn, axis=0)

    clump_ref[0:3, :] = velocity_ref[2 * me]
    clump_ref[3:6, :] = velocity_ref[2 * me + 1]


def per_device(
    fluid_state, sphere_state, sphere_offset, tile_list, tile_count, clump_ids, clump_state, clump_inverse
):
    owners = lax.axis_size("space")
    devices = owners * lax.axis_size("sub")
    spheres = sphere_state.shape[1]
    fluid = fluid_state.shape[1]
    clumps = clump_state.shape[1]
    slots = tile_list.shape[0]
    ids = clump_ids.reshape(1, spheres)
    vmem = pl.BlockSpec(memory_space=pltpu.VMEM)
    hbm = pl.BlockSpec(memory_space=pltpu.HBM)
    params = pltpu.CompilerParams(vmem_limit_bytes=48 * 1024 * 1024)

    partial = pl.pallas_call(
        loads_kernel,
        out_shape=jax.ShapeDtypeStruct((devices, 3, clumps), f32),
        in_specs=[hbm] * 6,
        out_specs=vmem,
        scratch_shapes=[
            pltpu.SMEM((1,), jnp.int32),
            pltpu.SMEM((2, slots), jnp.int32),
            pltpu.VMEM((8, fluid), f32),
            pltpu.VMEM((7, spheres), f32),
            pltpu.VMEM((3, spheres), f32),
            pltpu.VMEM((1, spheres), jnp.int32),
            pltpu.SemaphoreType.DMA((6,)),
            pltpu.VMEM((3, spheres), f32),
            pltpu.VMEM((3, fluid, TILE), f32),
            pltpu.VMEM((fluid // TILE, 32, 2 * TILE), bf16),
            pltpu.VMEM((UNROLL, 2 * TILE, TILE), bf16),
            pltpu.VMEM((16, spheres), f32),
        ],
        compiler_params=params,
        name="clump_loads",
    )(tile_count, tile_list.T, fluid_state, sphere_state, sphere_offset, ids)

    axes = ("space", "sub")
    arrived = lax.all_to_all(partial, axes, split_axis=0, concat_axis=0, tiled=True)
    rows = pl.pallas_call(
        update_kernel,
        out_shape=jax.ShapeDtypeStruct((devices, 3, clumps), f32),
        in_specs=[vmem] * 3,
        out_specs=vmem,
        compiler_params=params,
        name="clump_update",
    )(arrived, clump_state, clump_inverse)
    velocities = lax.all_to_all(rows, axes, split_axis=0, concat_axis=0, tiled=True)

    return pl.pallas_call(
        velocity_kernel,
        out_shape=(
            jax.ShapeDtypeStruct((6, clumps), f32),
            jax.ShapeDtypeStruct((3, spheres), f32),
        ),
        in_specs=[vmem] * 3,
        out_specs=(vmem, vmem),
        compiler_params=params,
        name="sphere_velocities",
    )(velocities, sphere_offset, ids)


def solution(mesh):
    in_specs = (
        P(None, "space"),
        P(None, "space"),
        P(None, "space"),
        P(("space", "sub"), None),
        P(("space", "sub")),
        P("space"),
        P(None, "space"),
        P(None, "space"),
    )
    out_specs = (P(None, "space"), P(None, "space"))
    return jax.shard_map(
        per_device, mesh=mesh, in_specs=in_specs, out_specs=out_specs, check_vma=False
    )
```

```python
import functools
import math

import jax
import jax.numpy as jnp
from jax import lax
from jax.experimental import pallas as pl
from jax.experimental.pallas import tpu as pltpu
from jax.sharding import PartitionSpec as P

TILE = 128
SLOT = 256
UNROLL = 4
FULL_VMEM = 63 * 1024 * 1024

support_radius = 0.5
press_coef = 4.0
visc_coef = 1.0
gravity_step = 0.1

f32 = jnp.float32
bf16 = jnp.bfloat16


def split_two(value):
    high = value.astype(bf16)
    return high, (value - high.astype(f32)).astype(bf16)


def cross(left, right):
    return [
        left[1] * right[2] - left[2] * right[1],
        left[2] * right[0] - left[0] * right[2],
        left[0] * right[1] - left[1] * right[0],
    ]


def group_of(owners):
    return math.gcd(owners, 16)


def loads_kernel(
    count_hbm, list_hbm, fluid_hbm, sphere_hbm, offset_hbm, ids_hbm, out_ref,
    count_ref, list_ref, fluid_ref, sphere_ref, offset_ref, ids_ref, arrived,
    place_ref, wide_ref, terms_ref, weight_ref, acc_ref,
):
    fluid_tiles = fluid_ref.shape[1] // TILE
    clumps = out_ref.shape[2]
    owners = out_ref.shape[0]

    pairs = (
        (fluid_hbm, fluid_ref),
        (sphere_hbm, sphere_ref),
        (list_hbm, list_ref),
        (count_hbm, count_ref),
        (offset_hbm, offset_ref),
        (ids_hbm, ids_ref),
    )
    copies = [
        pltpu.make_async_copy(source, target, arrived.at[k]) for k, (source, target) in enumerate(pairs)
    ]
    for copy in copies:
        copy.start()

    acc_ref[...] = jnp.zeros_like(acc_ref)
    weight_ref[...] = jnp.zeros_like(weight_ref)
    copies[0].wait()

    @pl.loop(0, fluid_tiles, unroll=8)
    def _(tile):
        cols = pl.ds(pl.multiple_of(tile * TILE, TILE), TILE)
        state = fluid_ref[:, cols]
        row = lax.broadcasted_iota(jnp.int32, state.shape, 0)
        state = jnp.where(row < 3, state * (1.0 / support_radius) - 1.0, state)
        mass = state[7:8]
        first = jnp.where(row < 7, state * mass, state)
        second = jnp.where(row < 3, state * (mass * state[6:7]), 0.0)
        high, low = split_two(jnp.concatenate([first, second], axis=0))
        both = jnp.concatenate([high, low], axis=0)
        terms_ref[tile] = jnp.concatenate([both, both], axis=1)
        turned = state.T
        for k in range(3):
            wide_ref[k, cols, :] = jnp.broadcast_to(turned[:, k : k + 1], (TILE, TILE))

    copies[1].wait()
    place_ref[...] = sphere_ref[0:3, :] * (1.0 / support_radius) - 1.0
    copies[2].wait()
    copies[3].wait()

    def pair_weights(slot, part):
        a = list_ref[0, slot]
        b = list_ref[1, slot]
        cols = pl.ds(pl.multiple_of(a * TILE, TILE), TILE)
        rows = pl.ds(pl.multiple_of(b * TILE, TILE), TILE)
        dx = place_ref[0:1, cols] - wide_ref[0, rows, :]
        dy = place_ref[1:2, cols] - wide_ref[1, rows, :]
        dz = place_ref[2:3, cols] - wide_ref[2, rows, :]
        square = jnp.maximum(dx * dx + dy * dy + dz * dz, 1e-30)
        falloff = jnp.maximum(1.0 - square * lax.rsqrt(square), 0.0)
        high, low = split_two(falloff * falloff * falloff)
        weight_ref[part, 0:TILE, :] = high
        weight_ref[part, TILE:, :] = low

    def add_sums(slot, part, live):
        a = list_ref[0, slot]
        b = list_ref[1, slot]
        cols = pl.ds(pl.multiple_of(a * TILE, TILE), TILE)
        sums = jnp.dot(terms_ref[b], weight_ref[part], preferred_element_type=f32)
        acc_ref[:, cols] += live * (sums[0:16] + sums[16:32])

    count = count_ref[0]
    trips = (count + UNROLL - 1) // UNROLL

    @pl.loop(0, trips + 1)
    def _(trip):
        for part in range(UNROLL):
            slot = (trip - 1) * UNROLL + part
            live = jnp.where((slot >= 0) & (slot < count), 1.0, 0.0).astype(f32)
            add_sums(jnp.maximum(slot, 0), part, live)
        for part in range(UNROLL):
            slot = jnp.minimum(trip * UNROLL + part, list_ref.shape[1] - 1)
            pair_weights(slot, part)

    copies[4].wait()
    copies[5].wait()
    group = group_of(owners)
    width = group * SLOT

    @pl.loop(0, owners // group)
    def _(block):
        cols = pl.ds(pl.multiple_of(block * width, width), width)
        acc = acc_ref[:, cols]
        place = place_ref[:, cols]
        sphere = sphere_ref[:, cols]
        offset = offset_ref[:, cols]
        total = acc[7:8]
        pull = total * place - acc[0:3]
        press = acc[6:7] * place - acc[8:11]
        scale = press_coef * support_radius
        force = scale * (sphere[6:7] * pull + press) + visc_coef * (acc[3:6] - total * sphere[3:6])
        force = [force[k : k + 1] for k in range(3)]
        turn = cross([offset[k : k + 1] for k in range(3)], force)
        loads = jnp.concatenate(force + turn + [jnp.zeros_like(force[0])] * 2, axis=0)
        high, low = split_two(loads)
        both = jnp.concatenate([high, low], axis=0)
        column = lax.broadcasted_iota(jnp.int32, (clumps, SLOT), 0)
        for k in range(group):
            here = pl.ds(pl.multiple_of(block * width + k * SLOT, SLOT), SLOT)
            one_hot = jnp.where(column == ids_ref[:, here], 1.0, 0.0).astype(bf16)
            sums = lax.dot_general(
                both[:, k * SLOT : (k + 1) * SLOT], one_hot, (((1,), (1,)), ((), ())),
                preferred_element_type=f32,
            )
            out_ref[block * group + k] = (sums[0:8] + sums[8:16])[0:6]


def update_kernel(arrived_ref, state_ref, inverse_ref, out_ref):
    totals = jnp.sum(arrived_ref[...], axis=0)
    inverse = inverse_ref[...]
    factor = jnp.concatenate([inverse[0:1]] * 3 + [inverse[1:4]], axis=0)
    row = lax.broadcasted_iota(jnp.int32, totals.shape, 0)
    still = state_ref[...] + jnp.where(row == 2, -gravity_step, 0.0)
    share = factor * totals + still * (1.0 / lax.axis_size("sub"))
    out_ref[...] = jnp.broadcast_to(share[None], out_ref.shape)


def velocity_kernel(shares_ref, offset_ref, ids_ref, clump_ref, sphere_ref, velocity_ref):
    owners, _, clumps = velocity_ref.shape
    group = group_of(owners)

    @pl.loop(0, owners // group)
    def _(block):
        for k in range(group):
            owner = block * group + k
            velocity = shares_ref[2 * owner] + shares_ref[2 * owner + 1]
            velocity_ref[owner] = velocity
            rows = jnp.concatenate([velocity, jnp.zeros((2, clumps), f32)], axis=0)
            both = jnp.concatenate(split_two(rows), axis=0)
            here = pl.ds(pl.multiple_of(owner * SLOT, SLOT), SLOT)
            column = lax.broadcasted_iota(jnp.int32, (clumps, SLOT), 0)
            one_hot = jnp.where(column == ids_ref[:, here], 1.0, 0.0).astype(bf16)
            picked = jnp.dot(both, one_hot, preferred_element_type=f32)
            picked = picked[0:8] + picked[8:16]
            offset = offset_ref[:, here]
            turn = cross([picked[3 + i : 4 + i] for i in range(3)], [offset[i : i + 1] for i in range(3)])
            sphere_ref[:, here] = picked[0:3] + jnp.concatenate(turn, axis=0)

    clump_ref[...] = velocity_ref[lax.axis_index("space")]


def per_device(
    fluid_state, sphere_state, sphere_offset, tile_list, tile_count, clump_ids, clump_state, clump_inverse
):
    owners = lax.axis_size("space")
    devices = owners * lax.axis_size("sub")
    spheres = sphere_state.shape[1]
    fluid = fluid_state.shape[1]
    clumps = clump_state.shape[1]
    slots = tile_list.shape[0]
    ids = clump_ids.reshape(1, spheres)
    vmem = pl.BlockSpec(memory_space=pltpu.VMEM)
    hbm = pl.BlockSpec(memory_space=pltpu.HBM)
    params = pltpu.CompilerParams(vmem_limit_bytes=48 * 1024 * 1024)

    partial = pl.pallas_call(
        loads_kernel,
        out_shape=jax.ShapeDtypeStruct((owners, 6, clumps), f32),
        in_specs=[hbm] * 6,
        out_specs=vmem,
        scratch_shapes=[
            pltpu.SMEM((1,), jnp.int32),
            pltpu.SMEM((2, slots), jnp.int32),
            pltpu.VMEM((8, fluid), f32),
            pltpu.VMEM((7, spheres), f32),
            pltpu.VMEM((3, spheres), f32),
            pltpu.VMEM((1, spheres), jnp.int32),
            pltpu.SemaphoreType.DMA((6,)),
            pltpu.VMEM((3, spheres), f32),
            pltpu.VMEM((3, fluid, TILE), f32),
            pltpu.VMEM((fluid // TILE, 32, 2 * TILE), bf16),
            pltpu.VMEM((UNROLL, 2 * TILE, TILE), bf16),
            pltpu.VMEM((16, spheres), f32),
        ],
        compiler_params=pltpu.CompilerParams(vmem_limit_bytes=FULL_VMEM),
        name="clump_loads",
    )(tile_count, tile_list.T, fluid_state, sphere_state, sphere_offset, ids)

    arrived = lax.all_to_all(partial, "space", split_axis=0, concat_axis=0, tiled=True)
    share = pl.pallas_call(
        update_kernel,
        out_shape=jax.ShapeDtypeStruct((devices, 6, clumps), f32),
        in_specs=[vmem] * 3,
        out_specs=vmem,
        compiler_params=params,
        name="clump_update",
    )(arrived, clump_state, clump_inverse)
    shares = lax.all_to_all(share, ("space", "sub"), split_axis=0, concat_axis=0, tiled=True)

    return pl.pallas_call(
        velocity_kernel,
        out_shape=(
            jax.ShapeDtypeStruct((6, clumps), f32),
            jax.ShapeDtypeStruct((3, spheres), f32),
        ),
        in_specs=[vmem] * 3,
        out_specs=(vmem, vmem),
        scratch_shapes=[pltpu.VMEM((owners, 6, clumps), f32)],
        compiler_params=params,
        name="sphere_velocities",
    )(shares, sphere_offset, ids)


def solution(mesh):
    in_specs = (
        P(None, "space"),
        P(None, "space"),
        P(None, "space"),
        P(("space", "sub"), None),
        P(("space", "sub")),
        P("space"),
        P(None, "space"),
        P(None, "space"),
    )
    out_specs = (P(None, "space"), P(None, "space"))
    return jax.shard_map(
        per_device, mesh=mesh, in_specs=in_specs, out_specs=out_specs, check_vma=False
    )
```

```python
import functools
import math

import jax
import jax.numpy as jnp
from jax import lax
from jax.experimental import pallas as pl
from jax.experimental.pallas import tpu as pltpu
from jax.sharding import PartitionSpec as P

TILE = 128
SLOT = 256
UNROLL = 4
FULL_VMEM = 63 * 1024 * 1024

support_radius = 0.5
press_coef = 4.0
visc_coef = 1.0
gravity_step = 0.1

f32 = jnp.float32
bf16 = jnp.bfloat16


def split_two(value):
    high = value.astype(bf16)
    return high, (value - high.astype(f32)).astype(bf16)


def cross(left, right):
    return [
        left[1] * right[2] - left[2] * right[1],
        left[2] * right[0] - left[0] * right[2],
        left[0] * right[1] - left[1] * right[0],
    ]


def group_of(owners):
    return math.gcd(owners, 16)


def loads_kernel(
    count_hbm, list_hbm, fluid_hbm, sphere_hbm, offset_hbm, ids_hbm, out_ref,
    count_ref, list_ref, fluid_ref, sphere_ref, offset_ref, ids_ref, arrived,
    place_ref, wide_ref, terms_ref, weight_ref, acc_ref,
):
    fluid_tiles = fluid_ref.shape[1] // TILE
    clumps = out_ref.shape[1]
    owners = out_ref.shape[0] // 6

    pairs = (
        (fluid_hbm, fluid_ref),
        (sphere_hbm, sphere_ref),
        (list_hbm, list_ref),
        (count_hbm, count_ref),
        (offset_hbm, offset_ref),
        (ids_hbm, ids_ref),
    )
    copies = [
        pltpu.make_async_copy(source, target, arrived.at[k]) for k, (source, target) in enumerate(pairs)
    ]
    for copy in copies:
        copy.start()

    acc_ref[...] = jnp.zeros_like(acc_ref)
    weight_ref[...] = jnp.zeros_like(weight_ref)
    copies[0].wait()

    @pl.loop(0, fluid_tiles, unroll=8)
    def _(tile):
        cols = pl.ds(pl.multiple_of(tile * TILE, TILE), TILE)
        state = fluid_ref[:, cols]
        row = lax.broadcasted_iota(jnp.int32, state.shape, 0)
        state = jnp.where(row < 3, state * (1.0 / support_radius) - 1.0, state)
        mass = state[7:8]
        first = jnp.where(row < 7, state * mass, state)
        second = jnp.where(row < 3, state * (mass * state[6:7]), 0.0)
        high, low = split_two(jnp.concatenate([first, second], axis=0))
        both = jnp.concatenate([high, low], axis=0)
        terms_ref[tile] = jnp.concatenate([both, both], axis=1)
        turned = state.T
        for k in range(3):
            wide_ref[k, cols, :] = jnp.broadcast_to(turned[:, k : k + 1], (TILE, TILE))

    copies[1].wait()
    place_ref[...] = sphere_ref[0:3, :] * (1.0 / support_radius) - 1.0
    copies[2].wait()
    copies[3].wait()

    def pair_weights(slot, part):
        a = list_ref[0, slot]
        b = list_ref[1, slot]
        cols = pl.ds(pl.multiple_of(a * TILE, TILE), TILE)
        rows = pl.ds(pl.multiple_of(b * TILE, TILE), TILE)
        dx = place_ref[0:1, cols] - wide_ref[0, rows, :]
        dy = place_ref[1:2, cols] - wide_ref[1, rows, :]
        dz = place_ref[2:3, cols] - wide_ref[2, rows, :]
        square = jnp.maximum(dx * dx + dy * dy + dz * dz, 1e-30)
        falloff = jnp.maximum(1.0 - square * lax.rsqrt(square), 0.0)
        high, low = split_two(falloff * falloff * falloff)
        weight_ref[part, 0:TILE, :] = high
        weight_ref[part, TILE:, :] = low

    def add_sums(slot, part, live):
        a = list_ref[0, slot]
        b = list_ref[1, slot]
        cols = pl.ds(pl.multiple_of(a * TILE, TILE), TILE)
        sums = jnp.dot(terms_ref[b], weight_ref[part], preferred_element_type=f32)
        acc_ref[:, cols] += live * (sums[0:16] + sums[16:32])

    count = count_ref[0]
    trips = (count + UNROLL - 1) // UNROLL

    @pl.loop(0, trips + 1)
    def _(trip):
        for part in range(UNROLL):
            slot = (trip - 1) * UNROLL + part
            live = jnp.where((slot >= 0) & (slot < count), 1.0, 0.0).astype(f32)
            add_sums(jnp.maximum(slot, 0), part, live)
        for part in range(UNROLL):
            slot = jnp.minimum(trip * UNROLL + part, list_ref.shape[1] - 1)
            pair_weights(slot, part)

    copies[4].wait()
    copies[5].wait()
    group = group_of(owners)
    width = group * SLOT

    @pl.loop(0, owners // group)
    def _(block):
        cols = pl.ds(pl.multiple_of(block * width, width), width)
        acc = acc_ref[:, cols]
        place = place_ref[:, cols]
        sphere = sphere_ref[:, cols]
        offset = offset_ref[:, cols]
        total = acc[7:8]
        pull = total * place - acc[0:3]
        press = acc[6:7] * place - acc[8:11]
        scale = press_coef * support_radius
        force = scale * (sphere[6:7] * pull + press) + visc_coef * (acc[3:6] - total * sphere[3:6])
        force = [force[k : k + 1] for k in range(3)]
        turn = cross([offset[k : k + 1] for k in range(3)], force)
        loads = jnp.concatenate(force + turn + [jnp.zeros_like(force[0])] * 2, axis=0)
        high, low = split_two(loads)
        both = jnp.concatenate([high, low], axis=0)
        column = lax.broadcasted_iota(jnp.int32, (clumps, SLOT), 0)
        results = []
        for k in range(group):
            here = pl.ds(pl.multiple_of(block * width + k * SLOT, SLOT), SLOT)
            one_hot = jnp.where(column == ids_ref[:, here], 1.0, 0.0).astype(bf16)
            sums = lax.dot_general(
                both[:, k * SLOT : (k + 1) * SLOT], one_hot, (((1,), (1,)), ((), ())),
                preferred_element_type=f32,
            )
            results.append((sums[0:8] + sums[8:16])[0:6])
        start = pl.multiple_of(block * (6 * group), math.gcd(6 * group, 8))
        out_ref[pl.ds(start, 6 * group), :] = jnp.concatenate(results, axis=0)


def velocity_kernel(
    mine_ref, other_ref, state_ref, offset_ref, ids_ref, clump_ref, sphere_ref, velocity_ref
):
    owners, _, clumps = velocity_ref.shape
    group = group_of(owners)
    me = lax.axis_index("space")
    row = lax.broadcasted_iota(jnp.int32, (6, clumps), 0)
    gravity = jnp.where(row == 2, -gravity_step, 0.0)

    @pl.loop(0, owners // group)
    def _(block):
        start = pl.multiple_of(block * (6 * group), math.gcd(6 * group, 8))
        totals = mine_ref[pl.ds(start, 6 * group), :] + other_ref[pl.ds(start, 6 * group), :]
        for k in range(group):
            owner = block * group + k
            state = state_ref[owner ^ me]
            factor = jnp.concatenate([state[6:7]] * 3 + [state[7:10]], axis=0)
            velocity = state[0:6] + factor * totals[6 * k : 6 * k + 6] + gravity
            velocity_ref[owner] = velocity
            rows = jnp.concatenate([velocity, jnp.zeros((2, clumps), f32)], axis=0)
            both = jnp.concatenate(split_two(rows), axis=0)
            here = pl.ds(pl.multiple_of(owner * SLOT, SLOT), SLOT)
            column = lax.broadcasted_iota(jnp.int32, (clumps, SLOT), 0)
            one_hot = jnp.where(column == ids_ref[:, here], 1.0, 0.0).astype(bf16)
            picked = jnp.dot(both, one_hot, preferred_element_type=f32)
            picked = picked[0:8] + picked[8:16]
            offset = offset_ref[:, here]
            turn = cross([picked[3 + i : 4 + i] for i in range(3)], [offset[i : i + 1] for i in range(3)])
            sphere_ref[:, here] = picked[0:3] + jnp.concatenate(turn, axis=0)

    clump_ref[...] = velocity_ref[me]


def swap(value, axis, bit):
    size = lax.axis_size(axis)
    return lax.ppermute(value, axis, [(k, k ^ bit) for k in range(size)])


def per_device(
    fluid_state, sphere_state, sphere_offset, tile_list, tile_count, clump_ids, clump_state, clump_inverse
):
    owners = lax.axis_size("space")
    spheres = sphere_state.shape[1]
    fluid = fluid_state.shape[1]
    clumps = clump_state.shape[1]
    slots = tile_list.shape[0]
    ids = clump_ids.reshape(1, spheres)
    vmem = pl.BlockSpec(memory_space=pltpu.VMEM)
    hbm = pl.BlockSpec(memory_space=pltpu.HBM)
    params = pltpu.CompilerParams(vmem_limit_bytes=48 * 1024 * 1024)

    partial = pl.pallas_call(
        loads_kernel,
        out_shape=jax.ShapeDtypeStruct((owners * 6, clumps), f32),
        in_specs=[hbm] * 6,
        out_specs=vmem,
        scratch_shapes=[
            pltpu.SMEM((1,), jnp.int32),
            pltpu.SMEM((2, slots), jnp.int32),
            pltpu.VMEM((8, fluid), f32),
            pltpu.VMEM((7, spheres), f32),
            pltpu.VMEM((3, spheres), f32),
            pltpu.VMEM((1, spheres), jnp.int32),
            pltpu.SemaphoreType.DMA((6,)),
            pltpu.VMEM((3, spheres), f32),
            pltpu.VMEM((3, fluid, TILE), f32),
            pltpu.VMEM((fluid // TILE, 32, 2 * TILE), bf16),
            pltpu.VMEM((UNROLL, 2 * TILE, TILE), bf16),
            pltpu.VMEM((16, spheres), f32),
        ],
        compiler_params=pltpu.CompilerParams(vmem_limit_bytes=FULL_VMEM),
        name="clump_loads",
    )(tile_count, tile_list.T, fluid_state, sphere_state, sphere_offset, ids)

    state = jnp.concatenate([clump_state, clump_inverse], axis=0)[None]
    other = swap(partial, "sub", 1)
    bit = 1
    while bit < owners:
        state = jnp.concatenate([state, swap(state, "space", bit)], axis=0)
        partial = partial + other
        other = swap(partial, "space", bit)
        bit *= 2

    return pl.pallas_call(
        velocity_kernel,
        out_shape=(
            jax.ShapeDtypeStruct((6, clumps), f32),
            jax.ShapeDtypeStruct((3, spheres), f32),
        ),
        in_specs=[vmem] * 5,
        out_specs=(vmem, vmem),
        scratch_shapes=[pltpu.VMEM((owners, 6, clumps), f32)],
        compiler_params=params,
        name="sphere_velocities",
    )(partial, other, state, sphere_offset, ids)


def solution(mesh):
    in_specs = (
        P(None, "space"),
        P(None, "space"),
        P(None, "space"),
        P(("space", "sub"), None),
        P(("space", "sub")),
        P("space"),
        P(None, "space"),
        P(None, "space"),
    )
    out_specs = (P(None, "space"), P(None, "space"))
    return jax.shard_map(
        per_device, mesh=mesh, in_specs=in_specs, out_specs=out_specs, check_vma=False
    )
```

```python
import functools
import math

import jax
import jax.numpy as jnp
from jax import lax
from jax.experimental import pallas as pl
from jax.experimental.pallas import tpu as pltpu
from jax.sharding import PartitionSpec as P

TILE = 128
SLOT = 256
UNROLL = 8

support_radius = 0.5
press_coef = 4.0
visc_coef = 1.0
gravity_step = 0.1

f32 = jnp.float32
bf16 = jnp.bfloat16


def split_two(value):
    high = value.astype(bf16)
    return high, (value - high.astype(f32)).astype(bf16)


def cross(left, right):
    return [
        left[1] * right[2] - left[2] * right[1],
        left[2] * right[0] - left[0] * right[2],
        left[0] * right[1] - left[1] * right[0],
    ]


def put_rows(ref, owner, rows, clumps):
    for half in range(2):
        for k in range(3):
            ref[2 * owner + half, :, k * clumps : (k + 1) * clumps] = rows[3 * half + k : 3 * half + k + 1]


def get_rows(ref, owner, clumps):
    return [
        ref[2 * owner + half, :, k * clumps : (k + 1) * clumps] for half in range(2) for k in range(3)
    ]


def group_of(owners):
    return math.gcd(owners, 16)


def loads_kernel(
    count_ref, list_hbm, fluid_hbm, sphere_hbm, offset_hbm, ids_hbm, out_ref,
    list_ref, fluid_ref, sphere_ref, offset_ref, ids_ref, arrived,
    place_ref, wide_ref, terms_ref, weight_ref, acc_ref,
):
    fluid_tiles = fluid_ref.shape[1] // TILE
    clumps = out_ref.shape[2] // 3
    owners = out_ref.shape[0] // 2

    pairs = (
        (fluid_hbm, fluid_ref),
        (sphere_hbm, sphere_ref),
        (list_hbm, list_ref),
        (offset_hbm, offset_ref),
        (ids_hbm, ids_ref),
    )
    copies = [
        pltpu.make_async_copy(source, target, arrived.at[k]) for k, (source, target) in enumerate(pairs)
    ]
    for copy in copies:
        copy.start()

    acc_ref[...] = jnp.zeros_like(acc_ref)
    copies[0].wait()

    @pl.loop(0, fluid_tiles, unroll=8)
    def _(tile):
        cols = pl.ds(pl.multiple_of(tile * TILE, TILE), TILE)
        state = fluid_ref[:, cols]
        row = lax.broadcasted_iota(jnp.int32, state.shape, 0)
        state = jnp.where(row < 3, state * (1.0 / support_radius) - 1.0, state)
        mass = state[7:8]
        first = jnp.where(row < 7, state * mass, state)
        second = jnp.where(row < 3, state * (mass * state[6:7]), 0.0)
        high, low = split_two(jnp.concatenate([first, second], axis=0))
        both = jnp.concatenate([high, low], axis=0)
        terms_ref[tile] = jnp.concatenate([both, both], axis=1)
        turned = state.T
        for k in range(3):
            wide_ref[k, cols, :] = jnp.broadcast_to(turned[:, k : k + 1], (TILE, TILE))

    copies[1].wait()
    place_ref[...] = sphere_ref[0:3, :] * (1.0 / support_radius) - 1.0
    copies[2].wait()

    def pair_weights(slot, part):
        a = list_ref[0, slot]
        b = list_ref[1, slot]
        cols = pl.ds(pl.multiple_of(a * TILE, TILE), TILE)
        rows = pl.ds(pl.multiple_of(b * TILE, TILE), TILE)
        dx = place_ref[0:1, cols] - wide_ref[0, rows, :]
        dy = place_ref[1:2, cols] - wide_ref[1, rows, :]
        dz = place_ref[2:3, cols] - wide_ref[2, rows, :]
        square = jnp.maximum(dx * dx + dy * dy + dz * dz, 1e-30)
        falloff = jnp.maximum(1.0 - square * lax.rsqrt(square), 0.0)
        high, low = split_two(falloff * falloff * falloff)
        weight_ref[part, 0:TILE, :] = high
        weight_ref[part, TILE:, :] = low

    def add_sums(slot, part, live):
        a = list_ref[0, slot]
        b = list_ref[1, slot]
        cols = pl.ds(pl.multiple_of(a * TILE, TILE), TILE)
        sums = jnp.dot(terms_ref[b], weight_ref[part], preferred_element_type=f32)
        acc_ref[:, cols] += live * (sums[0:16] + sums[16:32])

    count = count_ref[0]
    trips = (count + UNROLL - 1) // UNROLL
    last = list_ref.shape[1] - 1

    for part in range(UNROLL):
        pair_weights(min(part, last), part)

    @pl.loop(1, trips)
    def _(trip):
        for part in range(UNROLL):
            add_sums((trip - 1) * UNROLL + part, part, 1.0)
        for part in range(UNROLL):
            pair_weights(jnp.minimum(trip * UNROLL + part, last), part)

    for part in range(UNROLL):
        slot = (trips - 1) * UNROLL + part
        live = jnp.where(slot < count, 1.0, 0.0).astype(f32)
        add_sums(jnp.clip(slot, 0, last), part, live)

    copies[3].wait()
    copies[4].wait()
    group = group_of(owners)
    width = group * SLOT

    @pl.loop(0, owners // group)
    def _(block):
        cols = pl.ds(pl.multiple_of(block * width, width), width)
        acc = acc_ref[:, cols]
        place = place_ref[:, cols]
        sphere = sphere_ref[:, cols]
        offset = offset_ref[:, cols]
        total = acc[7:8]
        pull = total * place - acc[0:3]
        press = acc[6:7] * place - acc[8:11]
        scale = press_coef * support_radius
        force = scale * (sphere[6:7] * pull + press) + visc_coef * (acc[3:6] - total * sphere[3:6])
        force = [force[k : k + 1] for k in range(3)]
        turn = cross([offset[k : k + 1] for k in range(3)], force)
        loads = jnp.concatenate(force + turn + [jnp.zeros_like(force[0])] * 2, axis=0)
        high, low = split_two(loads)
        both = jnp.concatenate([high, low], axis=0)
        column = lax.broadcasted_iota(jnp.int32, (clumps, SLOT), 0)
        for k in range(group):
            here = pl.ds(pl.multiple_of(block * width + k * SLOT, SLOT), SLOT)
            one_hot = jnp.where(column == ids_ref[:, here], 1.0, 0.0).astype(bf16)
            sums = lax.dot_general(
                both[:, k * SLOT : (k + 1) * SLOT], one_hot, (((1,), (1,)), ((), ())),
                preferred_element_type=f32,
            )
            put_rows(out_ref, block * group + k, sums[0:8] + sums[8:16], clumps)


def update_kernel(arrived_ref, state_ref, inverse_ref, out_ref):
    devices, _, width = out_ref.shape
    clumps = width // 3
    totals = jnp.sum(arrived_ref[...], axis=0)
    first = lax.axis_index("sub") == 0
    for k in range(3):
        cols = slice(k * clumps, (k + 1) * clumps)
        state = jnp.where(first, state_ref[k : k + 1, :], state_ref[k + 3 : k + 4, :])
        factor = jnp.where(first, inverse_ref[0:1, :], inverse_ref[k + 1 : k + 2, :])
        row = state + factor * totals[:, cols]
        if k == 2:
            row = row + jnp.where(first, -gravity_step, 0.0)
        out_ref[:, :, cols] = jnp.broadcast_to(row[None], (devices, 1, clumps))


def velocity_kernel(velocity_ref, offset_ref, ids_ref, clump_ref, sphere_ref):
    owners = velocity_ref.shape[0] // 2
    clumps = velocity_ref.shape[2] // 3
    group = group_of(owners)
    me = lax.axis_index("space")

    @pl.loop(0, owners // group)
    def _(block):
        for k in range(group):
            owner = block * group + k
            rows = get_rows(velocity_ref, owner, clumps) + [jnp.zeros((2, clumps), f32)]
            both = jnp.concatenate(split_two(jnp.concatenate(rows, axis=0)), axis=0)
            here = pl.ds(pl.multiple_of(owner * SLOT, SLOT), SLOT)
            column = lax.broadcasted_iota(jnp.int32, (clumps, SLOT), 0)
            one_hot = jnp.where(column == ids_ref[:, here], 1.0, 0.0).astype(bf16)
            picked = jnp.dot(both, one_hot, preferred_element_type=f32)
            picked = picked[0:8] + picked[8:16]
            offset = offset_ref[:, here]
            turn = cross([picked[3 + i : 4 + i] for i in range(3)], [offset[i : i + 1] for i in range(3)])
            sphere_ref[:, here] = picked[0:3] + jnp.concatenate(turn, axis=0)

    clump_ref[...] = jnp.concatenate(get_rows(velocity_ref, me, clumps), axis=0)


def per_device(
    fluid_state, sphere_state, sphere_offset, tile_list, tile_count, clump_ids, clump_state, clump_inverse
):
    owners = lax.axis_size("space")
    devices = owners * lax.axis_size("sub")
    spheres = sphere_state.shape[1]
    fluid = fluid_state.shape[1]
    clumps = clump_state.shape[1]
    slots = tile_list.shape[0]
    ids = clump_ids.reshape(1, spheres)
    vmem = pl.BlockSpec(memory_space=pltpu.VMEM)
    hbm = pl.BlockSpec(memory_space=pltpu.HBM)
    params = pltpu.CompilerParams(vmem_limit_bytes=48 * 1024 * 1024)

    partial = pl.pallas_call(
        loads_kernel,
        out_shape=pltpu.VMEM((devices, 1, 3 * clumps), f32),
        in_specs=[pl.BlockSpec(memory_space=pltpu.SMEM)] + [hbm] * 5,
        out_specs=vmem,
        scratch_shapes=[
            pltpu.SMEM((2, slots), jnp.int32),
            pltpu.VMEM((8, fluid), f32),
            pltpu.VMEM((7, spheres), f32),
            pltpu.VMEM((3, spheres), f32),
            pltpu.VMEM((1, spheres), jnp.int32),
            pltpu.SemaphoreType.DMA((5,)),
            pltpu.VMEM((3, spheres), f32),
            pltpu.VMEM((3, fluid, TILE), f32),
            pltpu.VMEM((fluid // TILE, 32, 2 * TILE), bf16),
            pltpu.VMEM((UNROLL, 2 * TILE, TILE), bf16),
            pltpu.VMEM((16, spheres), f32),
        ],
        compiler_params=params,
        name="clump_loads",
    )(tile_count, *(
        pltpu.with_memory_space_constraint(value, pltpu.HBM)
        for value in (tile_list.T, fluid_state, sphere_state, sphere_offset, ids)
    ))

    axes = ("space", "sub")
    arrived = lax.all_to_all(partial, axes, split_axis=0, concat_axis=0, tiled=True)
    rows = pl.pallas_call(
        update_kernel,
        out_shape=jax.ShapeDtypeStruct((devices, 1, 3 * clumps), f32),
        in_specs=[vmem] * 3,
        out_specs=vmem,
        compiler_params=params,
        name="clump_update",
    )(arrived, clump_state, clump_inverse)
    velocities = lax.all_to_all(rows, axes, split_axis=0, concat_axis=0, tiled=True)

    return pl.pallas_call(
        velocity_kernel,
        out_shape=(
            jax.ShapeDtypeStruct((6, clumps), f32),
            jax.ShapeDtypeStruct((3, spheres), f32),
        ),
        in_specs=[vmem] * 3,
        out_specs=(vmem, vmem),
        compiler_params=params,
        name="sphere_velocities",
    )(velocities, sphere_offset, ids)


def solution(mesh):
    in_specs = (
        P(None, "space"),
        P(None, "space"),
        P(None, "space"),
        P(("space", "sub"), None),
        P(("space", "sub")),
        P("space"),
        P(None, "space"),
        P(None, "space"),
    )
    out_specs = (P(None, "space"), P(None, "space"))
    return jax.shard_map(
        per_device, mesh=mesh, in_specs=in_specs, out_specs=out_specs, check_vma=False
    )
```

```python
import functools
import math

import jax
import jax.numpy as jnp
from jax import lax
from jax.experimental import pallas as pl
from jax.experimental.pallas import tpu as pltpu
from jax.sharding import PartitionSpec as P

TILE = 128
SLOT = 256
UNROLL = 8

support_radius = 0.5
press_coef = 4.0
visc_coef = 1.0
gravity_step = 0.1

f32 = jnp.float32
bf16 = jnp.bfloat16


def split_two(value):
    high = value.astype(bf16)
    return high, (value - high.astype(f32)).astype(bf16)


def cross(left, right):
    return [
        left[1] * right[2] - left[2] * right[1],
        left[2] * right[0] - left[0] * right[2],
        left[0] * right[1] - left[1] * right[0],
    ]


def group_of(owners):
    return math.gcd(owners, 16)


def loads_kernel(
    count_ref, list_hbm, fluid_hbm, sphere_hbm, offset_hbm, ids_hbm, out_ref,
    list_ref, fluid_ref, sphere_ref, offset_ref, ids_ref, arrived,
    place_ref, wide_ref, terms_ref, weight_ref, acc_ref,
):
    fluid_tiles = fluid_ref.shape[1] // TILE
    clumps = out_ref.shape[1]
    owners = out_ref.shape[0] // 6

    pairs = (
        (fluid_hbm, fluid_ref),
        (sphere_hbm, sphere_ref),
        (list_hbm, list_ref),
        (offset_hbm, offset_ref),
        (ids_hbm, ids_ref),
    )
    copies = [
        pltpu.make_async_copy(source, target, arrived.at[k]) for k, (source, target) in enumerate(pairs)
    ]
    for copy in copies:
        copy.start()

    acc_ref[...] = jnp.zeros_like(acc_ref)
    copies[0].wait()

    @pl.loop(0, fluid_tiles, unroll=8)
    def _(tile):
        cols = pl.ds(pl.multiple_of(tile * TILE, TILE), TILE)
        state = fluid_ref[:, cols]
        row = lax.broadcasted_iota(jnp.int32, state.shape, 0)
        state = jnp.where(row < 3, state * (1.0 / support_radius) - 1.0, state)
        mass = state[7:8]
        first = jnp.where(row < 7, state * mass, state)
        second = jnp.where(row < 3, state * (mass * state[6:7]), 0.0)
        high, low = split_two(jnp.concatenate([first, second], axis=0))
        both = jnp.concatenate([high, low], axis=0)
        terms_ref[tile] = jnp.concatenate([both, both], axis=1)
        turned = state.T
        for k in range(3):
            wide_ref[k, cols, :] = jnp.broadcast_to(turned[:, k : k + 1], (TILE, TILE))

    copies[1].wait()
    place_ref[...] = sphere_ref[0:3, :] * (1.0 / support_radius) - 1.0
    copies[2].wait()

    def pair_weights(slot, part):
        a = list_ref[0, slot]
        b = list_ref[1, slot]
        cols = pl.ds(pl.multiple_of(a * TILE, TILE), TILE)
        rows = pl.ds(pl.multiple_of(b * TILE, TILE), TILE)
        dx = place_ref[0:1, cols] - wide_ref[0, rows, :]
        dy = place_ref[1:2, cols] - wide_ref[1, rows, :]
        dz = place_ref[2:3, cols] - wide_ref[2, rows, :]
        square = jnp.maximum(dx * dx + dy * dy + dz * dz, 1e-30)
        falloff = jnp.maximum(1.0 - square * lax.rsqrt(square), 0.0)
        high, low = split_two(falloff * falloff * falloff)
        weight_ref[part, 0:TILE, :] = high
        weight_ref[part, TILE:, :] = low

    def add_sums(slot, part, live):
        a = list_ref[0, slot]
        b = list_ref[1, slot]
        cols = pl.ds(pl.multiple_of(a * TILE, TILE), TILE)
        sums = jnp.dot(terms_ref[b], weight_ref[part], preferred_element_type=f32)
        acc_ref[:, cols] += live * (sums[0:16] + sums[16:32])

    count = count_ref[0]
    trips = (count + UNROLL - 1) // UNROLL
    last = list_ref.shape[1] - 1

    for part in range(UNROLL):
        pair_weights(min(part, last), part)

    @pl.loop(1, trips)
    def _(trip):
        for part in range(UNROLL):
            add_sums((trip - 1) * UNROLL + part, part, 1.0)
        for part in range(UNROLL):
            pair_weights(jnp.minimum(trip * UNROLL + part, last), part)

    for part in range(UNROLL):
        slot = (trips - 1) * UNROLL + part
        live = jnp.where(slot < count, 1.0, 0.0).astype(f32)
        add_sums(jnp.clip(slot, 0, last), part, live)

    copies[3].wait()
    copies[4].wait()
    group = group_of(owners)
    width = group * SLOT

    @pl.loop(0, owners // group)
    def _(block):
        cols = pl.ds(pl.multiple_of(block * width, width), width)
        acc = acc_ref[:, cols]
        place = place_ref[:, cols]
        sphere = sphere_ref[:, cols]
        offset = offset_ref[:, cols]
        total = acc[7:8]
        pull = total * place - acc[0:3]
        press = acc[6:7] * place - acc[8:11]
        scale = press_coef * support_radius
        force = scale * (sphere[6:7] * pull + press) + visc_coef * (acc[3:6] - total * sphere[3:6])
        force = [force[k : k + 1] for k in range(3)]
        turn = cross([offset[k : k + 1] for k in range(3)], force)
        loads = jnp.concatenate(force + turn + [jnp.zeros_like(force[0])] * 2, axis=0)
        high, low = split_two(loads)
        both = jnp.concatenate([high, low], axis=0)
        column = lax.broadcasted_iota(jnp.int32, (clumps, SLOT), 0)
        results = []
        for k in range(group):
            here = pl.ds(pl.multiple_of(block * width + k * SLOT, SLOT), SLOT)
            one_hot = jnp.where(column == ids_ref[:, here], 1.0, 0.0).astype(bf16)
            sums = lax.dot_general(
                both[:, k * SLOT : (k + 1) * SLOT], one_hot, (((1,), (1,)), ((), ())),
                preferred_element_type=f32,
            )
            results.append((sums[0:8] + sums[8:16])[0:6])
        start = pl.multiple_of(block * (6 * group), math.gcd(6 * group, 8))
        out_ref[pl.ds(start, 6 * group), :] = jnp.concatenate(results, axis=0)


def velocity_kernel(
    mine_ref, other_ref, offset_ref, ids_ref, clump_ref, sphere_ref, velocity_ref, state_ref
):
    owners, _, clumps = velocity_ref.shape
    group = group_of(owners)
    me = lax.axis_index("space")
    row = lax.broadcasted_iota(jnp.int32, (6, clumps), 0)
    gravity = jnp.where(row == 2, -gravity_step, 0.0)
    half = owners // 2
    for k in range(half):
        first = 6 * owners + 10 * k
        state_ref[me ^ k] = mine_ref[first : first + 10, :]
        state_ref[me ^ (k + half)] = other_ref[first : first + 10, :]

    @pl.loop(0, owners // group)
    def _(block):
        start = pl.multiple_of(block * (6 * group), math.gcd(6 * group, 8))
        totals = mine_ref[pl.ds(start, 6 * group), :] + other_ref[pl.ds(start, 6 * group), :]
        for k in range(group):
            owner = block * group + k
            state = state_ref[owner]
            factor = jnp.concatenate([state[6:7]] * 3 + [state[7:10]], axis=0)
            velocity = state[0:6] + factor * totals[6 * k : 6 * k + 6] + gravity
            velocity_ref[owner] = velocity
            rows = jnp.concatenate([velocity, jnp.zeros((2, clumps), f32)], axis=0)
            both = jnp.concatenate(split_two(rows), axis=0)
            here = pl.ds(pl.multiple_of(owner * SLOT, SLOT), SLOT)
            column = lax.broadcasted_iota(jnp.int32, (clumps, SLOT), 0)
            one_hot = jnp.where(column == ids_ref[:, here], 1.0, 0.0).astype(bf16)
            picked = jnp.dot(both, one_hot, preferred_element_type=f32)
            picked = picked[0:8] + picked[8:16]
            offset = offset_ref[:, here]
            turn = cross([picked[3 + i : 4 + i] for i in range(3)], [offset[i : i + 1] for i in range(3)])
            sphere_ref[:, here] = picked[0:3] + jnp.concatenate(turn, axis=0)

    clump_ref[...] = velocity_ref[me]


def swap(value, axis, bit):
    size = lax.axis_size(axis)
    return lax.ppermute(value, axis, [(k, k ^ bit) for k in range(size)])


def per_device(
    fluid_state, sphere_state, sphere_offset, tile_list, tile_count, clump_ids, clump_state, clump_inverse
):
    owners = lax.axis_size("space")
    spheres = sphere_state.shape[1]
    fluid = fluid_state.shape[1]
    clumps = clump_state.shape[1]
    slots = tile_list.shape[0]
    ids = clump_ids.reshape(1, spheres)
    vmem = pl.BlockSpec(memory_space=pltpu.VMEM)
    hbm = pl.BlockSpec(memory_space=pltpu.HBM)
    params = pltpu.CompilerParams(vmem_limit_bytes=48 * 1024 * 1024)

    partial = pl.pallas_call(
        loads_kernel,
        out_shape=pltpu.VMEM((6 * owners, clumps), f32),
        in_specs=[pl.BlockSpec(memory_space=pltpu.SMEM)] + [hbm] * 5,
        out_specs=vmem,
        scratch_shapes=[
            pltpu.SMEM((2, slots), jnp.int32),
            pltpu.VMEM((8, fluid), f32),
            pltpu.VMEM((7, spheres), f32),
            pltpu.VMEM((3, spheres), f32),
            pltpu.VMEM((1, spheres), jnp.int32),
            pltpu.SemaphoreType.DMA((5,)),
            pltpu.VMEM((3, spheres), f32),
            pltpu.VMEM((3, fluid, TILE), f32),
            pltpu.VMEM((fluid // TILE, 32, 2 * TILE), bf16),
            pltpu.VMEM((UNROLL, 2 * TILE, TILE), bf16),
            pltpu.VMEM((16, spheres), f32),
        ],
        compiler_params=params,
        name="clump_loads",
    )(tile_count, *(
        pltpu.with_memory_space_constraint(value, pltpu.HBM)
        for value in (tile_list.T, fluid_state, sphere_state, sphere_offset, ids)
    ))

    rows = 6 * owners
    partial = partial + swap(partial, "sub", 1)
    mine = jnp.concatenate([partial, clump_state, clump_inverse], axis=0)
    other = swap(mine, "space", 1)
    bit = 2
    while bit < owners:
        mine = jnp.concatenate([mine[:rows] + other[:rows], mine[rows:], other[rows:]], axis=0)
        other = swap(mine, "space", bit)
        bit *= 2

    return pl.pallas_call(
        velocity_kernel,
        out_shape=(
            jax.ShapeDtypeStruct((6, clumps), f32),
            jax.ShapeDtypeStruct((3, spheres), f32),
        ),
        in_specs=[vmem] * 4,
        out_specs=(vmem, vmem),
        scratch_shapes=[pltpu.VMEM((owners, 6, clumps), f32), pltpu.VMEM((owners, 10, clumps), f32)],
        compiler_params=params,
        name="sphere_velocities",
    )(mine, other, sphere_offset, ids)


def solution(mesh):
    in_specs = (
        P(None, "space"),
        P(None, "space"),
        P(None, "space"),
        P(("space", "sub"), None),
        P(("space", "sub")),
        P("space"),
        P(None, "space"),
        P(None, "space"),
    )
    out_specs = (P(None, "space"), P(None, "space"))
    return jax.shard_map(
        per_device, mesh=mesh, in_specs=in_specs, out_specs=out_specs, check_vma=False
    )
```

```python
import functools
import math

import jax
import jax.numpy as jnp
from jax import lax
from jax.experimental import pallas as pl
from jax.experimental.pallas import tpu as pltpu
from jax.sharding import PartitionSpec as P

TILE = 128
SLOT = 256
UNROLL = 8

support_radius = 0.5
press_coef = 4.0
visc_coef = 1.0
gravity_step = 0.1

f32 = jnp.float32
bf16 = jnp.bfloat16


def split_two(value):
    high = value.astype(bf16)
    return high, (value - high.astype(f32)).astype(bf16)


def cross(left, right):
    return [
        left[1] * right[2] - left[2] * right[1],
        left[2] * right[0] - left[0] * right[2],
        left[0] * right[1] - left[1] * right[0],
    ]


def group_of(owners):
    return math.gcd(owners, 16)


def loads_kernel(
    count_ref, list_hbm, fluid_hbm, sphere_hbm, offset_hbm, ids_hbm, state_hbm, inverse_hbm,
    keep_ref, send_ref,
    list_ref, fluid_ref, sphere_ref, offset_ref, ids_ref, state_ref, inverse_ref, arrived,
    place_ref, wide_ref, terms_ref, weight_ref, acc_ref,
):
    fluid_tiles = fluid_ref.shape[1] // TILE
    clumps = keep_ref.shape[1]
    owners = keep_ref.shape[0] // 3
    core = lax.axis_index("sub")
    me = jnp.where(core == 0, lax.axis_index("space"), -1)

    pairs = (
        (fluid_hbm, fluid_ref),
        (sphere_hbm, sphere_ref),
        (list_hbm, list_ref),
        (offset_hbm, offset_ref),
        (ids_hbm, ids_ref),
        (state_hbm, state_ref),
        (inverse_hbm, inverse_ref),
    )
    copies = [
        pltpu.make_async_copy(source, target, arrived.at[k]) for k, (source, target) in enumerate(pairs)
    ]
    for copy in copies:
        copy.start()

    acc_ref[...] = jnp.zeros_like(acc_ref)
    copies[0].wait()

    @pl.loop(0, fluid_tiles, unroll=8)
    def _(tile):
        cols = pl.ds(pl.multiple_of(tile * TILE, TILE), TILE)
        state = fluid_ref[:, cols]
        row = lax.broadcasted_iota(jnp.int32, state.shape, 0)
        state = jnp.where(row < 3, state * (1.0 / support_radius) - 1.0, state)
        mass = state[7:8]
        first = jnp.where(row < 7, state * mass, state)
        second = jnp.where(row < 3, state * (mass * state[6:7]), 0.0)
        high, low = split_two(jnp.concatenate([first, second], axis=0))
        both = jnp.concatenate([high, low], axis=0)
        terms_ref[tile] = jnp.concatenate([both, both], axis=1)
        turned = state.T
        for k in range(3):
            wide_ref[k, cols, :] = jnp.broadcast_to(turned[:, k : k + 1], (TILE, TILE))

    copies[1].wait()
    place_ref[...] = sphere_ref[0:3, :] * (1.0 / support_radius) - 1.0
    copies[2].wait()

    def pair_weights(slot, part):
        a = list_ref[0, slot]
        b = list_ref[1, slot]
        cols = pl.ds(pl.multiple_of(a * TILE, TILE), TILE)
        rows = pl.ds(pl.multiple_of(b * TILE, TILE), TILE)
        dx = place_ref[0:1, cols] - wide_ref[0, rows, :]
        dy = place_ref[1:2, cols] - wide_ref[1, rows, :]
        dz = place_ref[2:3, cols] - wide_ref[2, rows, :]
        square = jnp.maximum(dx * dx + dy * dy + dz * dz, 1e-30)
        falloff = jnp.maximum(1.0 - square * lax.rsqrt(square), 0.0)
        high, low = split_two(falloff * falloff * falloff)
        weight_ref[part, 0:TILE, :] = high
        weight_ref[part, TILE:, :] = low

    def add_sums(slot, part, live):
        a = list_ref[0, slot]
        b = list_ref[1, slot]
        cols = pl.ds(pl.multiple_of(a * TILE, TILE), TILE)
        sums = jnp.dot(terms_ref[b], weight_ref[part], preferred_element_type=f32)
        acc_ref[:, cols] += live * (sums[0:16] + sums[16:32])

    count = count_ref[0]
    trips = (count + UNROLL - 1) // UNROLL
    last = list_ref.shape[1] - 1

    for part in range(UNROLL):
        pair_weights(min(part, last), part)

    @pl.loop(1, trips)
    def _(trip):
        for part in range(UNROLL):
            add_sums((trip - 1) * UNROLL + part, part, 1.0)
        for part in range(UNROLL):
            pair_weights(jnp.minimum(trip * UNROLL + part, last), part)

    for part in range(UNROLL):
        slot = (trips - 1) * UNROLL + part
        live = jnp.where(slot < count, 1.0, 0.0).astype(f32)
        add_sums(jnp.clip(slot, 0, last), part, live)

    for copy in copies[3:]:
        copy.wait()
    group = group_of(owners)
    width = group * SLOT

    row = lax.broadcasted_iota(jnp.int32, state_ref.shape, 0)
    still = state_ref[...] + jnp.where(row == 2, -gravity_step, 0.0)
    still = still / jnp.concatenate([inverse_ref[0:1, :]] * 3 + [inverse_ref[1:4, :]], axis=0)

    @pl.loop(0, owners // group)
    def _(block):
        cols = pl.ds(pl.multiple_of(block * width, width), width)
        acc = acc_ref[:, cols]
        place = place_ref[:, cols]
        sphere = sphere_ref[:, cols]
        offset = offset_ref[:, cols]
        total = acc[7:8]
        pull = total * place - acc[0:3]
        press = acc[6:7] * place - acc[8:11]
        scale = press_coef * support_radius
        force = scale * (sphere[6:7] * pull + press) + visc_coef * (acc[3:6] - total * sphere[3:6])
        force = [force[k : k + 1] for k in range(3)]
        turn = cross([offset[k : k + 1] for k in range(3)], force)
        loads = jnp.concatenate(force + turn + [jnp.zeros_like(force[0])] * 2, axis=0)
        high, low = split_two(loads)
        both = jnp.concatenate([high, low], axis=0)
        column = lax.broadcasted_iota(jnp.int32, (clumps, SLOT), 0)
        keep, send = [], []
        for k in range(group):
            here = pl.ds(pl.multiple_of(block * width + k * SLOT, SLOT), SLOT)
            one_hot = jnp.where(column == ids_ref[:, here], 1.0, 0.0).astype(bf16)
            sums = lax.dot_general(
                both[:, k * SLOT : (k + 1) * SLOT], one_hot, (((1,), (1,)), ((), ())),
                preferred_element_type=f32,
            )
            own = jnp.where(block * group + k == me, 1.0, 0.0).astype(f32)
            sums = (sums[0:8] + sums[8:16])[0:6] + own * still
            keep.append(jnp.where(core == 0, sums[0:3], sums[3:6]))
            send.append(jnp.where(core == 0, sums[3:6], sums[0:3]))
        here = pl.ds(pl.multiple_of(block * (3 * group), math.gcd(3 * group, 8)), 3 * group)
        keep_ref[here, :] = jnp.concatenate(keep, axis=0)
        send_ref[here, :] = jnp.concatenate(send, axis=0)


def first_kernel(keep_ref, arrived_ref, inverse_ref, out_ref):
    rows = keep_ref.shape[0]
    out_ref[0:rows, :] = keep_ref[...] + arrived_ref[...]
    linear = jnp.concatenate([inverse_ref[0:1, :]] * 3, axis=0)
    out_ref[rows:, :] = jnp.where(lax.axis_index("sub") == 0, linear, inverse_ref[1:4, :])


def join_kernel(rows, mine_ref, arrived_ref, out_ref):
    more = mine_ref.shape[0] - rows
    out_ref[0:rows, :] = mine_ref[0:rows, :] + arrived_ref[0:rows, :]
    out_ref[rows : rows + more, :] = mine_ref[rows:, :]
    out_ref[rows + more :, :] = arrived_ref[rows:, :]


def update_kernel(partners, mine_ref, arrived_ref, out_ref, inverse_ref):
    owners = len(partners)
    rows = 3 * owners
    half = owners // 2
    me = lax.axis_index("space")
    for k in range(half):
        here = slice(rows + 3 * k, rows + 3 * k + 3)
        inverse_ref[me ^ partners[k]] = mine_ref[here, :]
        inverse_ref[me ^ partners[k + half]] = arrived_ref[here, :]
    totals = mine_ref[0:rows, :] + arrived_ref[0:rows, :]
    out_ref[...] = totals * jnp.concatenate([inverse_ref[k] for k in range(owners)], axis=0)


def velocity_kernel(mine_ref, arrived_ref, offset_ref, ids_ref, clump_ref, sphere_ref, velocity_ref):
    owners, _, clumps = velocity_ref.shape
    group = group_of(owners)
    core = lax.axis_index("sub")

    @pl.loop(0, owners // group)
    def _(block):
        rows = pl.ds(pl.multiple_of(block * (3 * group), math.gcd(3 * group, 8)), 3 * group)
        mine = mine_ref[rows, :]
        arrived = arrived_ref[rows, :]
        linear = jnp.where(core == 0, mine, arrived)
        angular = jnp.where(core == 0, arrived, mine)
        for k in range(group):
            owner = block * group + k
            three = slice(3 * k, 3 * k + 3)
            velocity = jnp.concatenate([linear[three], angular[three]], axis=0)
            velocity_ref[owner] = velocity
            both = jnp.concatenate(
                split_two(jnp.concatenate([velocity, jnp.zeros((2, clumps), f32)], axis=0)), axis=0
            )
            here = pl.ds(pl.multiple_of(owner * SLOT, SLOT), SLOT)
            column = lax.broadcasted_iota(jnp.int32, (clumps, SLOT), 0)
            one_hot = jnp.where(column == ids_ref[:, here], 1.0, 0.0).astype(bf16)
            picked = jnp.dot(both, one_hot, preferred_element_type=f32)
            picked = picked[0:8] + picked[8:16]
            offset = offset_ref[:, here]
            turn = cross([picked[3 + i : 4 + i] for i in range(3)], [offset[i : i + 1] for i in range(3)])
            sphere_ref[:, here] = picked[0:3] + jnp.concatenate(turn, axis=0)

    clump_ref[...] = velocity_ref[lax.axis_index("space")]


def swap(value, axis, bit):
    size = lax.axis_size(axis)
    return lax.ppermute(value, axis, [(k, k ^ bit) for k in range(size)])


def per_device(
    fluid_state, sphere_state, sphere_offset, tile_list, tile_count, clump_ids, clump_state, clump_inverse
):
    owners = lax.axis_size("space")
    spheres = sphere_state.shape[1]
    fluid = fluid_state.shape[1]
    clumps = clump_state.shape[1]
    slots = tile_list.shape[0]
    rows = 3 * owners
    ids = clump_ids.reshape(1, spheres)
    vmem = pl.BlockSpec(memory_space=pltpu.VMEM)
    hbm = pl.BlockSpec(memory_space=pltpu.HBM)
    params = pltpu.CompilerParams(vmem_limit_bytes=48 * 1024 * 1024)

    keep, send = pl.pallas_call(
        loads_kernel,
        out_shape=(pltpu.VMEM((rows, clumps), f32), pltpu.VMEM((rows, clumps), f32)),
        in_specs=[pl.BlockSpec(memory_space=pltpu.SMEM)] + [hbm] * 7,
        out_specs=(vmem, vmem),
        scratch_shapes=[
            pltpu.SMEM((2, slots), jnp.int32),
            pltpu.VMEM((8, fluid), f32),
            pltpu.VMEM((7, spheres), f32),
            pltpu.VMEM((3, spheres), f32),
            pltpu.VMEM((1, spheres), jnp.int32),
            pltpu.VMEM((6, clumps), f32),
            pltpu.VMEM((4, clumps), f32),
            pltpu.SemaphoreType.DMA((7,)),
            pltpu.VMEM((3, spheres), f32),
            pltpu.VMEM((3, fluid, TILE), f32),
            pltpu.VMEM((fluid // TILE, 32, 2 * TILE), bf16),
            pltpu.VMEM((UNROLL, 2 * TILE, TILE), bf16),
            pltpu.VMEM((16, spheres), f32),
        ],
        compiler_params=params,
        name="clump_loads",
    )(tile_count, *(
        pltpu.with_memory_space_constraint(value, pltpu.HBM)
        for value in (
            tile_list.T, fluid_state, sphere_state, sphere_offset, ids, clump_state, clump_inverse
        )
    ))

    def small(kernel, height, name, *operands, scratch=()):
        return pl.pallas_call(
            kernel,
            out_shape=pltpu.VMEM((height, clumps), f32),
            in_specs=[vmem] * len(operands),
            out_specs=vmem,
            scratch_shapes=scratch,
            compiler_params=params,
            name=name,
        )(*operands)

    mine = small(first_kernel, rows + 3, "core_sum", keep, swap(send, "sub", 1), clump_inverse)
    bits = []
    bit = owners // 2
    while bit > 0:
        arrived = swap(mine, "space", bit)
        bits.append(bit)
        if bit > 1:
            height = 2 * mine.shape[0] - rows
            mine = small(functools.partial(join_kernel, rows), height, "space_sum", mine, arrived)
        bit //= 2
    partners = [sum(bit for n, bit in enumerate(bits) if k >> n & 1) for k in range(owners)]
    velocities = small(
        functools.partial(update_kernel, partners), rows, "clump_update", mine, arrived,
        scratch=[pltpu.VMEM((owners, 3, clumps), f32)],
    )

    return pl.pallas_call(
        velocity_kernel,
        out_shape=(
            jax.ShapeDtypeStruct((6, clumps), f32),
            jax.ShapeDtypeStruct((3, spheres), f32),
        ),
        in_specs=[vmem] * 4,
        out_specs=(vmem, vmem),
        scratch_shapes=[pltpu.VMEM((owners, 6, clumps), f32)],
        compiler_params=params,
        name="sphere_velocities",
    )(velocities, swap(velocities, "sub", 1), sphere_offset, ids)


def solution(mesh):
    in_specs = (
        P(None, "space"),
        P(None, "space"),
        P(None, "space"),
        P(("space", "sub"), None),
        P(("space", "sub")),
        P("space"),
        P(None, "space"),
        P(None, "space"),
    )
    out_specs = (P(None, "space"), P(None, "space"))
    return jax.shard_map(
        per_device, mesh=mesh, in_specs=in_specs, out_specs=out_specs, check_vma=False
    )
```

```python
import functools
import math

import jax
import jax.numpy as jnp
from jax import lax
from jax.experimental import pallas as pl
from jax.experimental.pallas import tpu as pltpu
from jax.sharding import PartitionSpec as P

TILE = 128
SLOT = 256
UNROLL = 4

support_radius = 0.5
press_coef = 4.0
visc_coef = 1.0
gravity_step = 0.1

f32 = jnp.float32
bf16 = jnp.bfloat16


def split_two(value):
    high = value.astype(bf16)
    return high, (value - high.astype(f32)).astype(bf16)


def cross(left, right):
    return [
        left[1] * right[2] - left[2] * right[1],
        left[2] * right[0] - left[0] * right[2],
        left[0] * right[1] - left[1] * right[0],
    ]


def put_rows(ref, owner, rows, clumps):
    for half in range(2):
        for k in range(3):
            ref[2 * owner + half, :, k * clumps : (k + 1) * clumps] = rows[3 * half + k : 3 * half + k + 1]


def get_rows(ref, owner, clumps):
    return [
        ref[2 * owner + half, :, k * clumps : (k + 1) * clumps] for half in range(2) for k in range(3)
    ]


def group_of(owners):
    return math.gcd(owners, 16)


def loads_kernel(
    count_ref, list_hbm, fluid_hbm, sphere_hbm, offset_hbm, ids_hbm, out_ref,
    list_ref, fluid_ref, sphere_ref, offset_ref, ids_ref, arrived,
    place_ref, lines_ref, lanes_ref, terms_ref, weight_ref, acc_ref,
):
    fluid_tiles = fluid_ref.shape[1] // TILE
    clumps = out_ref.shape[2] // 3
    owners = out_ref.shape[0] // 2

    pairs = (
        (fluid_hbm, fluid_ref),
        (sphere_hbm, sphere_ref),
        (list_hbm, list_ref),
        (offset_hbm, offset_ref),
        (ids_hbm, ids_ref),
    )
    copies = [
        pltpu.make_async_copy(source, target, arrived.at[k]) for k, (source, target) in enumerate(pairs)
    ]
    for copy in copies:
        copy.start()

    acc_ref[...] = jnp.zeros_like(acc_ref)
    copies[0].wait()

    @pl.loop(0, fluid_tiles, unroll=4)
    def _(tile):
        cols = pl.ds(pl.multiple_of(tile * TILE, TILE), TILE)
        state = fluid_ref[:, cols]
        row = lax.broadcasted_iota(jnp.int32, state.shape, 0)
        state = jnp.where(row < 3, state * (1.0 / support_radius) - 1.0, state)
        mass = state[7:8]
        first = jnp.where(row < 7, state * mass, state)
        second = jnp.where(row < 3, state * (mass * state[6:7]), 0.0)
        high, low = split_two(jnp.concatenate([first, second], axis=0))
        both = jnp.concatenate([high, low], axis=0)
        terms_ref[tile] = jnp.concatenate([both, both], axis=1)

    assert 3 * fluid_tiles <= TILE
    lines_ref[...] = jnp.zeros_like(lines_ref)
    for k in range(3):
        for tile in range(fluid_tiles):
            at = k * fluid_tiles + tile
            lines_ref[at : at + 1, :] = fluid_ref[k : k + 1, tile * TILE : (tile + 1) * TILE]
    lanes_ref[...] = lines_ref[...].T * (1.0 / support_radius) - 1.0

    copies[1].wait()
    place_ref[...] = sphere_ref[0:3, :] * (1.0 / support_radius) - 1.0
    copies[2].wait()

    def pair_weights(slot, part):
        a = list_ref[0, slot]
        b = list_ref[1, slot]
        cols = pl.ds(pl.multiple_of(a * TILE, TILE), TILE)
        lanes = lanes_ref[...]
        dx, dy, dz = [
            place_ref[k : k + 1, cols]
            - jnp.take_along_axis(
                lanes, jnp.full((TILE, TILE), k * fluid_tiles + b, jnp.int32), axis=1, mode="promise_in_bounds"
            )
            for k in range(3)
        ]
        square = jnp.maximum(dx * dx + dy * dy + dz * dz, 1e-30)
        falloff = jnp.maximum(1.0 - square * lax.rsqrt(square), 0.0)
        high, low = split_two(falloff * falloff * falloff)
        weight_ref[part, 0:TILE, :] = high
        weight_ref[part, TILE:, :] = low

    def add_sums(slot, part, live):
        a = list_ref[0, slot]
        b = list_ref[1, slot]
        cols = pl.ds(pl.multiple_of(a * TILE, TILE), TILE)
        sums = jnp.dot(terms_ref[b], weight_ref[part], preferred_element_type=f32)
        acc_ref[:, cols] += live * (sums[0:16] + sums[16:32])

    count = count_ref[0]
    trips = (count + UNROLL - 1) // UNROLL
    last = list_ref.shape[1] - 1

    for part in range(UNROLL):
        pair_weights(min(part, last), part)

    @pl.loop(1, trips)
    def _(trip):
        for part in range(UNROLL):
            add_sums((trip - 1) * UNROLL + part, part, 1.0)
        for part in range(UNROLL):
            pair_weights(jnp.minimum(trip * UNROLL + part, last), part)

    for part in range(UNROLL):
        slot = (trips - 1) * UNROLL + part
        live = jnp.where(slot < count, 1.0, 0.0).astype(f32)
        add_sums(jnp.clip(slot, 0, last), part, live)

    copies[3].wait()
    copies[4].wait()
    group = group_of(owners)
    width = group * SLOT

    @pl.loop(0, owners // group)
    def _(block):
        cols = pl.ds(pl.multiple_of(block * width, width), width)
        acc = acc_ref[:, cols]
        place = place_ref[:, cols]
        sphere = sphere_ref[:, cols]
        offset = offset_ref[:, cols]
        total = acc[7:8]
        pull = total * place - acc[0:3]
        press = acc[6:7] * place - acc[8:11]
        scale = press_coef * support_radius
        force = scale * (sphere[6:7] * pull + press) + visc_coef * (acc[3:6] - total * sphere[3:6])
        force = [force[k : k + 1] for k in range(3)]
        turn = cross([offset[k : k + 1] for k in range(3)], force)
        loads = jnp.concatenate(force + turn + [jnp.zeros_like(force[0])] * 2, axis=0)
        high, low = split_two(loads)
        both = jnp.concatenate([high, low], axis=0)
        column = lax.broadcasted_iota(jnp.int32, (clumps, SLOT), 0)
        for k in range(group):
            here = pl.ds(pl.multiple_of(block * width + k * SLOT, SLOT), SLOT)
            one_hot = jnp.where(column == ids_ref[:, here], 1.0, 0.0).astype(bf16)
            sums = lax.dot_general(
                both[:, k * SLOT : (k + 1) * SLOT], one_hot, (((1,), (1,)), ((), ())),
                preferred_element_type=f32,
            )
            put_rows(out_ref, block * group + k, sums[0:8] + sums[8:16], clumps)


def update_kernel(arrived_ref, state_ref, inverse_ref, out_ref):
    devices, _, width = out_ref.shape
    clumps = width // 3
    totals = jnp.sum(arrived_ref[...], axis=0)
    first = lax.axis_index("sub") == 0
    for k in range(3):
        cols = slice(k * clumps, (k + 1) * clumps)
        state = jnp.where(first, state_ref[k : k + 1, :], state_ref[k + 3 : k + 4, :])
        factor = jnp.where(first, inverse_ref[0:1, :], inverse_ref[k + 1 : k + 2, :])
        row = state + factor * totals[:, cols]
        if k == 2:
            row = row + jnp.where(first, -gravity_step, 0.0)
        out_ref[:, :, cols] = jnp.broadcast_to(row[None], (devices, 1, clumps))


def velocity_kernel(velocity_ref, offset_ref, ids_ref, clump_ref, sphere_ref):
    owners = velocity_ref.shape[0] // 2
    clumps = velocity_ref.shape[2] // 3
    group = group_of(owners)
    me = lax.axis_index("space")

    @pl.loop(0, owners // group)
    def _(block):
        for k in range(group):
            owner = block * group + k
            rows = get_rows(velocity_ref, owner, clumps) + [jnp.zeros((2, clumps), f32)]
            both = jnp.concatenate(split_two(jnp.concatenate(rows, axis=0)), axis=0)
            here = pl.ds(pl.multiple_of(owner * SLOT, SLOT), SLOT)
            column = lax.broadcasted_iota(jnp.int32, (clumps, SLOT), 0)
            one_hot = jnp.where(column == ids_ref[:, here], 1.0, 0.0).astype(bf16)
            picked = jnp.dot(both, one_hot, preferred_element_type=f32)
            picked = picked[0:8] + picked[8:16]
            offset = offset_ref[:, here]
            turn = cross([picked[3 + i : 4 + i] for i in range(3)], [offset[i : i + 1] for i in range(3)])
            sphere_ref[:, here] = picked[0:3] + jnp.concatenate(turn, axis=0)

    clump_ref[...] = jnp.concatenate(get_rows(velocity_ref, me, clumps), axis=0)


def per_device(
    fluid_state, sphere_state, sphere_offset, tile_list, tile_count, clump_ids, clump_state, clump_inverse
):
    owners = lax.axis_size("space")
    devices = owners * lax.axis_size("sub")
    spheres = sphere_state.shape[1]
    fluid = fluid_state.shape[1]
    clumps = clump_state.shape[1]
    slots = tile_list.shape[0]
    ids = clump_ids.reshape(1, spheres)
    vmem = pl.BlockSpec(memory_space=pltpu.VMEM)
    hbm = pl.BlockSpec(memory_space=pltpu.HBM)
    params = pltpu.CompilerParams(vmem_limit_bytes=48 * 1024 * 1024)

    partial = pl.pallas_call(
        loads_kernel,
        out_shape=pltpu.VMEM((devices, 1, 3 * clumps), f32),
        in_specs=[pl.BlockSpec(memory_space=pltpu.SMEM)] + [hbm] * 5,
        out_specs=vmem,
        scratch_shapes=[
            pltpu.SMEM((2, slots), jnp.int32),
            pltpu.VMEM((8, fluid), f32),
            pltpu.VMEM((7, spheres), f32),
            pltpu.VMEM((3, spheres), f32),
            pltpu.VMEM((1, spheres), jnp.int32),
            pltpu.SemaphoreType.DMA((5,)),
            pltpu.VMEM((3, spheres), f32),
            pltpu.VMEM((TILE, TILE), f32),
            pltpu.VMEM((TILE, TILE), f32),
            pltpu.VMEM((fluid // TILE, 32, 2 * TILE), bf16),
            pltpu.VMEM((UNROLL, 2 * TILE, TILE), bf16),
            pltpu.VMEM((16, spheres), f32),
        ],
        compiler_params=params,
        name="clump_loads",
    )(tile_count, *(
        pltpu.with_memory_space_constraint(value, pltpu.HBM)
        for value in (tile_list.T, fluid_state, sphere_state, sphere_offset, ids)
    ))

    axes = ("space", "sub")
    arrived = lax.all_to_all(partial, axes, split_axis=0, concat_axis=0, tiled=True)
    rows = pl.pallas_call(
        update_kernel,
        out_shape=jax.ShapeDtypeStruct((devices, 1, 3 * clumps), f32),
        in_specs=[vmem] * 3,
        out_specs=vmem,
        compiler_params=params,
        name="clump_update",
    )(arrived, clump_state, clump_inverse)
    velocities = lax.all_to_all(rows, axes, split_axis=0, concat_axis=0, tiled=True)

    return pl.pallas_call(
        velocity_kernel,
        out_shape=(
            jax.ShapeDtypeStruct((6, clumps), f32),
            jax.ShapeDtypeStruct((3, spheres), f32),
        ),
        in_specs=[vmem] * 3,
        out_specs=(vmem, vmem),
        compiler_params=params,
        name="sphere_velocities",
    )(velocities, sphere_offset, ids)


def solution(mesh):
    in_specs = (
        P(None, "space"),
        P(None, "space"),
        P(None, "space"),
        P(("space", "sub"), None),
        P(("space", "sub")),
        P("space"),
        P(None, "space"),
        P(None, "space"),
    )
    out_specs = (P(None, "space"), P(None, "space"))
    return jax.shard_map(
        per_device, mesh=mesh, in_specs=in_specs, out_specs=out_specs, check_vma=False
    )
```

```python
import functools
import math

import jax
import jax.numpy as jnp
from jax import lax
from jax.experimental import pallas as pl
from jax.experimental.pallas import tpu as pltpu
from jax.sharding import PartitionSpec as P

TILE = 128
SLOT = 256
UNROLL = 4

support_radius = 0.5
press_coef = 4.0
visc_coef = 1.0
gravity_step = 0.1

f32 = jnp.float32
bf16 = jnp.bfloat16


def split_two(value):
    high = value.astype(bf16)
    return high, (value - high.astype(f32)).astype(bf16)


def split_three(value):
    high = value.astype(bf16).astype(f32)
    middle = (value - high).astype(bf16).astype(f32)
    return high, middle, (value - high) - middle


def cross(left, right):
    return [
        left[1] * right[2] - left[2] * right[1],
        left[2] * right[0] - left[0] * right[2],
        left[0] * right[1] - left[1] * right[0],
    ]


def put_rows(ref, owner, rows, clumps):
    for half in range(2):
        for k in range(3):
            ref[2 * owner + half, :, k * clumps : (k + 1) * clumps] = rows[3 * half + k : 3 * half + k + 1]


def get_rows(ref, owner, clumps):
    return [
        ref[2 * owner + half, :, k * clumps : (k + 1) * clumps] for half in range(2) for k in range(3)
    ]


def group_of(owners):
    return math.gcd(owners, 16)


def loads_kernel(
    count_ref, list_hbm, fluid_hbm, sphere_hbm, offset_hbm, ids_hbm, out_ref,
    list_ref, fluid_ref, sphere_ref, offset_ref, ids_ref, arrived,
    place_ref, fluid_parts_ref, sphere_parts_ref, terms_ref, weight_ref, acc_ref,
):
    fluid_tiles = fluid_ref.shape[1] // TILE
    sphere_tiles = sphere_ref.shape[1] // TILE
    clumps = out_ref.shape[2] // 3
    owners = out_ref.shape[0] // 2

    pairs = (
        (fluid_hbm, fluid_ref),
        (sphere_hbm, sphere_ref),
        (list_hbm, list_ref),
        (offset_hbm, offset_ref),
        (ids_hbm, ids_ref),
    )
    copies = [
        pltpu.make_async_copy(source, target, arrived.at[k]) for k, (source, target) in enumerate(pairs)
    ]
    for copy in copies:
        copy.start()

    acc_ref[...] = jnp.zeros_like(acc_ref)
    copies[0].wait()

    @pl.loop(0, fluid_tiles, unroll=4)
    def _(tile):
        cols = pl.ds(pl.multiple_of(tile * TILE, TILE), TILE)
        state = fluid_ref[:, cols]
        row = lax.broadcasted_iota(jnp.int32, state.shape, 0)
        state = jnp.where(row < 3, state * (1.0 / support_radius) - 1.0, state)
        mass = state[7:8]
        first = jnp.where(row < 7, state * mass, state)
        second = jnp.where(row < 3, state * (mass * state[6:7]), 0.0)
        high, low = split_two(jnp.concatenate([first, second], axis=0))
        both = jnp.concatenate([high, low], axis=0)
        terms_ref[tile] = jnp.concatenate([both, both], axis=1)
        parts = split_three(state[0:3])
        rows = jnp.concatenate([*parts, jnp.ones((3, TILE), f32), jnp.zeros((4, TILE), f32)], axis=0)
        fluid_parts_ref[tile] = rows.astype(bf16)

    copies[1].wait()
    place_ref[...] = sphere_ref[0:3, :] * (1.0 / support_radius) - 1.0
    row = lax.broadcasted_iota(jnp.int32, (9, 3 * TILE), 0)
    column = lax.broadcasted_iota(jnp.int32, (9, 3 * TILE), 1)
    select = jnp.where(lax.rem(row, 3) == column // TILE, -1.0, 0.0)

    @pl.loop(0, sphere_tiles, unroll=4)
    def _(tile):
        cols = pl.ds(pl.multiple_of(tile * TILE, TILE), TILE)
        parts = split_three(place_ref[:, cols])
        lines = [jnp.concatenate([part[k : k + 1] for k in range(3)], axis=1) for part in parts]
        rows = jnp.concatenate([select, *lines, jnp.zeros((4, 3 * TILE), f32)], axis=0)
        sphere_parts_ref[tile] = rows.astype(bf16)

    copies[2].wait()

    def pair_weights(slot, part):
        a = list_ref[0, slot]
        b = list_ref[1, slot]
        apart = lax.dot_general(
            fluid_parts_ref[b], sphere_parts_ref[a], (((0,), (0,)), ((), ())), preferred_element_type=f32
        )
        dx, dy, dz = [apart[:, k * TILE : (k + 1) * TILE] for k in range(3)]
        square = jnp.maximum(dx * dx + dy * dy + dz * dz, 1e-30)
        falloff = jnp.maximum(1.0 - square * lax.rsqrt(square), 0.0)
        high, low = split_two(falloff * falloff * falloff)
        weight_ref[part, 0:TILE, :] = high
        weight_ref[part, TILE:, :] = low

    def add_sums(slot, part, live):
        a = list_ref[0, slot]
        b = list_ref[1, slot]
        cols = pl.ds(pl.multiple_of(a * TILE, TILE), TILE)
        sums = jnp.dot(terms_ref[b], weight_ref[part], preferred_element_type=f32)
        acc_ref[:, cols] += live * (sums[0:16] + sums[16:32])

    count = count_ref[0]
    trips = (count + UNROLL - 1) // UNROLL
    last = list_ref.shape[1] - 1

    for part in range(UNROLL):
        pair_weights(min(part, last), part)

    @pl.loop(1, trips)
    def _(trip):
        for part in range(UNROLL):
            add_sums((trip - 1) * UNROLL + part, part, 1.0)
        for part in range(UNROLL):
            pair_weights(jnp.minimum(trip * UNROLL + part, last), part)

    for part in range(UNROLL):
        slot = (trips - 1) * UNROLL + part
        live = jnp.where(slot < count, 1.0, 0.0).astype(f32)
        add_sums(jnp.clip(slot, 0, last), part, live)

    copies[3].wait()
    copies[4].wait()
    group = group_of(owners)
    width = group * SLOT

    @pl.loop(0, owners // group)
    def _(block):
        cols = pl.ds(pl.multiple_of(block * width, width), width)
        acc = acc_ref[:, cols]
        place = place_ref[:, cols]
        sphere = sphere_ref[:, cols]
        offset = offset_ref[:, cols]
        total = acc[7:8]
        pull = total * place - acc[0:3]
        press = acc[6:7] * place - acc[8:11]
        scale = press_coef * support_radius
        force = scale * (sphere[6:7] * pull + press) + visc_coef * (acc[3:6] - total * sphere[3:6])
        force = [force[k : k + 1] for k in range(3)]
        turn = cross([offset[k : k + 1] for k in range(3)], force)
        loads = jnp.concatenate(force + turn + [jnp.zeros_like(force[0])] * 2, axis=0)
        high, low = split_two(loads)
        both = jnp.concatenate([high, low], axis=0)
        column = lax.broadcasted_iota(jnp.int32, (clumps, SLOT), 0)
        for k in range(group):
            here = pl.ds(pl.multiple_of(block * width + k * SLOT, SLOT), SLOT)
            one_hot = jnp.where(column == ids_ref[:, here], 1.0, 0.0).astype(bf16)
            sums = lax.dot_general(
                both[:, k * SLOT : (k + 1) * SLOT], one_hot, (((1,), (1,)), ((), ())),
                preferred_element_type=f32,
            )
            put_rows(out_ref, block * group + k, sums[0:8] + sums[8:16], clumps)


def update_kernel(arrived_ref, state_ref, inverse_ref, out_ref):
    devices, _, width = out_ref.shape
    clumps = width // 3
    totals = jnp.sum(arrived_ref[...], axis=0)
    first = lax.axis_index("sub") == 0
    for k in range(3):
        cols = slice(k * clumps, (k + 1) * clumps)
        state = jnp.where(first, state_ref[k : k + 1, :], state_ref[k + 3 : k + 4, :])
        factor = jnp.where(first, inverse_ref[0:1, :], inverse_ref[k + 1 : k + 2, :])
        row = state + factor * totals[:, cols]
        if k == 2:
            row = row + jnp.where(first, -gravity_step, 0.0)
        out_ref[:, :, cols] = jnp.broadcast_to(row[None], (devices, 1, clumps))


def velocity_kernel(velocity_ref, offset_ref, ids_ref, clump_ref, sphere_ref):
    owners = velocity_ref.shape[0] // 2
    clumps = velocity_ref.shape[2] // 3
    group = group_of(owners)
    me = lax.axis_index("space")

    @pl.loop(0, owners // group)
    def _(block):
        for k in range(group):
            owner = block * group + k
            rows = get_rows(velocity_ref, owner, clumps) + [jnp.zeros((2, clumps), f32)]
            both = jnp.concatenate(split_two(jnp.concatenate(rows, axis=0)), axis=0)
            here = pl.ds(pl.multiple_of(owner * SLOT, SLOT), SLOT)
            column = lax.broadcasted_iota(jnp.int32, (clumps, SLOT), 0)
            one_hot = jnp.where(column == ids_ref[:, here], 1.0, 0.0).astype(bf16)
            picked = jnp.dot(both, one_hot, preferred_element_type=f32)
            picked = picked[0:8] + picked[8:16]
            offset = offset_ref[:, here]
            turn = cross([picked[3 + i : 4 + i] for i in range(3)], [offset[i : i + 1] for i in range(3)])
            sphere_ref[:, here] = picked[0:3] + jnp.concatenate(turn, axis=0)

    clump_ref[...] = jnp.concatenate(get_rows(velocity_ref, me, clumps), axis=0)


def per_device(
    fluid_state, sphere_state, sphere_offset, tile_list, tile_count, clump_ids, clump_state, clump_inverse
):
    owners = lax.axis_size("space")
    devices = owners * lax.axis_size("sub")
    spheres = sphere_state.shape[1]
    fluid = fluid_state.shape[1]
    clumps = clump_state.shape[1]
    slots = tile_list.shape[0]
    ids = clump_ids.reshape(1, spheres)
    vmem = pl.BlockSpec(memory_space=pltpu.VMEM)
    hbm = pl.BlockSpec(memory_space=pltpu.HBM)
    params = pltpu.CompilerParams(vmem_limit_bytes=48 * 1024 * 1024)

    partial = pl.pallas_call(
        loads_kernel,
        out_shape=pltpu.VMEM((devices, 1, 3 * clumps), f32),
        in_specs=[pl.BlockSpec(memory_space=pltpu.SMEM)] + [hbm] * 5,
        out_specs=vmem,
        scratch_shapes=[
            pltpu.SMEM((2, slots), jnp.int32),
            pltpu.VMEM((8, fluid), f32),
            pltpu.VMEM((7, spheres), f32),
            pltpu.VMEM((3, spheres), f32),
            pltpu.VMEM((1, spheres), jnp.int32),
            pltpu.SemaphoreType.DMA((5,)),
            pltpu.VMEM((3, spheres), f32),
            pltpu.VMEM((fluid // TILE, 16, TILE), bf16),
            pltpu.VMEM((spheres // TILE, 16, 3 * TILE), bf16),
            pltpu.VMEM((fluid // TILE, 32, 2 * TILE), bf16),
            pltpu.VMEM((UNROLL, 2 * TILE, TILE), bf16),
            pltpu.VMEM((16, spheres), f32),
        ],
        compiler_params=params,
        name="clump_loads",
    )(tile_count, *(
        pltpu.with_memory_space_constraint(value, pltpu.HBM)
        for value in (tile_list.T, fluid_state, sphere_state, sphere_offset, ids)
    ))

    axes = ("space", "sub")
    arrived = lax.all_to_all(partial, axes, split_axis=0, concat_axis=0, tiled=True)
    rows = pl.pallas_call(
        update_kernel,
        out_shape=jax.ShapeDtypeStruct((devices, 1, 3 * clumps), f32),
        in_specs=[vmem] * 3,
        out_specs=vmem,
        compiler_params=params,
        name="clump_update",
    )(arrived, clump_state, clump_inverse)
    velocities = lax.all_to_all(rows, axes, split_axis=0, concat_axis=0, tiled=True)

    return pl.pallas_call(
        velocity_kernel,
        out_shape=(
            jax.ShapeDtypeStruct((6, clumps), f32),
            jax.ShapeDtypeStruct((3, spheres), f32),
        ),
        in_specs=[vmem] * 3,
        out_specs=(vmem, vmem),
        compiler_params=params,
        name="sphere_velocities",
    )(velocities, sphere_offset, ids)


def solution(mesh):
    in_specs = (
        P(None, "space"),
        P(None, "space"),
        P(None, "space"),
        P(("space", "sub"), None),
        P(("space", "sub")),
        P("space"),
        P(None, "space"),
        P(None, "space"),
    )
    out_specs = (P(None, "space"), P(None, "space"))
    return jax.shard_map(
        per_device, mesh=mesh, in_specs=in_specs, out_specs=out_specs, check_vma=False
    )
```

```python
import functools
import math

import jax
import jax.numpy as jnp
from jax import lax
from jax.experimental import pallas as pl
from jax.experimental.pallas import tpu as pltpu
from jax.sharding import PartitionSpec as P

TILE = 128
SLOT = 256
UNROLL = 8

support_radius = 0.5
press_coef = 4.0
visc_coef = 1.0
gravity_step = 0.1

f32 = jnp.float32
bf16 = jnp.bfloat16


def split_two(value):
    high = value.astype(bf16)
    return high, (value - high.astype(f32)).astype(bf16)


def split_three(value):
    high = value.astype(bf16).astype(f32)
    middle = (value - high).astype(bf16).astype(f32)
    return high, middle, (value - high) - middle


def cross(left, right):
    return [
        left[1] * right[2] - left[2] * right[1],
        left[2] * right[0] - left[0] * right[2],
        left[0] * right[1] - left[1] * right[0],
    ]


def put_rows(ref, owner, rows, clumps):
    for half in range(2):
        for k in range(3):
            ref[2 * owner + half, :, k * clumps : (k + 1) * clumps] = rows[3 * half + k : 3 * half + k + 1]


def get_rows(ref, owner, clumps):
    return [
        ref[2 * owner + half, :, k * clumps : (k + 1) * clumps] for half in range(2) for k in range(3)
    ]


def group_of(owners):
    return math.gcd(owners, 16)


def loads_kernel(
    count_ref, list_hbm, fluid_hbm, sphere_hbm, offset_hbm, ids_hbm, out_ref,
    list_ref, fluid_ref, sphere_ref, offset_ref, ids_ref, arrived,
    place_ref, wide_ref, terms_ref, weight_ref, acc_ref,
):
    fluid_tiles = fluid_ref.shape[1] // TILE
    clumps = out_ref.shape[2] // 3
    owners = out_ref.shape[0] // 2

    pairs = (
        (fluid_hbm, fluid_ref),
        (sphere_hbm, sphere_ref),
        (list_hbm, list_ref),
        (offset_hbm, offset_ref),
        (ids_hbm, ids_ref),
    )
    copies = [
        pltpu.make_async_copy(source, target, arrived.at[k]) for k, (source, target) in enumerate(pairs)
    ]
    for copy in copies:
        copy.start()

    acc_ref[...] = jnp.zeros_like(acc_ref)
    copies[0].wait()

    row = lax.broadcasted_iota(jnp.int32, (TILE, TILE), 0)
    column = lax.broadcasted_iota(jnp.int32, (TILE, TILE), 1)
    unit = jnp.where(row == column, 1.0, 0.0).astype(bf16)
    ones = jnp.ones((3 * TILE, TILE), bf16)

    @pl.loop(0, fluid_tiles, unroll=4)
    def _(tile):
        cols = pl.ds(pl.multiple_of(tile * TILE, TILE), TILE)
        state = fluid_ref[:, cols]
        row = lax.broadcasted_iota(jnp.int32, state.shape, 0)
        state = jnp.where(row < 3, state * (1.0 / support_radius) - 1.0, state)
        mass = state[7:8]
        first = jnp.where(row < 7, state * mass, state)
        second = jnp.where(row < 3, state * (mass * state[6:7]), 0.0)
        high, low = split_two(jnp.concatenate([first, second], axis=0))
        both = jnp.concatenate([high, low], axis=0)
        terms_ref[tile] = jnp.concatenate([both, both], axis=1)
        parts = [part.astype(bf16) for part in split_three(state[0:3])]
        for k in range(3):
            lines = [unit * jnp.broadcast_to(part[k : k + 1], (TILE, TILE)) for part in parts]
            wide_ref[k, cols, :] = jnp.dot(
                jnp.concatenate(lines, axis=1), ones, preferred_element_type=f32
            )

    copies[1].wait()
    place_ref[...] = sphere_ref[0:3, :] * (1.0 / support_radius) - 1.0
    copies[2].wait()

    def pair_weights(slot, part):
        a = list_ref[0, slot]
        b = list_ref[1, slot]
        cols = pl.ds(pl.multiple_of(a * TILE, TILE), TILE)
        rows = pl.ds(pl.multiple_of(b * TILE, TILE), TILE)
        dx = place_ref[0:1, cols] - wide_ref[0, rows, :]
        dy = place_ref[1:2, cols] - wide_ref[1, rows, :]
        dz = place_ref[2:3, cols] - wide_ref[2, rows, :]
        square = jnp.maximum(dx * dx + dy * dy + dz * dz, 1e-30)
        falloff = jnp.maximum(1.0 - square * lax.rsqrt(square), 0.0)
        high, low = split_two(falloff * falloff * falloff)
        weight_ref[part, 0:TILE, :] = high
        weight_ref[part, TILE:, :] = low

    def add_sums(slot, part, live):
        a = list_ref[0, slot]
        b = list_ref[1, slot]
        cols = pl.ds(pl.multiple_of(a * TILE, TILE), TILE)
        sums = jnp.dot(terms_ref[b], weight_ref[part], preferred_element_type=f32)
        acc_ref[:, cols] += live * (sums[0:16] + sums[16:32])

    count = count_ref[0]
    trips = (count + UNROLL - 1) // UNROLL
    last = list_ref.shape[1] - 1

    for part in range(UNROLL):
        pair_weights(min(part, last), part)

    @pl.loop(1, trips)
    def _(trip):
        for part in range(UNROLL):
            add_sums((trip - 1) * UNROLL + part, part, 1.0)
        for part in range(UNROLL):
            pair_weights(jnp.minimum(trip * UNROLL + part, last), part)

    for part in range(UNROLL):
        slot = (trips - 1) * UNROLL + part
        live = jnp.where(slot < count, 1.0, 0.0).astype(f32)
        add_sums(jnp.clip(slot, 0, last), part, live)

    copies[3].wait()
    copies[4].wait()
    group = group_of(owners)
    width = group * SLOT

    @pl.loop(0, owners // group)
    def _(block):
        cols = pl.ds(pl.multiple_of(block * width, width), width)
        acc = acc_ref[:, cols]
        place = place_ref[:, cols]
        sphere = sphere_ref[:, cols]
        offset = offset_ref[:, cols]
        total = acc[7:8]
        pull = total * place - acc[0:3]
        press = acc[6:7] * place - acc[8:11]
        scale = press_coef * support_radius
        force = scale * (sphere[6:7] * pull + press) + visc_coef * (acc[3:6] - total * sphere[3:6])
        force = [force[k : k + 1] for k in range(3)]
        turn = cross([offset[k : k + 1] for k in range(3)], force)
        loads = jnp.concatenate(force + turn + [jnp.zeros_like(force[0])] * 2, axis=0)
        high, low = split_two(loads)
        both = jnp.concatenate([high, low], axis=0)
        column = lax.broadcasted_iota(jnp.int32, (clumps, SLOT), 0)
        for k in range(group):
            here = pl.ds(pl.multiple_of(block * width + k * SLOT, SLOT), SLOT)
            one_hot = jnp.where(column == ids_ref[:, here], 1.0, 0.0).astype(bf16)
            sums = lax.dot_general(
                both[:, k * SLOT : (k + 1) * SLOT], one_hot, (((1,), (1,)), ((), ())),
                preferred_element_type=f32,
            )
            put_rows(out_ref, block * group + k, sums[0:8] + sums[8:16], clumps)


def update_kernel(arrived_ref, state_ref, inverse_ref, out_ref):
    devices, _, width = out_ref.shape
    clumps = width // 3
    totals = jnp.sum(arrived_ref[...], axis=0)
    first = lax.axis_index("sub") == 0
    for k in range(3):
        cols = slice(k * clumps, (k + 1) * clumps)
        state = jnp.where(first, state_ref[k : k + 1, :], state_ref[k + 3 : k + 4, :])
        factor = jnp.where(first, inverse_ref[0:1, :], inverse_ref[k + 1 : k + 2, :])
        row = state + factor * totals[:, cols]
        if k == 2:
            row = row + jnp.where(first, -gravity_step, 0.0)
        out_ref[:, :, cols] = jnp.broadcast_to(row[None], (devices, 1, clumps))


def velocity_kernel(velocity_ref, offset_ref, ids_ref, clump_ref, sphere_ref):
    owners = velocity_ref.shape[0] // 2
    clumps = velocity_ref.shape[2] // 3
    group = group_of(owners)
    me = lax.axis_index("space")

    @pl.loop(0, owners // group)
    def _(block):
        for k in range(group):
            owner = block * group + k
            rows = get_rows(velocity_ref, owner, clumps) + [jnp.zeros((2, clumps), f32)]
            both = jnp.concatenate(split_two(jnp.concatenate(rows, axis=0)), axis=0)
            here = pl.ds(pl.multiple_of(owner * SLOT, SLOT), SLOT)
            column = lax.broadcasted_iota(jnp.int32, (clumps, SLOT), 0)
            one_hot = jnp.where(column == ids_ref[:, here], 1.0, 0.0).astype(bf16)
            picked = jnp.dot(both, one_hot, preferred_element_type=f32)
            picked = picked[0:8] + picked[8:16]
            offset = offset_ref[:, here]
            turn = cross([picked[3 + i : 4 + i] for i in range(3)], [offset[i : i + 1] for i in range(3)])
            sphere_ref[:, here] = picked[0:3] + jnp.concatenate(turn, axis=0)

    clump_ref[...] = jnp.concatenate(get_rows(velocity_ref, me, clumps), axis=0)


def per_device(
    fluid_state, sphere_state, sphere_offset, tile_list, tile_count, clump_ids, clump_state, clump_inverse
):
    owners = lax.axis_size("space")
    devices = owners * lax.axis_size("sub")
    spheres = sphere_state.shape[1]
    fluid = fluid_state.shape[1]
    clumps = clump_state.shape[1]
    slots = tile_list.shape[0]
    ids = clump_ids.reshape(1, spheres)
    vmem = pl.BlockSpec(memory_space=pltpu.VMEM)
    hbm = pl.BlockSpec(memory_space=pltpu.HBM)
    params = pltpu.CompilerParams(vmem_limit_bytes=48 * 1024 * 1024)

    partial = pl.pallas_call(
        loads_kernel,
        out_shape=pltpu.VMEM((devices, 1, 3 * clumps), f32),
        in_specs=[pl.BlockSpec(memory_space=pltpu.SMEM)] + [hbm] * 5,
        out_specs=vmem,
        scratch_shapes=[
            pltpu.SMEM((2, slots), jnp.int32),
            pltpu.VMEM((8, fluid), f32),
            pltpu.VMEM((7, spheres), f32),
            pltpu.VMEM((3, spheres), f32),
            pltpu.VMEM((1, spheres), jnp.int32),
            pltpu.SemaphoreType.DMA((5,)),
            pltpu.VMEM((3, spheres), f32),
            pltpu.VMEM((3, fluid, TILE), f32),
            pltpu.VMEM((fluid // TILE, 32, 2 * TILE), bf16),
            pltpu.VMEM((UNROLL, 2 * TILE, TILE), bf16),
            pltpu.VMEM((16, spheres), f32),
        ],
        compiler_params=params,
        name="clump_loads",
    )(tile_count, *(
        pltpu.with_memory_space_constraint(value, pltpu.HBM)
        for value in (tile_list.T, fluid_state, sphere_state, sphere_offset, ids)
    ))

    axes = ("space", "sub")
    arrived = lax.all_to_all(partial, axes, split_axis=0, concat_axis=0, tiled=True)
    rows = pl.pallas_call(
        update_kernel,
        out_shape=jax.ShapeDtypeStruct((devices, 1, 3 * clumps), f32),
        in_specs=[vmem] * 3,
        out_specs=vmem,
        compiler_params=params,
        name="clump_update",
    )(arrived, clump_state, clump_inverse)
    velocities = lax.all_to_all(rows, axes, split_axis=0, concat_axis=0, tiled=True)

    return pl.pallas_call(
        velocity_kernel,
        out_shape=(
            jax.ShapeDtypeStruct((6, clumps), f32),
            jax.ShapeDtypeStruct((3, spheres), f32),
        ),
        in_specs=[vmem] * 3,
        out_specs=(vmem, vmem),
        compiler_params=params,
        name="sphere_velocities",
    )(velocities, sphere_offset, ids)


def solution(mesh):
    in_specs = (
        P(None, "space"),
        P(None, "space"),
        P(None, "space"),
        P(("space", "sub"), None),
        P(("space", "sub")),
        P("space"),
        P(None, "space"),
        P(None, "space"),
    )
    out_specs = (P(None, "space"), P(None, "space"))
    return jax.shard_map(
        per_device, mesh=mesh, in_specs=in_specs, out_specs=out_specs, check_vma=False
    )
```

```python
import functools
import math

import jax
import jax.numpy as jnp
from jax import lax
from jax.experimental import pallas as pl
from jax.experimental.pallas import tpu as pltpu
from jax.sharding import PartitionSpec as P

TILE = 128
HALF = TILE // 2
SLOT = 256
UNROLL = 4

support_radius = 0.5
press_coef = 4.0
visc_coef = 1.0
gravity_step = 0.1

f32 = jnp.float32
bf16 = jnp.bfloat16


def split_two(value):
    high = value.astype(bf16)
    return high, (value - high.astype(f32)).astype(bf16)


def cross(left, right):
    return [
        left[1] * right[2] - left[2] * right[1],
        left[2] * right[0] - left[0] * right[2],
        left[0] * right[1] - left[1] * right[0],
    ]


def put_rows(ref, owner, rows, clumps):
    for half in range(2):
        for k in range(3):
            ref[2 * owner + half, :, k * clumps : (k + 1) * clumps] = rows[3 * half + k : 3 * half + k + 1]


def get_rows(ref, owner, clumps):
    return [
        ref[2 * owner + half, :, k * clumps : (k + 1) * clumps] for half in range(2) for k in range(3)
    ]


def group_of(owners):
    return math.gcd(owners, 16)


def loads_kernel(
    count_ref, list_hbm, fluid_hbm, sphere_hbm, offset_hbm, ids_hbm, out_ref,
    list_ref, fluid_ref, sphere_ref, offset_ref, ids_ref, arrived,
    place_ref, lines_ref, lanes_ref, wide_ref, terms_ref, weight_ref, acc_ref,
):
    fluid_tiles = fluid_ref.shape[1] // TILE
    clumps = out_ref.shape[2] // 3
    owners = out_ref.shape[0] // 2

    pairs = (
        (fluid_hbm, fluid_ref),
        (sphere_hbm, sphere_ref),
        (list_hbm, list_ref),
        (offset_hbm, offset_ref),
        (ids_hbm, ids_ref),
    )
    copies = [
        pltpu.make_async_copy(source, target, arrived.at[k]) for k, (source, target) in enumerate(pairs)
    ]
    for copy in copies:
        copy.start()

    acc_ref[...] = jnp.zeros_like(acc_ref)
    copies[0].wait()

    assert 3 * fluid_tiles <= TILE
    lines_ref[...] = jnp.zeros_like(lines_ref)
    for k in range(3):
        for tile in range(fluid_tiles):
            at = k * fluid_tiles + tile
            lines_ref[at : at + 1, :] = fluid_ref[k : k + 1, tile * TILE : (tile + 1) * TILE]
    lanes_ref[...] = lines_ref[...].T * (1.0 / support_radius) - 1.0

    def spread(k, tile, rows):
        lanes = lanes_ref[rows, :]
        lane = jnp.full(lanes.shape, k * fluid_tiles + tile, jnp.int32)
        return jnp.take_along_axis(lanes, lane, axis=1, mode="promise_in_bounds")

    @pl.loop(0, fluid_tiles, unroll=4)
    def _(tile):
        wide_ref[tile, 0:TILE, :] = spread(0, tile, slice(0, TILE))
        wide_ref[tile, TILE:, :] = spread(1, tile, slice(0, HALF))
        cols = pl.ds(pl.multiple_of(tile * TILE, TILE), TILE)
        state = fluid_ref[:, cols]
        row = lax.broadcasted_iota(jnp.int32, state.shape, 0)
        state = jnp.where(row < 3, state * (1.0 / support_radius) - 1.0, state)
        mass = state[7:8]
        first = jnp.where(row < 7, state * mass, state)
        second = jnp.where(row < 3, state * (mass * state[6:7]), 0.0)
        high, low = split_two(jnp.concatenate([first, second], axis=0))
        both = jnp.concatenate([high, low], axis=0)
        terms_ref[tile] = jnp.concatenate([both, both], axis=1)

    copies[1].wait()
    place_ref[...] = sphere_ref[0:3, :] * (1.0 / support_radius) - 1.0
    copies[2].wait()

    def pair_weights(slot, part):
        a = list_ref[0, slot]
        b = list_ref[1, slot]
        cols = pl.ds(pl.multiple_of(a * TILE, TILE), TILE)
        for half in range(2):
            rows = slice(half * HALF, (half + 1) * HALF)
            x = wide_ref[b, rows, :]
            y = wide_ref[b, TILE:, :] if half == 0 else spread(1, b, rows)
            dx = place_ref[0:1, cols] - x
            dy = place_ref[1:2, cols] - y
            dz = place_ref[2:3, cols] - spread(2, b, rows)
            square = jnp.maximum(dx * dx + dy * dy + dz * dz, 1e-30)
            falloff = jnp.maximum(1.0 - square * lax.rsqrt(square), 0.0)
            high, low = split_two(falloff * falloff * falloff)
            weight_ref[part, rows, :] = high
            weight_ref[part, TILE + half * HALF : TILE + (half + 1) * HALF, :] = low

    def add_sums(slot, part, live):
        a = list_ref[0, slot]
        b = list_ref[1, slot]
        cols = pl.ds(pl.multiple_of(a * TILE, TILE), TILE)
        sums = jnp.dot(terms_ref[b], weight_ref[part], preferred_element_type=f32)
        acc_ref[:, cols] += live * (sums[0:16] + sums[16:32])

    count = count_ref[0]
    trips = (count + UNROLL - 1) // UNROLL
    last = list_ref.shape[1] - 1

    for part in range(UNROLL):
        pair_weights(min(part, last), part)

    @pl.loop(1, trips)
    def _(trip):
        for part in range(UNROLL):
            add_sums((trip - 1) * UNROLL + part, part, 1.0)
        for part in range(UNROLL):
            pair_weights(jnp.minimum(trip * UNROLL + part, last), part)

    for part in range(UNROLL):
        slot = (trips - 1) * UNROLL + part
        live = jnp.where(slot < count, 1.0, 0.0).astype(f32)
        add_sums(jnp.clip(slot, 0, last), part, live)

    copies[3].wait()
    copies[4].wait()
    group = group_of(owners)
    width = group * SLOT

    @pl.loop(0, owners // group)
    def _(block):
        cols = pl.ds(pl.multiple_of(block * width, width), width)
        acc = acc_ref[:, cols]
        place = place_ref[:, cols]
        sphere = sphere_ref[:, cols]
        offset = offset_ref[:, cols]
        total = acc[7:8]
        pull = total * place - acc[0:3]
        press = acc[6:7] * place - acc[8:11]
        scale = press_coef * support_radius
        force = scale * (sphere[6:7] * pull + press) + visc_coef * (acc[3:6] - total * sphere[3:6])
        force = [force[k : k + 1] for k in range(3)]
        turn = cross([offset[k : k + 1] for k in range(3)], force)
        loads = jnp.concatenate(force + turn + [jnp.zeros_like(force[0])] * 2, axis=0)
        high, low = split_two(loads)
        both = jnp.concatenate([high, low], axis=0)
        column = lax.broadcasted_iota(jnp.int32, (clumps, SLOT), 0)
        for k in range(group):
            here = pl.ds(pl.multiple_of(block * width + k * SLOT, SLOT), SLOT)
            one_hot = jnp.where(column == ids_ref[:, here], 1.0, 0.0).astype(bf16)
            sums = lax.dot_general(
                both[:, k * SLOT : (k + 1) * SLOT], one_hot, (((1,), (1,)), ((), ())),
                preferred_element_type=f32,
            )
            put_rows(out_ref, block * group + k, sums[0:8] + sums[8:16], clumps)


def update_kernel(arrived_ref, state_ref, inverse_ref, out_ref):
    devices, _, width = out_ref.shape
    clumps = width // 3
    totals = jnp.sum(arrived_ref[...], axis=0)
    first = lax.axis_index("sub") == 0
    for k in range(3):
        cols = slice(k * clumps, (k + 1) * clumps)
        state = jnp.where(first, state_ref[k : k + 1, :], state_ref[k + 3 : k + 4, :])
        factor = jnp.where(first, inverse_ref[0:1, :], inverse_ref[k + 1 : k + 2, :])
        row = state + factor * totals[:, cols]
        if k == 2:
            row = row + jnp.where(first, -gravity_step, 0.0)
        out_ref[:, :, cols] = jnp.broadcast_to(row[None], (devices, 1, clumps))


def velocity_kernel(velocity_ref, offset_ref, ids_ref, clump_ref, sphere_ref):
    owners = velocity_ref.shape[0] // 2
    clumps = velocity_ref.shape[2] // 3
    group = group_of(owners)
    me = lax.axis_index("space")

    @pl.loop(0, owners // group)
    def _(block):
        for k in range(group):
            owner = block * group + k
            rows = get_rows(velocity_ref, owner, clumps) + [jnp.zeros((2, clumps), f32)]
            both = jnp.concatenate(split_two(jnp.concatenate(rows, axis=0)), axis=0)
            here = pl.ds(pl.multiple_of(owner * SLOT, SLOT), SLOT)
            column = lax.broadcasted_iota(jnp.int32, (clumps, SLOT), 0)
            one_hot = jnp.where(column == ids_ref[:, here], 1.0, 0.0).astype(bf16)
            picked = jnp.dot(both, one_hot, preferred_element_type=f32)
            picked = picked[0:8] + picked[8:16]
            offset = offset_ref[:, here]
            turn = cross([picked[3 + i : 4 + i] for i in range(3)], [offset[i : i + 1] for i in range(3)])
            sphere_ref[:, here] = picked[0:3] + jnp.concatenate(turn, axis=0)

    clump_ref[...] = jnp.concatenate(get_rows(velocity_ref, me, clumps), axis=0)


def per_device(
    fluid_state, sphere_state, sphere_offset, tile_list, tile_count, clump_ids, clump_state, clump_inverse
):
    owners = lax.axis_size("space")
    devices = owners * lax.axis_size("sub")
    spheres = sphere_state.shape[1]
    fluid = fluid_state.shape[1]
    clumps = clump_state.shape[1]
    slots = tile_list.shape[0]
    ids = clump_ids.reshape(1, spheres)
    vmem = pl.BlockSpec(memory_space=pltpu.VMEM)
    hbm = pl.BlockSpec(memory_space=pltpu.HBM)
    params = pltpu.CompilerParams(vmem_limit_bytes=48 * 1024 * 1024)

    partial = pl.pallas_call(
        loads_kernel,
        out_shape=pltpu.VMEM((devices, 1, 3 * clumps), f32),
        in_specs=[pl.BlockSpec(memory_space=pltpu.SMEM)] + [hbm] * 5,
        out_specs=vmem,
        scratch_shapes=[
            pltpu.SMEM((2, slots), jnp.int32),
            pltpu.VMEM((8, fluid), f32),
            pltpu.VMEM((7, spheres), f32),
            pltpu.VMEM((3, spheres), f32),
            pltpu.VMEM((1, spheres), jnp.int32),
            pltpu.SemaphoreType.DMA((5,)),
            pltpu.VMEM((3, spheres), f32),
            pltpu.VMEM((TILE, TILE), f32),
            pltpu.VMEM((TILE, TILE), f32),
            pltpu.VMEM((fluid // TILE, TILE + HALF, TILE), f32),
            pltpu.VMEM((fluid // TILE, 32, 2 * TILE), bf16),
            pltpu.VMEM((UNROLL, 2 * TILE, TILE), bf16),
            pltpu.VMEM((16, spheres), f32),
        ],
        compiler_params=params,
        name="clump_loads",
    )(tile_count, *(
        pltpu.with_memory_space_constraint(value, pltpu.HBM)
        for value in (tile_list.T, fluid_state, sphere_state, sphere_offset, ids)
    ))

    axes = ("space", "sub")
    arrived = lax.all_to_all(partial, axes, split_axis=0, concat_axis=0, tiled=True)
    rows = pl.pallas_call(
        update_kernel,
        out_shape=jax.ShapeDtypeStruct((devices, 1, 3 * clumps), f32),
        in_specs=[vmem] * 3,
        out_specs=vmem,
        compiler_params=params,
        name="clump_update",
    )(arrived, clump_state, clump_inverse)
    velocities = lax.all_to_all(rows, axes, split_axis=0, concat_axis=0, tiled=True)

    return pl.pallas_call(
        velocity_kernel,
        out_shape=(
            jax.ShapeDtypeStruct((6, clumps), f32),
            jax.ShapeDtypeStruct((3, spheres), f32),
        ),
        in_specs=[vmem] * 3,
        out_specs=(vmem, vmem),
        compiler_params=params,
        name="sphere_velocities",
    )(velocities, sphere_offset, ids)


def solution(mesh):
    in_specs = (
        P(None, "space"),
        P(None, "space"),
        P(None, "space"),
        P(("space", "sub"), None),
        P(("space", "sub")),
        P("space"),
        P(None, "space"),
        P(None, "space"),
    )
    out_specs = (P(None, "space"), P(None, "space"))
    return jax.shard_map(
        per_device, mesh=mesh, in_specs=in_specs, out_specs=out_specs, check_vma=False
    )
```

```python
import functools
import math

import jax
import jax.numpy as jnp
from jax import lax
from jax.experimental import pallas as pl
from jax.experimental.pallas import tpu as pltpu
from jax.sharding import PartitionSpec as P

TILE = 128
LANES = 16
BLOCK = TILE // LANES
SLOT = 256
UNROLL = 8

support_radius = 0.5
press_coef = 4.0
visc_coef = 1.0
gravity_step = 0.1

f32 = jnp.float32
bf16 = jnp.bfloat16


def split_two(value):
    high = value.astype(bf16)
    return high, (value - high.astype(f32)).astype(bf16)


def split_three(value):
    high = value.astype(bf16).astype(f32)
    middle = (value - high).astype(bf16).astype(f32)
    return high, middle, (value - high) - middle


def cross(left, right):
    return [
        left[1] * right[2] - left[2] * right[1],
        left[2] * right[0] - left[0] * right[2],
        left[0] * right[1] - left[1] * right[0],
    ]


def put_rows(ref, owner, rows, clumps):
    for half in range(2):
        for k in range(3):
            ref[2 * owner + half, :, k * clumps : (k + 1) * clumps] = rows[3 * half + k : 3 * half + k + 1]


def get_rows(ref, owner, clumps):
    return [
        ref[2 * owner + half, :, k * clumps : (k + 1) * clumps] for half in range(2) for k in range(3)
    ]


def group_of(owners):
    return math.gcd(owners, 16)


def loads_kernel(
    count_ref, list_hbm, fluid_hbm, sphere_hbm, offset_hbm, ids_hbm, out_ref,
    list_ref, fluid_ref, sphere_ref, offset_ref, ids_ref, arrived,
    place_ref, choose_ref, wide_ref, terms_ref, weight_ref, acc_ref,
):
    fluid_tiles = fluid_ref.shape[1] // TILE
    clumps = out_ref.shape[2] // 3
    owners = out_ref.shape[0] // 2

    pairs = (
        (fluid_hbm, fluid_ref),
        (sphere_hbm, sphere_ref),
        (list_hbm, list_ref),
        (offset_hbm, offset_ref),
        (ids_hbm, ids_ref),
    )
    copies = [
        pltpu.make_async_copy(source, target, arrived.at[k]) for k, (source, target) in enumerate(pairs)
    ]
    for copy in copies:
        copy.start()

    acc_ref[...] = jnp.zeros_like(acc_ref)

    lane = lax.broadcasted_iota(jnp.int32, (TILE, 3 * TILE), 0)
    target = lax.broadcasted_iota(jnp.int32, (TILE, 3 * TILE), 1) // TILE
    part = lane % LANES
    wanted = (part == target) | (part == target + 3) | (part == target + 6)
    for j in range(BLOCK):
        choose_ref[j] = jnp.where(wanted & (lane // LANES == j), 1.0, 0.0).astype(bf16)
    copies[0].wait()

    @pl.loop(0, fluid_tiles // BLOCK)
    def _(block):
        row = lax.broadcasted_iota(jnp.int32, (8, TILE), 0)
        lines = []
        for j in range(BLOCK):
            tile = block * BLOCK + j
            state = fluid_ref[:, pl.ds(pl.multiple_of(tile * TILE, TILE), TILE)]
            state = jnp.where(row < 3, state * (1.0 / support_radius) - 1.0, state)
            mass = state[7:8]
            first = jnp.where(row < 7, state * mass, state)
            second = jnp.where(row < 3, state * (mass * state[6:7]), 0.0)
            high, low = split_two(jnp.concatenate([first, second], axis=0))
            both = jnp.concatenate([high, low], axis=0)
            terms_ref[tile] = jnp.concatenate([both, both], axis=1)
            lines += [*split_three(state[0:3]), jnp.zeros((LANES - 9, TILE), f32)]
        turned = jnp.concatenate(lines, axis=0).T.astype(bf16)
        for j in range(BLOCK):
            wide_ref[block * BLOCK + j] = jnp.dot(turned, choose_ref[j], preferred_element_type=f32)

    copies[1].wait()
    place_ref[...] = sphere_ref[0:3, :] * (1.0 / support_radius) - 1.0
    copies[2].wait()

    def pair_weights(slot, part):
        a = list_ref[0, slot]
        b = list_ref[1, slot]
        cols = pl.ds(pl.multiple_of(a * TILE, TILE), TILE)
        dx, dy, dz = [
            place_ref[k : k + 1, cols] - wide_ref[b, :, k * TILE : (k + 1) * TILE] for k in range(3)
        ]
        square = jnp.maximum(dx * dx + dy * dy + dz * dz, 1e-30)
        falloff = jnp.maximum(1.0 - square * lax.rsqrt(square), 0.0)
        high, low = split_two(falloff * falloff * falloff)
        weight_ref[part, 0:TILE, :] = high
        weight_ref[part, TILE:, :] = low

    def add_sums(slot, part, live):
        a = list_ref[0, slot]
        b = list_ref[1, slot]
        cols = pl.ds(pl.multiple_of(a * TILE, TILE), TILE)
        sums = jnp.dot(terms_ref[b], weight_ref[part], preferred_element_type=f32)
        acc_ref[:, cols] += live * (sums[0:16] + sums[16:32])

    count = count_ref[0]
    trips = (count + UNROLL - 1) // UNROLL
    last = list_ref.shape[1] - 1

    for part in range(UNROLL):
        pair_weights(min(part, last), part)

    @pl.loop(1, trips)
    def _(trip):
        for part in range(UNROLL):
            add_sums((trip - 1) * UNROLL + part, part, 1.0)
        for part in range(UNROLL):
            pair_weights(jnp.minimum(trip * UNROLL + part, last), part)

    for part in range(UNROLL):
        slot = (trips - 1) * UNROLL + part
        live = jnp.where(slot < count, 1.0, 0.0).astype(f32)
        add_sums(jnp.clip(slot, 0, last), part, live)

    copies[3].wait()
    copies[4].wait()
    group = group_of(owners)
    width = group * SLOT

    @pl.loop(0, owners // group)
    def _(block):
        cols = pl.ds(pl.multiple_of(block * width, width), width)
        acc = acc_ref[:, cols]
        place = place_ref[:, cols]
        sphere = sphere_ref[:, cols]
        offset = offset_ref[:, cols]
        total = acc[7:8]
        pull = total * place - acc[0:3]
        press = acc[6:7] * place - acc[8:11]
        scale = press_coef * support_radius
        force = scale * (sphere[6:7] * pull + press) + visc_coef * (acc[3:6] - total * sphere[3:6])
        force = [force[k : k + 1] for k in range(3)]
        turn = cross([offset[k : k + 1] for k in range(3)], force)
        loads = jnp.concatenate(force + turn + [jnp.zeros_like(force[0])] * 2, axis=0)
        high, low = split_two(loads)
        both = jnp.concatenate([high, low], axis=0)
        column = lax.broadcasted_iota(jnp.int32, (clumps, SLOT), 0)
        for k in range(group):
            here = pl.ds(pl.multiple_of(block * width + k * SLOT, SLOT), SLOT)
            one_hot = jnp.where(column == ids_ref[:, here], 1.0, 0.0).astype(bf16)
            sums = lax.dot_general(
                both[:, k * SLOT : (k + 1) * SLOT], one_hot, (((1,), (1,)), ((), ())),
                preferred_element_type=f32,
            )
            put_rows(out_ref, block * group + k, sums[0:8] + sums[8:16], clumps)


def update_kernel(arrived_ref, state_ref, inverse_ref, out_ref):
    devices, _, width = out_ref.shape
    clumps = width // 3
    totals = jnp.sum(arrived_ref[...], axis=0)
    first = lax.axis_index("sub") == 0
    for k in range(3):
        cols = slice(k * clumps, (k + 1) * clumps)
        state = jnp.where(first, state_ref[k : k + 1, :], state_ref[k + 3 : k + 4, :])
        factor = jnp.where(first, inverse_ref[0:1, :], inverse_ref[k + 1 : k + 2, :])
        row = state + factor * totals[:, cols]
        if k == 2:
            row = row + jnp.where(first, -gravity_step, 0.0)
        out_ref[:, :, cols] = jnp.broadcast_to(row[None], (devices, 1, clumps))


def velocity_kernel(velocity_ref, offset_ref, ids_ref, clump_ref, sphere_ref):
    owners = velocity_ref.shape[0] // 2
    clumps = velocity_ref.shape[2] // 3
    group = group_of(owners)
    me = lax.axis_index("space")

    @pl.loop(0, owners // group)
    def _(block):
        for k in range(group):
            owner = block * group + k
            rows = get_rows(velocity_ref, owner, clumps) + [jnp.zeros((2, clumps), f32)]
            both = jnp.concatenate(split_two(jnp.concatenate(rows, axis=0)), axis=0)
            here = pl.ds(pl.multiple_of(owner * SLOT, SLOT), SLOT)
            column = lax.broadcasted_iota(jnp.int32, (clumps, SLOT), 0)
            one_hot = jnp.where(column == ids_ref[:, here], 1.0, 0.0).astype(bf16)
            picked = jnp.dot(both, one_hot, preferred_element_type=f32)
            picked = picked[0:8] + picked[8:16]
            offset = offset_ref[:, here]
            turn = cross([picked[3 + i : 4 + i] for i in range(3)], [offset[i : i + 1] for i in range(3)])
            sphere_ref[:, here] = picked[0:3] + jnp.concatenate(turn, axis=0)

    clump_ref[...] = jnp.concatenate(get_rows(velocity_ref, me, clumps), axis=0)


def per_device(
    fluid_state, sphere_state, sphere_offset, tile_list, tile_count, clump_ids, clump_state, clump_inverse
):
    owners = lax.axis_size("space")
    devices = owners * lax.axis_size("sub")
    spheres = sphere_state.shape[1]
    fluid = fluid_state.shape[1]
    clumps = clump_state.shape[1]
    slots = tile_list.shape[0]
    ids = clump_ids.reshape(1, spheres)
    vmem = pl.BlockSpec(memory_space=pltpu.VMEM)
    hbm = pl.BlockSpec(memory_space=pltpu.HBM)
    params = pltpu.CompilerParams(vmem_limit_bytes=48 * 1024 * 1024)

    partial = pl.pallas_call(
        loads_kernel,
        out_shape=pltpu.VMEM((devices, 1, 3 * clumps), f32),
        in_specs=[pl.BlockSpec(memory_space=pltpu.SMEM)] + [hbm] * 5,
        out_specs=vmem,
        scratch_shapes=[
            pltpu.SMEM((2, slots), jnp.int32),
            pltpu.VMEM((8, fluid), f32),
            pltpu.VMEM((7, spheres), f32),
            pltpu.VMEM((3, spheres), f32),
            pltpu.VMEM((1, spheres), jnp.int32),
            pltpu.SemaphoreType.DMA((5,)),
            pltpu.VMEM((3, spheres), f32),
            pltpu.VMEM((BLOCK, TILE, 3 * TILE), bf16),
            pltpu.VMEM((fluid // TILE, TILE, 3 * TILE), f32),
            pltpu.VMEM((fluid // TILE, 32, 2 * TILE), bf16),
            pltpu.VMEM((UNROLL, 2 * TILE, TILE), bf16),
            pltpu.VMEM((16, spheres), f32),
        ],
        compiler_params=params,
        name="clump_loads",
    )(tile_count, *(
        pltpu.with_memory_space_constraint(value, pltpu.HBM)
        for value in (tile_list.T, fluid_state, sphere_state, sphere_offset, ids)
    ))

    axes = ("space", "sub")
    arrived = lax.all_to_all(partial, axes, split_axis=0, concat_axis=0, tiled=True)
    rows = pl.pallas_call(
        update_kernel,
        out_shape=jax.ShapeDtypeStruct((devices, 1, 3 * clumps), f32),
        in_specs=[vmem] * 3,
        out_specs=vmem,
        compiler_params=params,
        name="clump_update",
    )(arrived, clump_state, clump_inverse)
    velocities = lax.all_to_all(rows, axes, split_axis=0, concat_axis=0, tiled=True)

    return pl.pallas_call(
        velocity_kernel,
        out_shape=(
            jax.ShapeDtypeStruct((6, clumps), f32),
            jax.ShapeDtypeStruct((3, spheres), f32),
        ),
        in_specs=[vmem] * 3,
        out_specs=(vmem, vmem),
        compiler_params=params,
        name="sphere_velocities",
    )(velocities, sphere_offset, ids)


def solution(mesh):
    in_specs = (
        P(None, "space"),
        P(None, "space"),
        P(None, "space"),
        P(("space", "sub"), None),
        P(("space", "sub")),
        P("space"),
        P(None, "space"),
        P(None, "space"),
    )
    out_specs = (P(None, "space"), P(None, "space"))
    return jax.shard_map(
        per_device, mesh=mesh, in_specs=in_specs, out_specs=out_specs, check_vma=False
    )
```

```python
import functools
import math

import jax
import jax.numpy as jnp
from jax import lax
from jax.experimental import pallas as pl
from jax.experimental.pallas import tpu as pltpu
from jax.sharding import PartitionSpec as P

TILE = 128
LANES = 16
BLOCK = TILE // LANES
SLOT = 256
UNROLL = 8

support_radius = 0.5
press_coef = 4.0
visc_coef = 1.0
gravity_step = 0.1

f32 = jnp.float32
bf16 = jnp.bfloat16


def split_two(value):
    high = value.astype(bf16)
    return high, (value - high.astype(f32)).astype(bf16)


def split_three(value):
    high = value.astype(bf16).astype(f32)
    middle = (value - high).astype(bf16).astype(f32)
    return high, middle, (value - high) - middle


def cross(left, right):
    return [
        left[1] * right[2] - left[2] * right[1],
        left[2] * right[0] - left[0] * right[2],
        left[0] * right[1] - left[1] * right[0],
    ]


def put_rows(ref, owner, rows):
    clumps = rows.shape[1]
    for k in range(3):
        ref[owner, :, k * clumps : (k + 1) * clumps] = rows[k : k + 1]


def get_rows(ref, owner):
    clumps = ref.shape[2] // 3
    return [ref[owner, :, k * clumps : (k + 1) * clumps] for k in range(3)]


def swap_cores(value):
    return lax.ppermute(value, "sub", [(0, 1), (1, 0)])


def group_of(owners):
    return math.gcd(owners, 16)


def loads_kernel(
    count_ref, list_hbm, fluid_hbm, sphere_hbm, offset_hbm, ids_hbm, keep_ref, send_ref,
    list_ref, fluid_ref, sphere_ref, offset_ref, ids_ref, arrived,
    place_ref, choose_ref, wide_ref, terms_ref, weight_ref, acc_ref,
):
    fluid_tiles = fluid_ref.shape[1] // TILE
    clumps = keep_ref.shape[2] // 3
    owners = keep_ref.shape[0]
    first_core = lax.axis_index("sub") == 0

    pairs = (
        (fluid_hbm, fluid_ref),
        (sphere_hbm, sphere_ref),
        (list_hbm, list_ref),
        (offset_hbm, offset_ref),
        (ids_hbm, ids_ref),
    )
    copies = [
        pltpu.make_async_copy(source, target, arrived.at[k]) for k, (source, target) in enumerate(pairs)
    ]
    for copy in copies:
        copy.start()

    acc_ref[...] = jnp.zeros_like(acc_ref)

    lane = lax.broadcasted_iota(jnp.int32, (TILE, 3 * TILE), 0)
    target = lax.broadcasted_iota(jnp.int32, (TILE, 3 * TILE), 1) // TILE
    part = lane % LANES
    wanted = (part == target) | (part == target + 3) | (part == target + 6)
    for j in range(BLOCK):
        choose_ref[j] = jnp.where(wanted & (lane // LANES == j), 1.0, 0.0).astype(bf16)
    copies[0].wait()

    @pl.loop(0, fluid_tiles // BLOCK)
    def _(block):
        row = lax.broadcasted_iota(jnp.int32, (8, TILE), 0)
        lines = []
        for j in range(BLOCK):
            tile = block * BLOCK + j
            state = fluid_ref[:, pl.ds(pl.multiple_of(tile * TILE, TILE), TILE)]
            state = jnp.where(row < 3, state * (1.0 / support_radius) - 1.0, state)
            mass = state[7:8]
            first = jnp.where(row < 7, state * mass, state)
            second = jnp.where(row < 3, state * (mass * state[6:7]), 0.0)
            high, low = split_two(jnp.concatenate([first, second], axis=0))
            both = jnp.concatenate([high, low], axis=0)
            terms_ref[tile] = jnp.concatenate([both, both], axis=1)
            lines += [*split_three(state[0:3]), jnp.zeros((LANES - 9, TILE), f32)]
        turned = jnp.concatenate(lines, axis=0).T.astype(bf16)
        for j in range(BLOCK):
            wide_ref[block * BLOCK + j] = jnp.dot(turned, choose_ref[j], preferred_element_type=f32)

    copies[1].wait()
    place_ref[...] = sphere_ref[0:3, :] * (1.0 / support_radius) - 1.0
    copies[2].wait()

    def pair_weights(slot, part):
        a = list_ref[0, slot]
        b = list_ref[1, slot]
        cols = pl.ds(pl.multiple_of(a * TILE, TILE), TILE)
        dx, dy, dz = [
            place_ref[k : k + 1, cols] - wide_ref[b, :, k * TILE : (k + 1) * TILE] for k in range(3)
        ]
        square = jnp.maximum(dx * dx + dy * dy + dz * dz, 1e-30)
        falloff = jnp.maximum(1.0 - square * lax.rsqrt(square), 0.0)
        high, low = split_two(falloff * falloff * falloff)
        weight_ref[part, 0:TILE, :] = high
        weight_ref[part, TILE:, :] = low

    def add_sums(slot, part, live):
        a = list_ref[0, slot]
        b = list_ref[1, slot]
        cols = pl.ds(pl.multiple_of(a * TILE, TILE), TILE)
        sums = jnp.dot(terms_ref[b], weight_ref[part], preferred_element_type=f32)
        acc_ref[:, cols] += live * (sums[0:16] + sums[16:32])

    count = count_ref[0]
    trips = (count + UNROLL - 1) // UNROLL
    last = list_ref.shape[1] - 1

    for part in range(UNROLL):
        pair_weights(min(part, last), part)

    @pl.loop(1, trips)
    def _(trip):
        for part in range(UNROLL):
            add_sums((trip - 1) * UNROLL + part, part, 1.0)
        for part in range(UNROLL):
            pair_weights(jnp.minimum(trip * UNROLL + part, last), part)

    for part in range(UNROLL):
        slot = (trips - 1) * UNROLL + part
        live = jnp.where(slot < count, 1.0, 0.0).astype(f32)
        add_sums(jnp.clip(slot, 0, last), part, live)

    copies[3].wait()
    copies[4].wait()
    group = group_of(owners)
    width = group * SLOT

    @pl.loop(0, owners // group)
    def _(block):
        cols = pl.ds(pl.multiple_of(block * width, width), width)
        acc = acc_ref[:, cols]
        place = place_ref[:, cols]
        sphere = sphere_ref[:, cols]
        offset = offset_ref[:, cols]
        total = acc[7:8]
        pull = total * place - acc[0:3]
        press = acc[6:7] * place - acc[8:11]
        scale = press_coef * support_radius
        force = scale * (sphere[6:7] * pull + press) + visc_coef * (acc[3:6] - total * sphere[3:6])
        force = [force[k : k + 1] for k in range(3)]
        turn = cross([offset[k : k + 1] for k in range(3)], force)
        loads = jnp.concatenate(force + turn + [jnp.zeros_like(force[0])] * 2, axis=0)
        high, low = split_two(loads)
        both = jnp.concatenate([high, low], axis=0)
        column = lax.broadcasted_iota(jnp.int32, (clumps, SLOT), 0)
        for k in range(group):
            here = pl.ds(pl.multiple_of(block * width + k * SLOT, SLOT), SLOT)
            one_hot = jnp.where(column == ids_ref[:, here], 1.0, 0.0).astype(bf16)
            sums = lax.dot_general(
                both[:, k * SLOT : (k + 1) * SLOT], one_hot, (((1,), (1,)), ((), ())),
                preferred_element_type=f32,
            )
            sums = sums[0:8] + sums[8:16]
            put_rows(keep_ref, block * group + k, jnp.where(first_core, sums[0:3], sums[3:6]))
            put_rows(send_ref, block * group + k, jnp.where(first_core, sums[3:6], sums[0:3]))


def update_kernel(arrived_ref, state_ref, inverse_ref, out_ref):
    owners, _, width = out_ref.shape
    clumps = width // 3
    totals = jnp.sum(arrived_ref[...], axis=0)
    first = lax.axis_index("sub") == 0
    for k in range(3):
        cols = slice(k * clumps, (k + 1) * clumps)
        state = jnp.where(first, state_ref[k : k + 1, :], state_ref[k + 3 : k + 4, :])
        factor = jnp.where(first, inverse_ref[0:1, :], inverse_ref[k + 1 : k + 2, :])
        row = state + factor * totals[:, cols]
        if k == 2:
            row = row + jnp.where(first, -gravity_step, 0.0)
        out_ref[:, :, cols] = jnp.broadcast_to(row[None], (owners, 1, clumps))


def velocity_kernel(mine_ref, arrived_ref, offset_ref, ids_ref, clump_ref, sphere_ref):
    owners = mine_ref.shape[0]
    clumps = mine_ref.shape[2] // 3
    group = group_of(owners)
    first_core = lax.axis_index("sub") == 0

    def six_rows(owner):
        mine, arrived = [jnp.concatenate(get_rows(ref, owner), axis=0) for ref in (mine_ref, arrived_ref)]
        return [jnp.where(first_core, mine, arrived), jnp.where(first_core, arrived, mine)]

    me = lax.axis_index("space")

    @pl.loop(0, owners // group)
    def _(block):
        for k in range(group):
            owner = block * group + k
            rows = six_rows(owner) + [jnp.zeros((2, clumps), f32)]
            both = jnp.concatenate(split_two(jnp.concatenate(rows, axis=0)), axis=0)
            here = pl.ds(pl.multiple_of(owner * SLOT, SLOT), SLOT)
            column = lax.broadcasted_iota(jnp.int32, (clumps, SLOT), 0)
            one_hot = jnp.where(column == ids_ref[:, here], 1.0, 0.0).astype(bf16)
            picked = jnp.dot(both, one_hot, preferred_element_type=f32)
            picked = picked[0:8] + picked[8:16]
            offset = offset_ref[:, here]
            turn = cross([picked[3 + i : 4 + i] for i in range(3)], [offset[i : i + 1] for i in range(3)])
            sphere_ref[:, here] = picked[0:3] + jnp.concatenate(turn, axis=0)

    clump_ref[...] = jnp.concatenate(six_rows(me), axis=0)


def per_device(
    fluid_state, sphere_state, sphere_offset, tile_list, tile_count, clump_ids, clump_state, clump_inverse
):
    owners = lax.axis_size("space")
    spheres = sphere_state.shape[1]
    fluid = fluid_state.shape[1]
    clumps = clump_state.shape[1]
    slots = tile_list.shape[0]
    ids = clump_ids.reshape(1, spheres)
    vmem = pl.BlockSpec(memory_space=pltpu.VMEM)
    hbm = pl.BlockSpec(memory_space=pltpu.HBM)
    params = pltpu.CompilerParams(vmem_limit_bytes=48 * 1024 * 1024)

    keep, send = pl.pallas_call(
        loads_kernel,
        out_shape=(pltpu.VMEM((owners, 1, 3 * clumps), f32),) * 2,
        in_specs=[pl.BlockSpec(memory_space=pltpu.SMEM)] + [hbm] * 5,
        out_specs=(vmem, vmem),
        scratch_shapes=[
            pltpu.SMEM((2, slots), jnp.int32),
            pltpu.VMEM((8, fluid), f32),
            pltpu.VMEM((7, spheres), f32),
            pltpu.VMEM((3, spheres), f32),
            pltpu.VMEM((1, spheres), jnp.int32),
            pltpu.SemaphoreType.DMA((5,)),
            pltpu.VMEM((3, spheres), f32),
            pltpu.VMEM((BLOCK, TILE, 3 * TILE), bf16),
            pltpu.VMEM((fluid // TILE, TILE, 3 * TILE), f32),
            pltpu.VMEM((fluid // TILE, 32, 2 * TILE), bf16),
            pltpu.VMEM((UNROLL, 2 * TILE, TILE), bf16),
            pltpu.VMEM((16, spheres), f32),
        ],
        compiler_params=params,
        name="clump_loads",
    )(tile_count, *(
        pltpu.with_memory_space_constraint(value, pltpu.HBM)
        for value in (tile_list.T, fluid_state, sphere_state, sphere_offset, ids)
    ))

    partial = keep + swap_cores(send)
    arrived = lax.all_to_all(partial, "space", split_axis=0, concat_axis=0, tiled=True)
    rows = pl.pallas_call(
        update_kernel,
        out_shape=jax.ShapeDtypeStruct((owners, 1, 3 * clumps), f32),
        in_specs=[vmem] * 3,
        out_specs=vmem,
        compiler_params=params,
        name="clump_update",
    )(arrived, clump_state, clump_inverse)
    velocities = lax.all_to_all(rows, "space", split_axis=0, concat_axis=0, tiled=True)

    return pl.pallas_call(
        velocity_kernel,
        out_shape=(
            jax.ShapeDtypeStruct((6, clumps), f32),
            jax.ShapeDtypeStruct((3, spheres), f32),
        ),
        in_specs=[vmem] * 4,
        out_specs=(vmem, vmem),
        compiler_params=params,
        name="sphere_velocities",
    )(velocities, swap_cores(velocities), sphere_offset, ids)


def solution(mesh):
    in_specs = (
        P(None, "space"),
        P(None, "space"),
        P(None, "space"),
        P(("space", "sub"), None),
        P(("space", "sub")),
        P("space"),
        P(None, "space"),
        P(None, "space"),
    )
    out_specs = (P(None, "space"), P(None, "space"))
    return jax.shard_map(
        per_device, mesh=mesh, in_specs=in_specs, out_specs=out_specs, check_vma=False
    )
```

```python
import functools
import math

import jax
import jax.numpy as jnp
from jax import lax
from jax.experimental import pallas as pl
from jax.experimental.pallas import tpu as pltpu
from jax.sharding import PartitionSpec as P

TILE = 128
SLOT = 256
UNROLL = 8
LANES = 16
BLOCK = TILE // LANES

support_radius = 0.5
press_coef = 4.0
visc_coef = 1.0
gravity_step = 0.1

f32 = jnp.float32
bf16 = jnp.bfloat16


def split_two(value):
    high = value.astype(bf16)
    return high, (value - high.astype(f32)).astype(bf16)


def split_three(value):
    high = value.astype(bf16).astype(f32)
    middle = (value - high).astype(bf16).astype(f32)
    return high, middle, (value - high) - middle


def cross(left, right):
    return [
        left[1] * right[2] - left[2] * right[1],
        left[2] * right[0] - left[0] * right[2],
        left[0] * right[1] - left[1] * right[0],
    ]


def group_of(owners):
    return math.gcd(owners, 16)


def loads_kernel(
    count_ref, list_hbm, fluid_hbm, sphere_hbm, offset_hbm, ids_hbm, state_hbm, inverse_hbm,
    keep_ref, send_ref,
    list_ref, fluid_ref, sphere_ref, offset_ref, ids_ref, state_ref, inverse_ref, arrived,
    place_ref, choose_ref, wide_ref, terms_ref, weight_ref, acc_ref,
):
    fluid_tiles = fluid_ref.shape[1] // TILE
    clumps = keep_ref.shape[1]
    owners = keep_ref.shape[0] // 3
    core = lax.axis_index("sub")
    me = jnp.where(core == 0, lax.axis_index("space"), -1)

    pairs = (
        (fluid_hbm, fluid_ref),
        (sphere_hbm, sphere_ref),
        (list_hbm, list_ref),
        (offset_hbm, offset_ref),
        (ids_hbm, ids_ref),
        (state_hbm, state_ref),
        (inverse_hbm, inverse_ref),
    )
    copies = [
        pltpu.make_async_copy(source, target, arrived.at[k]) for k, (source, target) in enumerate(pairs)
    ]
    for copy in copies:
        copy.start()

    acc_ref[...] = jnp.zeros_like(acc_ref)

    lane = lax.broadcasted_iota(jnp.int32, (TILE, 3 * TILE), 0)
    target = lax.broadcasted_iota(jnp.int32, (TILE, 3 * TILE), 1) // TILE
    part = lane % LANES
    wanted = (part == target) | (part == target + 3) | (part == target + 6)
    for j in range(BLOCK):
        choose_ref[j] = jnp.where(wanted & (lane // LANES == j), 1.0, 0.0).astype(bf16)
    copies[0].wait()

    @pl.loop(0, fluid_tiles // BLOCK)
    def _(block):
        row = lax.broadcasted_iota(jnp.int32, (8, TILE), 0)
        lines = []
        for j in range(BLOCK):
            tile = block * BLOCK + j
            state = fluid_ref[:, pl.ds(pl.multiple_of(tile * TILE, TILE), TILE)]
            state = jnp.where(row < 3, state * (1.0 / support_radius) - 1.0, state)
            mass = state[7:8]
            first = jnp.where(row < 7, state * mass, state)
            second = jnp.where(row < 3, state * (mass * state[6:7]), 0.0)
            high, low = split_two(jnp.concatenate([first, second], axis=0))
            both = jnp.concatenate([high, low], axis=0)
            terms_ref[tile] = jnp.concatenate([both, both], axis=1)
            lines += [*split_three(state[0:3]), jnp.zeros((LANES - 9, TILE), f32)]
        turned = jnp.concatenate(lines, axis=0).T.astype(bf16)
        for j in range(BLOCK):
            wide_ref[block * BLOCK + j] = jnp.dot(turned, choose_ref[j], preferred_element_type=f32)

    copies[1].wait()
    place_ref[...] = sphere_ref[0:3, :] * (1.0 / support_radius) - 1.0
    copies[2].wait()

    def pair_weights(slot, part):
        a = list_ref[0, slot]
        b = list_ref[1, slot]
        cols = pl.ds(pl.multiple_of(a * TILE, TILE), TILE)
        dx, dy, dz = [
            place_ref[k : k + 1, cols] - wide_ref[b, :, k * TILE : (k + 1) * TILE] for k in range(3)
        ]
        square = jnp.maximum(dx * dx + dy * dy + dz * dz, 1e-30)
        falloff = jnp.maximum(1.0 - square * lax.rsqrt(square), 0.0)
        high, low = split_two(falloff * falloff * falloff)
        weight_ref[part, 0:TILE, :] = high
        weight_ref[part, TILE:, :] = low

    def add_sums(slot, part, live):
        a = list_ref[0, slot]
        b = list_ref[1, slot]
        cols = pl.ds(pl.multiple_of(a * TILE, TILE), TILE)
        sums = jnp.dot(terms_ref[b], weight_ref[part], preferred_element_type=f32)
        acc_ref[:, cols] += live * (sums[0:16] + sums[16:32])

    count = count_ref[0]
    trips = (count + UNROLL - 1) // UNROLL
    last = list_ref.shape[1] - 1

    for part in range(UNROLL):
        pair_weights(min(part, last), part)

    @pl.loop(1, trips)
    def _(trip):
        for part in range(UNROLL):
            add_sums((trip - 1) * UNROLL + part, part, 1.0)
        for part in range(UNROLL):
            pair_weights(jnp.minimum(trip * UNROLL + part, last), part)

    for part in range(UNROLL):
        slot = (trips - 1) * UNROLL + part
        live = jnp.where(slot < count, 1.0, 0.0).astype(f32)
        add_sums(jnp.clip(slot, 0, last), part, live)

    for copy in copies[3:]:
        copy.wait()
    group = group_of(owners)
    width = group * SLOT

    row = lax.broadcasted_iota(jnp.int32, state_ref.shape, 0)
    still = state_ref[...] + jnp.where(row == 2, -gravity_step, 0.0)
    still = still / jnp.concatenate([inverse_ref[0:1, :]] * 3 + [inverse_ref[1:4, :]], axis=0)

    @pl.loop(0, owners // group)
    def _(block):
        cols = pl.ds(pl.multiple_of(block * width, width), width)
        acc = acc_ref[:, cols]
        place = place_ref[:, cols]
        sphere = sphere_ref[:, cols]
        offset = offset_ref[:, cols]
        total = acc[7:8]
        pull = total * place - acc[0:3]
        press = acc[6:7] * place - acc[8:11]
        scale = press_coef * support_radius
        force = scale * (sphere[6:7] * pull + press) + visc_coef * (acc[3:6] - total * sphere[3:6])
        force = [force[k : k + 1] for k in range(3)]
        turn = cross([offset[k : k + 1] for k in range(3)], force)
        loads = jnp.concatenate(force + turn + [jnp.zeros_like(force[0])] * 2, axis=0)
        high, low = split_two(loads)
        both = jnp.concatenate([high, low], axis=0)
        column = lax.broadcasted_iota(jnp.int32, (clumps, SLOT), 0)
        keep, send = [], []
        for k in range(group):
            here = pl.ds(pl.multiple_of(block * width + k * SLOT, SLOT), SLOT)
            one_hot = jnp.where(column == ids_ref[:, here], 1.0, 0.0).astype(bf16)
            sums = lax.dot_general(
                both[:, k * SLOT : (k + 1) * SLOT], one_hot, (((1,), (1,)), ((), ())),
                preferred_element_type=f32,
            )
            own = jnp.where(block * group + k == me, 1.0, 0.0).astype(f32)
            sums = (sums[0:8] + sums[8:16])[0:6] + own * still
            keep.append(jnp.where(core == 0, sums[0:3], sums[3:6]))
            send.append(jnp.where(core == 0, sums[3:6], sums[0:3]))
        here = pl.ds(pl.multiple_of(block * (3 * group), math.gcd(3 * group, 8)), 3 * group)
        keep_ref[here, :] = jnp.concatenate(keep, axis=0)
        send_ref[here, :] = jnp.concatenate(send, axis=0)


def first_kernel(keep_ref, arrived_ref, inverse_ref, out_ref):
    rows = keep_ref.shape[0]
    out_ref[0:rows, :] = keep_ref[...] + arrived_ref[...]
    linear = jnp.concatenate([inverse_ref[0:1, :]] * 3, axis=0)
    out_ref[rows:, :] = jnp.where(lax.axis_index("sub") == 0, linear, inverse_ref[1:4, :])


def sum_rows(refs, rows):
    sums = [ref[0:rows, :] for ref in refs]
    while len(sums) > 1:
        sums = [left + right for left, right in zip(sums[0::2], sums[1::2])]
    return sums[0]


def join_kernel(rows, *refs):
    *parts, out_ref = refs
    more = parts[0].shape[0] - rows
    out_ref[0:rows, :] = sum_rows(parts, rows)
    for k, ref in enumerate(parts):
        out_ref[rows + k * more : rows + (k + 1) * more, :] = ref[rows:, :]


def update_kernel(partners, *refs):
    *parts, out_ref, inverse_ref = refs
    owners = len(partners)
    rows = 3 * owners
    held = owners // len(parts)
    me = lax.axis_index("space")
    for k, partner in enumerate(partners):
        first = rows + 3 * (k % held)
        inverse_ref[me ^ partner] = parts[k // held][first : first + 3, :]
    out_ref[...] = sum_rows(parts, rows) * jnp.concatenate([inverse_ref[k] for k in range(owners)], axis=0)


def velocity_kernel(mine_ref, arrived_ref, offset_ref, ids_ref, clump_ref, sphere_ref, velocity_ref):
    owners, _, clumps = velocity_ref.shape
    group = group_of(owners)
    core = lax.axis_index("sub")

    @pl.loop(0, owners // group)
    def _(block):
        rows = pl.ds(pl.multiple_of(block * (3 * group), math.gcd(3 * group, 8)), 3 * group)
        mine = mine_ref[rows, :]
        arrived = arrived_ref[rows, :]
        linear = jnp.where(core == 0, mine, arrived)
        angular = jnp.where(core == 0, arrived, mine)
        for k in range(group):
            owner = block * group + k
            three = slice(3 * k, 3 * k + 3)
            velocity = jnp.concatenate([linear[three], angular[three]], axis=0)
            velocity_ref[owner] = velocity
            both = jnp.concatenate(
                split_two(jnp.concatenate([velocity, jnp.zeros((2, clumps), f32)], axis=0)), axis=0
            )
            here = pl.ds(pl.multiple_of(owner * SLOT, SLOT), SLOT)
            column = lax.broadcasted_iota(jnp.int32, (clumps, SLOT), 0)
            one_hot = jnp.where(column == ids_ref[:, here], 1.0, 0.0).astype(bf16)
            picked = jnp.dot(both, one_hot, preferred_element_type=f32)
            picked = picked[0:8] + picked[8:16]
            offset = offset_ref[:, here]
            turn = cross([picked[3 + i : 4 + i] for i in range(3)], [offset[i : i + 1] for i in range(3)])
            sphere_ref[:, here] = picked[0:3] + jnp.concatenate(turn, axis=0)

    clump_ref[...] = velocity_ref[lax.axis_index("space")]


def swap(value, axis, bit):
    size = lax.axis_size(axis)
    return lax.ppermute(value, axis, [(k, k ^ bit) for k in range(size)])


def per_device(
    fluid_state, sphere_state, sphere_offset, tile_list, tile_count, clump_ids, clump_state, clump_inverse
):
    owners = lax.axis_size("space")
    spheres = sphere_state.shape[1]
    fluid = fluid_state.shape[1]
    clumps = clump_state.shape[1]
    slots = tile_list.shape[0]
    rows = 3 * owners
    ids = clump_ids.reshape(1, spheres)
    vmem = pl.BlockSpec(memory_space=pltpu.VMEM)
    hbm = pl.BlockSpec(memory_space=pltpu.HBM)
    params = pltpu.CompilerParams(vmem_limit_bytes=48 * 1024 * 1024)

    keep, send = pl.pallas_call(
        loads_kernel,
        out_shape=(pltpu.VMEM((rows, clumps), f32), pltpu.VMEM((rows, clumps), f32)),
        in_specs=[pl.BlockSpec(memory_space=pltpu.SMEM)] + [hbm] * 7,
        out_specs=(vmem, vmem),
        scratch_shapes=[
            pltpu.SMEM((2, slots), jnp.int32),
            pltpu.VMEM((8, fluid), f32),
            pltpu.VMEM((7, spheres), f32),
            pltpu.VMEM((3, spheres), f32),
            pltpu.VMEM((1, spheres), jnp.int32),
            pltpu.VMEM((6, clumps), f32),
            pltpu.VMEM((4, clumps), f32),
            pltpu.SemaphoreType.DMA((7,)),
            pltpu.VMEM((3, spheres), f32),
            pltpu.VMEM((BLOCK, TILE, 3 * TILE), bf16),
            pltpu.VMEM((fluid // TILE, TILE, 3 * TILE), f32),
            pltpu.VMEM((fluid // TILE, 32, 2 * TILE), bf16),
            pltpu.VMEM((UNROLL, 2 * TILE, TILE), bf16),
            pltpu.VMEM((16, spheres), f32),
        ],
        compiler_params=params,
        name="clump_loads",
    )(tile_count, *(
        pltpu.with_memory_space_constraint(value, pltpu.HBM)
        for value in (
            tile_list.T, fluid_state, sphere_state, sphere_offset, ids, clump_state, clump_inverse
        )
    ))

    def small(kernel, height, name, *operands, scratch=()):
        return pl.pallas_call(
            kernel,
            out_shape=pltpu.VMEM((height, clumps), f32),
            in_specs=[vmem] * len(operands),
            out_specs=vmem,
            scratch_shapes=scratch,
            compiler_params=params,
            name=name,
        )(*operands)

    mine = small(first_kernel, rows + 3, "core_sum", keep, swap(send, "sub", 1), clump_inverse)
    bits = []
    left = owners
    while left > 1:
        step = [left // 2, left // 4] if left > 2 else [1]
        left //= 2 ** len(step)
        bits += step
        others = step if len(step) == 1 else [*step, sum(step)]
        parts = [mine] + [swap(mine, "space", bit) for bit in others]
        if left > 1:
            height = rows + len(parts) * (mine.shape[0] - rows)
            mine = small(functools.partial(join_kernel, rows), height, "space_sum", *parts)
    partners = [sum(bit for n, bit in enumerate(bits) if k >> n & 1) for k in range(owners)]
    velocities = small(
        functools.partial(update_kernel, partners), rows, "clump_update", *parts,
        scratch=[pltpu.VMEM((owners, 3, clumps), f32)],
    )

    return pl.pallas_call(
        velocity_kernel,
        out_shape=(
            jax.ShapeDtypeStruct((6, clumps), f32),
            jax.ShapeDtypeStruct((3, spheres), f32),
        ),
        in_specs=[vmem] * 4,
        out_specs=(vmem, vmem),
        scratch_shapes=[pltpu.VMEM((owners, 6, clumps), f32)],
        compiler_params=params,
        name="sphere_velocities",
    )(velocities, swap(velocities, "sub", 1), sphere_offset, ids)


def solution(mesh):
    in_specs = (
        P(None, "space"),
        P(None, "space"),
        P(None, "space"),
        P(("space", "sub"), None),
        P(("space", "sub")),
        P("space"),
        P(None, "space"),
        P(None, "space"),
    )
    out_specs = (P(None, "space"), P(None, "space"))
    return jax.shard_map(
        per_device, mesh=mesh, in_specs=in_specs, out_specs=out_specs, check_vma=False
    )
```

```python
import functools
import math

import jax
import jax.numpy as jnp
from jax import lax
from jax.experimental import pallas as pl
from jax.experimental.pallas import tpu as pltpu
from jax.sharding import PartitionSpec as P

TILE = 128
SLOT = 256
UNROLL = 8
LANES = 16
BLOCK = TILE // LANES

support_radius = 0.5
press_coef = 4.0
visc_coef = 1.0
gravity_step = 0.1

f32 = jnp.float32
bf16 = jnp.bfloat16


def split_two(value):
    high = value.astype(bf16)
    return high, (value - high.astype(f32)).astype(bf16)


def split_three(value):
    high = value.astype(bf16).astype(f32)
    middle = (value - high).astype(bf16).astype(f32)
    return high, middle, (value - high) - middle


def cross(left, right):
    return [
        left[1] * right[2] - left[2] * right[1],
        left[2] * right[0] - left[0] * right[2],
        left[0] * right[1] - left[1] * right[0],
    ]


def group_of(owners):
    return math.gcd(owners, 16)


def loads_kernel(
    count_ref, list_hbm, fluid_hbm, sphere_hbm, offset_hbm, ids_hbm, state_hbm, inverse_hbm,
    out_ref,
    list_ref, fluid_ref, sphere_ref, offset_ref, ids_ref, state_ref, inverse_ref, arrived,
    place_ref, choose_ref, wide_ref, terms_ref, weight_ref, acc_ref,
):
    fluid_tiles = fluid_ref.shape[1] // TILE
    clumps = out_ref.shape[1]
    owners = out_ref.shape[0] // 6
    me = jnp.where(lax.axis_index("sub") == 0, lax.axis_index("space"), -1)

    pairs = (
        (fluid_hbm, fluid_ref),
        (sphere_hbm, sphere_ref),
        (list_hbm, list_ref),
        (offset_hbm, offset_ref),
        (ids_hbm, ids_ref),
        (state_hbm, state_ref),
        (inverse_hbm, inverse_ref),
    )
    copies = [
        pltpu.make_async_copy(source, target, arrived.at[k]) for k, (source, target) in enumerate(pairs)
    ]
    for copy in copies:
        copy.start()

    acc_ref[...] = jnp.zeros_like(acc_ref)

    lane = lax.broadcasted_iota(jnp.int32, (TILE, 3 * TILE), 0)
    target = lax.broadcasted_iota(jnp.int32, (TILE, 3 * TILE), 1) // TILE
    part = lane % LANES
    wanted = (part == target) | (part == target + 3) | (part == target + 6)
    for j in range(BLOCK):
        choose_ref[j] = jnp.where(wanted & (lane // LANES == j), 1.0, 0.0).astype(bf16)
    copies[0].wait()

    @pl.loop(0, fluid_tiles // BLOCK)
    def _(block):
        row = lax.broadcasted_iota(jnp.int32, (8, TILE), 0)
        lines = []
        for j in range(BLOCK):
            tile = block * BLOCK + j
            state = fluid_ref[:, pl.ds(pl.multiple_of(tile * TILE, TILE), TILE)]
            state = jnp.where(row < 3, state * (1.0 / support_radius) - 1.0, state)
            mass = state[7:8]
            first = jnp.where(row < 7, state * mass, state)
            second = jnp.where(row < 3, state * (mass * state[6:7]), 0.0)
            high, low = split_two(jnp.concatenate([first, second], axis=0))
            both = jnp.concatenate([high, low], axis=0)
            terms_ref[tile] = jnp.concatenate([both, both], axis=1)
            lines += [*split_three(state[0:3]), jnp.zeros((LANES - 9, TILE), f32)]
        turned = jnp.concatenate(lines, axis=0).T.astype(bf16)
        for j in range(BLOCK):
            wide_ref[block * BLOCK + j] = jnp.dot(turned, choose_ref[j], preferred_element_type=f32)

    copies[1].wait()
    place_ref[...] = sphere_ref[0:3, :] * (1.0 / support_radius) - 1.0
    copies[2].wait()

    def pair_weights(slot, part):
        a = list_ref[0, slot]
        b = list_ref[1, slot]
        cols = pl.ds(pl.multiple_of(a * TILE, TILE), TILE)
        dx, dy, dz = [
            place_ref[k : k + 1, cols] - wide_ref[b, :, k * TILE : (k + 1) * TILE] for k in range(3)
        ]
        square = jnp.maximum(dx * dx + dy * dy + dz * dz, 1e-30)
        falloff = jnp.maximum(1.0 - square * lax.rsqrt(square), 0.0)
        high, low = split_two(falloff * falloff * falloff)
        weight_ref[part, 0:TILE, :] = high
        weight_ref[part, TILE:, :] = low

    def add_sums(slot, part, live):
        a = list_ref[0, slot]
        b = list_ref[1, slot]
        cols = pl.ds(pl.multiple_of(a * TILE, TILE), TILE)
        sums = jnp.dot(terms_ref[b], weight_ref[part], preferred_element_type=f32)
        acc_ref[:, cols] += live * (sums[0:16] + sums[16:32])

    count = count_ref[0]
    trips = (count + UNROLL - 1) // UNROLL
    last = list_ref.shape[1] - 1

    for part in range(UNROLL):
        pair_weights(min(part, last), part)

    @pl.loop(1, trips)
    def _(trip):
        for part in range(UNROLL):
            add_sums((trip - 1) * UNROLL + part, part, 1.0)
        for part in range(UNROLL):
            pair_weights(jnp.minimum(trip * UNROLL + part, last), part)

    for part in range(UNROLL):
        slot = (trips - 1) * UNROLL + part
        live = jnp.where(slot < count, 1.0, 0.0).astype(f32)
        add_sums(jnp.clip(slot, 0, last), part, live)

    for copy in copies[3:]:
        copy.wait()
    group = group_of(owners)
    width = group * SLOT

    row = lax.broadcasted_iota(jnp.int32, state_ref.shape, 0)
    still = state_ref[...] + jnp.where(row == 2, -gravity_step, 0.0)
    still = still / jnp.concatenate([inverse_ref[0:1, :]] * 3 + [inverse_ref[1:4, :]], axis=0)

    @pl.loop(0, owners // group)
    def _(block):
        cols = pl.ds(pl.multiple_of(block * width, width), width)
        acc = acc_ref[:, cols]
        place = place_ref[:, cols]
        sphere = sphere_ref[:, cols]
        offset = offset_ref[:, cols]
        total = acc[7:8]
        pull = total * place - acc[0:3]
        press = acc[6:7] * place - acc[8:11]
        scale = press_coef * support_radius
        force = scale * (sphere[6:7] * pull + press) + visc_coef * (acc[3:6] - total * sphere[3:6])
        force = [force[k : k + 1] for k in range(3)]
        turn = cross([offset[k : k + 1] for k in range(3)], force)
        loads = jnp.concatenate(force + turn + [jnp.zeros_like(force[0])] * 2, axis=0)
        high, low = split_two(loads)
        both = jnp.concatenate([high, low], axis=0)
        column = lax.broadcasted_iota(jnp.int32, (clumps, SLOT), 0)
        results = []
        for k in range(group):
            here = pl.ds(pl.multiple_of(block * width + k * SLOT, SLOT), SLOT)
            one_hot = jnp.where(column == ids_ref[:, here], 1.0, 0.0).astype(bf16)
            sums = lax.dot_general(
                both[:, k * SLOT : (k + 1) * SLOT], one_hot, (((1,), (1,)), ((), ())),
                preferred_element_type=f32,
            )
            own = jnp.where(block * group + k == me, 1.0, 0.0).astype(f32)
            results.append((sums[0:8] + sums[8:16])[0:6] + own * still)
        here = pl.ds(pl.multiple_of(block * (6 * group), math.gcd(6 * group, 8)), 6 * group)
        out_ref[here, :] = jnp.concatenate(results, axis=0)


def first_kernel(mine_ref, arrived_ref, inverse_ref, out_ref):
    rows = mine_ref.shape[0]
    out_ref[0:rows, :] = mine_ref[...] + arrived_ref[...]
    out_ref[rows:, :] = inverse_ref[...]


def sum_rows(refs, rows):
    sums = [ref[0:rows, :] for ref in refs]
    while len(sums) > 1:
        sums = [left + right for left, right in zip(sums[0::2], sums[1::2])]
    return sums[0]


def join_kernel(rows, *refs):
    *parts, out_ref = refs
    more = parts[0].shape[0] - rows
    out_ref[0:rows, :] = sum_rows(parts, rows)
    for k, ref in enumerate(parts):
        out_ref[rows + k * more : rows + (k + 1) * more, :] = ref[rows:, :]


def update_kernel(partners, *refs):
    *parts, out_ref, inverse_ref = refs
    owners = len(partners)
    rows = 6 * owners
    held = owners // len(parts)
    me = lax.axis_index("space")
    for k, partner in enumerate(partners):
        first = rows + 4 * (k % held)
        inverse = parts[k // held][first : first + 4, :]
        inverse_ref[me ^ partner] = jnp.concatenate([inverse[0:1]] * 3 + [inverse[1:4]], axis=0)
    out_ref[...] = sum_rows(parts, rows) * jnp.concatenate([inverse_ref[k] for k in range(owners)], axis=0)


def velocity_kernel(mine_ref, arrived_ref, offset_ref, ids_ref, clump_ref, sphere_ref, velocity_ref):
    owners, _, clumps = velocity_ref.shape
    group = group_of(owners)
    core = lax.axis_index("sub")

    @pl.loop(0, owners // group)
    def _(block):
        rows = pl.ds(pl.multiple_of(block * (6 * group), math.gcd(6 * group, 8)), 6 * group)
        velocities = jnp.where(core == 1, mine_ref[rows, :], arrived_ref[rows, :])
        for k in range(group):
            owner = block * group + k
            velocity = velocities[6 * k : 6 * k + 6]
            velocity_ref[owner] = velocity
            both = jnp.concatenate(
                split_two(jnp.concatenate([velocity, jnp.zeros((2, clumps), f32)], axis=0)), axis=0
            )
            here = pl.ds(pl.multiple_of(owner * SLOT, SLOT), SLOT)
            column = lax.broadcasted_iota(jnp.int32, (clumps, SLOT), 0)
            one_hot = jnp.where(column == ids_ref[:, here], 1.0, 0.0).astype(bf16)
            picked = jnp.dot(both, one_hot, preferred_element_type=f32)
            picked = picked[0:8] + picked[8:16]
            offset = offset_ref[:, here]
            turn = cross([picked[3 + i : 4 + i] for i in range(3)], [offset[i : i + 1] for i in range(3)])
            sphere_ref[:, here] = picked[0:3] + jnp.concatenate(turn, axis=0)

    clump_ref[...] = velocity_ref[lax.axis_index("space")]


def swap(value, bit):
    pairs = [(2 * k + 1, 2 * (k ^ bit) + 1) for k in range(lax.axis_size("space"))]
    return lax.ppermute(value, ("space", "sub"), pairs)


def per_device(
    fluid_state, sphere_state, sphere_offset, tile_list, tile_count, clump_ids, clump_state, clump_inverse
):
    owners = lax.axis_size("space")
    spheres = sphere_state.shape[1]
    fluid = fluid_state.shape[1]
    clumps = clump_state.shape[1]
    slots = tile_list.shape[0]
    rows = 6 * owners
    ids = clump_ids.reshape(1, spheres)
    vmem = pl.BlockSpec(memory_space=pltpu.VMEM)
    hbm = pl.BlockSpec(memory_space=pltpu.HBM)
    params = pltpu.CompilerParams(vmem_limit_bytes=48 * 1024 * 1024)

    partial = pl.pallas_call(
        loads_kernel,
        out_shape=pltpu.VMEM((rows, clumps), f32),
        in_specs=[pl.BlockSpec(memory_space=pltpu.SMEM)] + [hbm] * 7,
        out_specs=vmem,
        scratch_shapes=[
            pltpu.SMEM((2, slots), jnp.int32),
            pltpu.VMEM((8, fluid), f32),
            pltpu.VMEM((7, spheres), f32),
            pltpu.VMEM((3, spheres), f32),
            pltpu.VMEM((1, spheres), jnp.int32),
            pltpu.VMEM((6, clumps), f32),
            pltpu.VMEM((4, clumps), f32),
            pltpu.SemaphoreType.DMA((7,)),
            pltpu.VMEM((3, spheres), f32),
            pltpu.VMEM((BLOCK, TILE, 3 * TILE), bf16),
            pltpu.VMEM((fluid // TILE, TILE, 3 * TILE), f32),
            pltpu.VMEM((fluid // TILE, 32, 2 * TILE), bf16),
            pltpu.VMEM((UNROLL, 2 * TILE, TILE), bf16),
            pltpu.VMEM((16, spheres), f32),
        ],
        compiler_params=params,
        name="clump_loads",
    )(tile_count, *(
        pltpu.with_memory_space_constraint(value, pltpu.HBM)
        for value in (
            tile_list.T, fluid_state, sphere_state, sphere_offset, ids, clump_state, clump_inverse
        )
    ))

    def small(kernel, height, name, *operands, scratch=()):
        return pl.pallas_call(
            kernel,
            out_shape=pltpu.VMEM((height, clumps), f32),
            in_specs=[vmem] * len(operands),
            out_specs=vmem,
            scratch_shapes=scratch,
            compiler_params=params,
            name=name,
        )(*operands)

    arrived = lax.ppermute(partial, "sub", [(0, 1)])
    mine = small(first_kernel, rows + 4, "core_sum", partial, arrived, clump_inverse)
    bits = []
    left = owners
    while left > 1:
        step = [left // 2, left // 4] if left > 2 else [1]
        left //= 2 ** len(step)
        bits += step
        others = step if len(step) == 1 else [*step, sum(step)]
        parts = [mine] + [swap(mine, bit) for bit in others]
        if left > 1:
            height = rows + len(parts) * (mine.shape[0] - rows)
            mine = small(functools.partial(join_kernel, rows), height, "space_sum", *parts)
    partners = [sum(bit for n, bit in enumerate(bits) if k >> n & 1) for k in range(owners)]
    velocities = small(
        functools.partial(update_kernel, partners), rows, "clump_update", *parts,
        scratch=[pltpu.VMEM((owners, 6, clumps), f32)],
    )

    return pl.pallas_call(
        velocity_kernel,
        out_shape=(
            jax.ShapeDtypeStruct((6, clumps), f32),
            jax.ShapeDtypeStruct((3, spheres), f32),
        ),
        in_specs=[vmem] * 4,
        out_specs=(vmem, vmem),
        scratch_shapes=[pltpu.VMEM((owners, 6, clumps), f32)],
        compiler_params=params,
        name="sphere_velocities",
    )(velocities, lax.ppermute(velocities, "sub", [(1, 0)]), sphere_offset, ids)


def solution(mesh):
    in_specs = (
        P(None, "space"),
        P(None, "space"),
        P(None, "space"),
        P(("space", "sub"), None),
        P(("space", "sub")),
        P("space"),
        P(None, "space"),
        P(None, "space"),
    )
    out_specs = (P(None, "space"), P(None, "space"))
    return jax.shard_map(
        per_device, mesh=mesh, in_specs=in_specs, out_specs=out_specs, check_vma=False
    )
```

```python
import functools
import math

import jax
import jax.numpy as jnp
from jax import lax
from jax.experimental import pallas as pl
from jax.experimental.pallas import tpu as pltpu
from jax.sharding import PartitionSpec as P

TILE = 128
SLOT = 256
UNROLL = 8
LANES = 16
BLOCK = TILE // LANES

support_radius = 0.5
press_coef = 4.0
visc_coef = 1.0
gravity_step = 0.1

f32 = jnp.float32
bf16 = jnp.bfloat16


def split_two(value):
    high = value.astype(bf16)
    return high, (value - high.astype(f32)).astype(bf16)


def split_three(value):
    high = value.astype(bf16).astype(f32)
    middle = (value - high).astype(bf16).astype(f32)
    return high, middle, (value - high) - middle


def cross(left, right):
    return [
        left[1] * right[2] - left[2] * right[1],
        left[2] * right[0] - left[0] * right[2],
        left[0] * right[1] - left[1] * right[0],
    ]


def group_of(owners):
    return math.gcd(owners, 16)


def loads_kernel(
    count_ref, list_hbm, fluid_hbm, sphere_hbm, offset_hbm, ids_hbm, state_hbm, inverse_hbm,
    out_ref,
    list_ref, fluid_ref, sphere_ref, offset_ref, ids_ref, state_ref, inverse_ref, arrived,
    place_ref, choose_ref, wide_ref, terms_ref, weight_ref, acc_ref,
):
    fluid_tiles = fluid_ref.shape[1] // TILE
    clumps = out_ref.shape[1]
    owners = out_ref.shape[0] // 6
    me = jnp.where(lax.axis_index("sub") == 0, lax.axis_index("space"), -1)

    pairs = (
        (fluid_hbm, fluid_ref),
        (sphere_hbm, sphere_ref),
        (list_hbm, list_ref),
        (offset_hbm, offset_ref),
        (ids_hbm, ids_ref),
        (state_hbm, state_ref),
        (inverse_hbm, inverse_ref),
    )
    copies = [
        pltpu.make_async_copy(source, target, arrived.at[k]) for k, (source, target) in enumerate(pairs)
    ]
    for copy in copies:
        copy.start()

    acc_ref[...] = jnp.zeros_like(acc_ref)

    lane = lax.broadcasted_iota(jnp.int32, (TILE, 3 * TILE), 0)
    target = lax.broadcasted_iota(jnp.int32, (TILE, 3 * TILE), 1) // TILE
    part = lane % LANES
    wanted = (part == target) | (part == target + 3) | (part == target + 6)
    for j in range(BLOCK):
        choose_ref[j] = jnp.where(wanted & (lane // LANES == j), 1.0, 0.0).astype(bf16)
    copies[0].wait()

    @pl.loop(0, fluid_tiles // BLOCK)
    def _(block):
        row = lax.broadcasted_iota(jnp.int32, (8, TILE), 0)
        lines = []
        for j in range(BLOCK):
            tile = block * BLOCK + j
            state = fluid_ref[:, pl.ds(pl.multiple_of(tile * TILE, TILE), TILE)]
            state = jnp.where(row < 3, state * (1.0 / support_radius) - 1.0, state)
            mass = state[7:8]
            first = jnp.where(row < 7, state * mass, state)
            second = jnp.where(row < 3, state * (mass * state[6:7]), 0.0)
            high, low = split_two(jnp.concatenate([first, second], axis=0))
            both = jnp.concatenate([high, low], axis=0)
            terms_ref[tile] = jnp.concatenate([both, both], axis=1)
            lines += [*split_three(state[0:3]), jnp.zeros((LANES - 9, TILE), f32)]
        turned = jnp.concatenate(lines, axis=0).T.astype(bf16)
        for j in range(BLOCK):
            wide_ref[block * BLOCK + j] = jnp.dot(turned, choose_ref[j], preferred_element_type=f32)

    copies[1].wait()
    place_ref[...] = sphere_ref[0:3, :] * (1.0 / support_radius) - 1.0
    copies[2].wait()

    def pair_weights(slot, part):
        a = list_ref[0, slot]
        b = list_ref[1, slot]
        cols = pl.ds(pl.multiple_of(a * TILE, TILE), TILE)
        dx, dy, dz = [
            place_ref[k : k + 1, cols] - wide_ref[b, :, k * TILE : (k + 1) * TILE] for k in range(3)
        ]
        square = jnp.maximum(dx * dx + dy * dy + dz * dz, 1e-30)
        falloff = jnp.maximum(1.0 - square * lax.rsqrt(square), 0.0)
        high, low = split_two(falloff * falloff * falloff)
        weight_ref[part, 0:TILE, :] = high
        weight_ref[part, TILE:, :] = low

    def add_sums(slot, part, live):
        a = list_ref[0, slot]
        b = list_ref[1, slot]
        cols = pl.ds(pl.multiple_of(a * TILE, TILE), TILE)
        sums = jnp.dot(terms_ref[b], weight_ref[part], preferred_element_type=f32)
        acc_ref[:, cols] += live * (sums[0:16] + sums[16:32])

    count = count_ref[0]
    trips = (count + UNROLL - 1) // UNROLL
    last = list_ref.shape[1] - 1

    for part in range(UNROLL):
        pair_weights(min(part, last), part)

    @pl.loop(1, trips)
    def _(trip):
        for part in range(UNROLL):
            add_sums((trip - 1) * UNROLL + part, part, 1.0)
        for part in range(UNROLL):
            pair_weights(jnp.minimum(trip * UNROLL + part, last), part)

    for part in range(UNROLL):
        slot = (trips - 1) * UNROLL + part
        live = jnp.where(slot < count, 1.0, 0.0).astype(f32)
        add_sums(jnp.clip(slot, 0, last), part, live)

    for copy in copies[3:]:
        copy.wait()
    group = group_of(owners)
    width = group * SLOT

    row = lax.broadcasted_iota(jnp.int32, state_ref.shape, 0)
    still = state_ref[...] + jnp.where(row == 2, -gravity_step, 0.0)
    still = still / jnp.concatenate([inverse_ref[0:1, :]] * 3 + [inverse_ref[1:4, :]], axis=0)

    @pl.loop(0, owners // group)
    def _(block):
        cols = pl.ds(pl.multiple_of(block * width, width), width)
        acc = acc_ref[:, cols]
        place = place_ref[:, cols]
        sphere = sphere_ref[:, cols]
        offset = offset_ref[:, cols]
        total = acc[7:8]
        pull = total * place - acc[0:3]
        press = acc[6:7] * place - acc[8:11]
        scale = press_coef * support_radius
        force = scale * (sphere[6:7] * pull + press) + visc_coef * (acc[3:6] - total * sphere[3:6])
        force = [force[k : k + 1] for k in range(3)]
        turn = cross([offset[k : k + 1] for k in range(3)], force)
        loads = jnp.concatenate(force + turn + [jnp.zeros_like(force[0])] * 2, axis=0)
        high, low = split_two(loads)
        both = jnp.concatenate([high, low], axis=0)
        column = lax.broadcasted_iota(jnp.int32, (clumps, SLOT), 0)
        results = []
        for k in range(group):
            here = pl.ds(pl.multiple_of(block * width + k * SLOT, SLOT), SLOT)
            one_hot = jnp.where(column == ids_ref[:, here], 1.0, 0.0).astype(bf16)
            sums = lax.dot_general(
                both[:, k * SLOT : (k + 1) * SLOT], one_hot, (((1,), (1,)), ((), ())),
                preferred_element_type=f32,
            )
            own = jnp.where(block * group + k == me, 1.0, 0.0).astype(f32)
            results.append((sums[0:8] + sums[8:16])[0:6] + own * still)
        here = pl.ds(pl.multiple_of(block * (6 * group), math.gcd(6 * group, 8)), 6 * group)
        out_ref[here, :] = jnp.concatenate(results, axis=0)


def first_kernel(mine_ref, arrived_ref, inverse_ref, out_ref):
    rows = mine_ref.shape[0]
    out_ref[0:rows, :] = mine_ref[...] + arrived_ref[...]
    out_ref[rows:, :] = inverse_ref[...]


def sum_rows(refs, rows):
    sums = [ref[0:rows, :] for ref in refs]
    while len(sums) > 1:
        sums = [left + right for left, right in zip(sums[0::2], sums[1::2])]
    return sums[0]


def join_kernel(rows, *refs):
    *parts, out_ref = refs
    more = parts[0].shape[0] - rows
    out_ref[0:rows, :] = sum_rows(parts, rows)
    for k, ref in enumerate(parts):
        out_ref[rows + k * more : rows + (k + 1) * more, :] = ref[rows:, :]


def update_kernel(partners, *refs):
    *parts, out_ref, inverse_ref = refs
    owners = len(partners)
    rows = 6 * owners
    held = owners // len(parts)
    me = lax.axis_index("space")
    for k, partner in enumerate(partners):
        first = rows + 4 * (k % held)
        inverse = parts[k // held][first : first + 4, :]
        inverse_ref[me ^ partner] = jnp.concatenate([inverse[0:1]] * 3 + [inverse[1:4]], axis=0)
    out_ref[...] = sum_rows(parts, rows) * jnp.concatenate([inverse_ref[k] for k in range(owners)], axis=0)


def velocity_kernel(mine_ref, arrived_ref, offset_ref, ids_ref, clump_ref, sphere_ref, velocity_ref):
    owners, _, clumps = velocity_ref.shape
    group = group_of(owners)
    core = lax.axis_index("sub")

    @pl.loop(0, owners // group)
    def _(block):
        rows = pl.ds(pl.multiple_of(block * (6 * group), math.gcd(6 * group, 8)), 6 * group)
        velocities = jnp.where(core == 1, mine_ref[rows, :], arrived_ref[rows, :])
        for k in range(group):
            owner = block * group + k
            velocity = velocities[6 * k : 6 * k + 6]
            velocity_ref[owner] = velocity
            both = jnp.concatenate(
                split_two(jnp.concatenate([velocity, jnp.zeros((2, clumps), f32)], axis=0)), axis=0
            )
            here = pl.ds(pl.multiple_of(owner * SLOT, SLOT), SLOT)
            column = lax.broadcasted_iota(jnp.int32, (clumps, SLOT), 0)
            one_hot = jnp.where(column == ids_ref[:, here], 1.0, 0.0).astype(bf16)
            picked = jnp.dot(both, one_hot, preferred_element_type=f32)
            picked = picked[0:8] + picked[8:16]
            offset = offset_ref[:, here]
            turn = cross([picked[3 + i : 4 + i] for i in range(3)], [offset[i : i + 1] for i in range(3)])
            sphere_ref[:, here] = picked[0:3] + jnp.concatenate(turn, axis=0)

    clump_ref[...] = velocity_ref[lax.axis_index("space")]


def swap(value, bit):
    chips = range(lax.axis_size("space"))
    pairs = [(2 * k, 2 * k) for k in chips] + [(2 * k + 1, 2 * (k ^ bit) + 1) for k in chips]
    return lax.ppermute(value, ("space", "sub"), pairs)


def per_device(
    fluid_state, sphere_state, sphere_offset, tile_list, tile_count, clump_ids, clump_state, clump_inverse
):
    owners = lax.axis_size("space")
    spheres = sphere_state.shape[1]
    fluid = fluid_state.shape[1]
    clumps = clump_state.shape[1]
    slots = tile_list.shape[0]
    rows = 6 * owners
    ids = clump_ids.reshape(1, spheres)
    vmem = pl.BlockSpec(memory_space=pltpu.VMEM)
    hbm = pl.BlockSpec(memory_space=pltpu.HBM)
    params = pltpu.CompilerParams(vmem_limit_bytes=48 * 1024 * 1024)

    partial = pl.pallas_call(
        loads_kernel,
        out_shape=pltpu.VMEM((rows, clumps), f32),
        in_specs=[pl.BlockSpec(memory_space=pltpu.SMEM)] + [hbm] * 7,
        out_specs=vmem,
        scratch_shapes=[
            pltpu.SMEM((2, slots), jnp.int32),
            pltpu.VMEM((8, fluid), f32),
            pltpu.VMEM((7, spheres), f32),
            pltpu.VMEM((3, spheres), f32),
            pltpu.VMEM((1, spheres), jnp.int32),
            pltpu.VMEM((6, clumps), f32),
            pltpu.VMEM((4, clumps), f32),
            pltpu.SemaphoreType.DMA((7,)),
            pltpu.VMEM((3, spheres), f32),
            pltpu.VMEM((BLOCK, TILE, 3 * TILE), bf16),
            pltpu.VMEM((fluid // TILE, TILE, 3 * TILE), f32),
            pltpu.VMEM((fluid // TILE, 32, 2 * TILE), bf16),
            pltpu.VMEM((UNROLL, 2 * TILE, TILE), bf16),
            pltpu.VMEM((16, spheres), f32),
        ],
        compiler_params=params,
        name="clump_loads",
    )(tile_count, *(
        pltpu.with_memory_space_constraint(value, pltpu.HBM)
        for value in (
            tile_list.T, fluid_state, sphere_state, sphere_offset, ids, clump_state, clump_inverse
        )
    ))

    def small(kernel, height, name, *operands, scratch=()):
        return pl.pallas_call(
            kernel,
            out_shape=pltpu.VMEM((height, clumps), f32),
            in_specs=[vmem] * len(operands),
            out_specs=vmem,
            scratch_shapes=scratch,
            compiler_params=params,
            name=name,
        )(*operands)

    arrived = lax.ppermute(partial, "sub", [(0, 1), (1, 0)])
    mine = small(first_kernel, rows + 4, "core_sum", partial, arrived, clump_inverse)
    bits = []
    left = owners
    while left > 1:
        step = [left // 2, left // 4] if left > 2 else [1]
        left //= 2 ** len(step)
        bits += step
        others = step if len(step) == 1 else [*step, sum(step)]
        parts = [mine] + [swap(mine, bit) for bit in others]
        if left > 1:
            height = rows + len(parts) * (mine.shape[0] - rows)
            mine = small(functools.partial(join_kernel, rows), height, "space_sum", *parts)
    partners = [sum(bit for n, bit in enumerate(bits) if k >> n & 1) for k in range(owners)]
    velocities = small(
        functools.partial(update_kernel, partners), rows, "clump_update", *parts,
        scratch=[pltpu.VMEM((owners, 6, clumps), f32)],
    )

    return pl.pallas_call(
        velocity_kernel,
        out_shape=(
            jax.ShapeDtypeStruct((6, clumps), f32),
            jax.ShapeDtypeStruct((3, spheres), f32),
        ),
        in_specs=[vmem] * 4,
        out_specs=(vmem, vmem),
        scratch_shapes=[pltpu.VMEM((owners, 6, clumps), f32)],
        compiler_params=params,
        name="sphere_velocities",
    )(velocities, lax.ppermute(velocities, "sub", [(0, 1), (1, 0)]), sphere_offset, ids)


def solution(mesh):
    in_specs = (
        P(None, "space"),
        P(None, "space"),
        P(None, "space"),
        P(("space", "sub"), None),
        P(("space", "sub")),
        P("space"),
        P(None, "space"),
        P(None, "space"),
    )
    out_specs = (P(None, "space"), P(None, "space"))
    return jax.shard_map(
        per_device, mesh=mesh, in_specs=in_specs, out_specs=out_specs, check_vma=False
    )
```

```python
import functools
import math

import jax
import jax.numpy as jnp
from jax import lax
from jax.experimental import pallas as pl
from jax.experimental.pallas import tpu as pltpu
from jax.sharding import PartitionSpec as P

TILE = 128
SLOT = 256
UNROLL = 8
LANES = 16
BLOCK = TILE // LANES

support_radius = 0.5
press_coef = 4.0
visc_coef = 1.0
gravity_step = 0.1

f32 = jnp.float32
bf16 = jnp.bfloat16


def split_two(value):
    high = value.astype(bf16)
    return high, (value - high.astype(f32)).astype(bf16)


def split_three(value):
    high = value.astype(bf16).astype(f32)
    middle = (value - high).astype(bf16).astype(f32)
    return high, middle, (value - high) - middle


def cross(left, right):
    return [
        left[1] * right[2] - left[2] * right[1],
        left[2] * right[0] - left[0] * right[2],
        left[0] * right[1] - left[1] * right[0],
    ]


def group_of(owners):
    return math.gcd(owners, 16)


def loads_kernel(
    count_ref, list_hbm, fluid_hbm, sphere_hbm, offset_hbm, ids_hbm, state_hbm, inverse_hbm,
    keep_ref, send_ref,
    list_ref, fluid_ref, sphere_ref, offset_ref, ids_ref, state_ref, inverse_ref, arrived,
    place_ref, choose_ref, wide_ref, terms_ref, weight_ref, acc_ref,
):
    fluid_tiles = fluid_ref.shape[1] // TILE
    clumps = keep_ref.shape[1]
    owners = keep_ref.shape[0] // 3
    core = lax.axis_index("sub")
    me = jnp.where(core == 0, lax.axis_index("space"), -1)

    pairs = (
        (fluid_hbm, fluid_ref),
        (sphere_hbm, sphere_ref),
        (list_hbm, list_ref),
        (offset_hbm, offset_ref),
        (ids_hbm, ids_ref),
        (state_hbm, state_ref),
        (inverse_hbm, inverse_ref),
    )
    copies = [
        pltpu.make_async_copy(source, target, arrived.at[k]) for k, (source, target) in enumerate(pairs)
    ]
    for copy in copies:
        copy.start()

    acc_ref[...] = jnp.zeros_like(acc_ref)

    lane = lax.broadcasted_iota(jnp.int32, (TILE, 3 * TILE), 0)
    target = lax.broadcasted_iota(jnp.int32, (TILE, 3 * TILE), 1) // TILE
    part = lane % LANES
    wanted = (part == target) | (part == target + 3) | (part == target + 6)
    for j in range(BLOCK):
        choose_ref[j] = jnp.where(wanted & (lane // LANES == j), 1.0, 0.0).astype(bf16)
    copies[0].wait()

    @pl.loop(0, fluid_tiles // BLOCK)
    def _(block):
        row = lax.broadcasted_iota(jnp.int32, (8, TILE), 0)
        lines = []
        for j in range(BLOCK):
            tile = block * BLOCK + j
            state = fluid_ref[:, pl.ds(pl.multiple_of(tile * TILE, TILE), TILE)]
            state = jnp.where(row < 3, state * (1.0 / support_radius) - 1.0, state)
            mass = state[7:8]
            first = jnp.where(row < 7, state * mass, state)
            second = jnp.where(row < 3, state * (mass * state[6:7]), 0.0)
            high, low = split_two(jnp.concatenate([first, second], axis=0))
            both = jnp.concatenate([high, low], axis=0)
            terms_ref[tile] = jnp.concatenate([both, both], axis=1)
            lines += [*split_three(state[0:3]), jnp.zeros((LANES - 9, TILE), f32)]
        turned = jnp.concatenate(lines, axis=0).T.astype(bf16)
        for j in range(BLOCK):
            wide_ref[block * BLOCK + j] = jnp.dot(turned, choose_ref[j], preferred_element_type=f32)

    copies[1].wait()
    place_ref[...] = sphere_ref[0:3, :] * (1.0 / support_radius) - 1.0
    copies[2].wait()

    def pair_weights(slot, part):
        a = list_ref[0, slot]
        b = list_ref[1, slot]
        cols = pl.ds(pl.multiple_of(a * TILE, TILE), TILE)
        dx, dy, dz = [
            place_ref[k : k + 1, cols] - wide_ref[b, :, k * TILE : (k + 1) * TILE] for k in range(3)
        ]
        square = jnp.maximum(dx * dx + dy * dy + dz * dz, 1e-30)
        falloff = jnp.maximum(1.0 - square * lax.rsqrt(square), 0.0)
        high, low = split_two(falloff * falloff * falloff)
        weight_ref[part, 0:TILE, :] = high
        weight_ref[part, TILE:, :] = low

    def add_sums(slot, part, live):
        a = list_ref[0, slot]
        b = list_ref[1, slot]
        cols = pl.ds(pl.multiple_of(a * TILE, TILE), TILE)
        sums = jnp.dot(terms_ref[b], weight_ref[part], preferred_element_type=f32)
        acc_ref[:, cols] += live * (sums[0:16] + sums[16:32])

    count = count_ref[0]
    trips = (count + UNROLL - 1) // UNROLL
    last = list_ref.shape[1] - 1

    for part in range(UNROLL):
        pair_weights(min(part, last), part)

    @pl.loop(1, trips)
    def _(trip):
        for part in range(UNROLL):
            add_sums((trip - 1) * UNROLL + part, part, 1.0)
        for part in range(UNROLL):
            pair_weights(jnp.minimum(trip * UNROLL + part, last), part)

    for part in range(UNROLL):
        slot = (trips - 1) * UNROLL + part
        live = jnp.where(slot < count, 1.0, 0.0).astype(f32)
        add_sums(jnp.clip(slot, 0, last), part, live)

    for copy in copies[3:]:
        copy.wait()
    group = group_of(owners)
    width = group * SLOT

    row = lax.broadcasted_iota(jnp.int32, state_ref.shape, 0)
    still = state_ref[...] + jnp.where(row == 2, -gravity_step, 0.0)
    still = still / jnp.concatenate([inverse_ref[0:1, :]] * 3 + [inverse_ref[1:4, :]], axis=0)

    @pl.loop(0, owners // group)
    def _(block):
        cols = pl.ds(pl.multiple_of(block * width, width), width)
        acc = acc_ref[:, cols]
        place = place_ref[:, cols]
        sphere = sphere_ref[:, cols]
        offset = offset_ref[:, cols]
        total = acc[7:8]
        pull = total * place - acc[0:3]
        press = acc[6:7] * place - acc[8:11]
        scale = press_coef * support_radius
        force = scale * (sphere[6:7] * pull + press) + visc_coef * (acc[3:6] - total * sphere[3:6])
        force = [force[k : k + 1] for k in range(3)]
        turn = cross([offset[k : k + 1] for k in range(3)], force)
        loads = jnp.concatenate(force + turn + [jnp.zeros_like(force[0])] * 2, axis=0)
        high, low = split_two(loads)
        both = jnp.concatenate([high, low], axis=0)
        column = lax.broadcasted_iota(jnp.int32, (clumps, SLOT), 0)
        keep, send = [], []
        for k in range(group):
            here = pl.ds(pl.multiple_of(block * width + k * SLOT, SLOT), SLOT)
            one_hot = jnp.where(column == ids_ref[:, here], 1.0, 0.0).astype(bf16)
            sums = lax.dot_general(
                both[:, k * SLOT : (k + 1) * SLOT], one_hot, (((1,), (1,)), ((), ())),
                preferred_element_type=f32,
            )
            own = jnp.where(block * group + k == me, 1.0, 0.0).astype(f32)
            sums = (sums[0:8] + sums[8:16])[0:6] + own * still
            keep.append(jnp.where(core == 0, sums[0:3], sums[3:6]))
            send.append(jnp.where(core == 0, sums[3:6], sums[0:3]))
        here = pl.ds(pl.multiple_of(block * (3 * group), math.gcd(3 * group, 8)), 3 * group)
        keep_ref[here, :] = jnp.concatenate(keep, axis=0)
        send_ref[here, :] = jnp.concatenate(send, axis=0)


def first_kernel(keep_ref, arrived_ref, inverse_ref, out_ref):
    rows = keep_ref.shape[0]
    out_ref[0:rows, :] = keep_ref[...] + arrived_ref[...]
    linear = jnp.concatenate([inverse_ref[0:1, :]] * 3, axis=0)
    out_ref[rows:, :] = jnp.where(lax.axis_index("sub") == 0, linear, inverse_ref[1:4, :])


def sum_rows(parts, rows):
    return functools.reduce(lambda total, part: total + part, [part[0:rows, :] for part in parts])


def join_kernel(rows, parts_ref, out_ref):
    parts = [parts_ref.at[k] for k in range(parts_ref.shape[0])]
    more = parts_ref.shape[1] - rows
    out_ref[0:rows, :] = sum_rows(parts, rows)
    for k, part in enumerate(parts):
        out_ref[rows + k * more : rows + (k + 1) * more, :] = part[rows:, :]


def update_kernel(holders, parts_ref, out_ref, inverse_ref):
    parts = [parts_ref.at[k] for k in range(parts_ref.shape[0])]
    owners = len(holders)
    rows = 3 * owners
    held = owners // len(parts)
    for k, owner in enumerate(holders):
        first = rows + 3 * (k % held)
        inverse_ref[owner] = parts[k // held][first : first + 3, :]
    out_ref[...] = sum_rows(parts, rows) * jnp.concatenate([inverse_ref[k] for k in range(owners)], axis=0)


def velocity_kernel(mine_ref, arrived_ref, offset_ref, ids_ref, clump_ref, sphere_ref, velocity_ref):
    owners, _, clumps = velocity_ref.shape
    group = group_of(owners)
    core = lax.axis_index("sub")

    @pl.loop(0, owners // group)
    def _(block):
        rows = pl.ds(pl.multiple_of(block * (3 * group), math.gcd(3 * group, 8)), 3 * group)
        mine = mine_ref[rows, :]
        arrived = arrived_ref[rows, :]
        linear = jnp.where(core == 0, mine, arrived)
        angular = jnp.where(core == 0, arrived, mine)
        for k in range(group):
            owner = block * group + k
            three = slice(3 * k, 3 * k + 3)
            velocity = jnp.concatenate([linear[three], angular[three]], axis=0)
            velocity_ref[owner] = velocity
            both = jnp.concatenate(
                split_two(jnp.concatenate([velocity, jnp.zeros((2, clumps), f32)], axis=0)), axis=0
            )
            here = pl.ds(pl.multiple_of(owner * SLOT, SLOT), SLOT)
            column = lax.broadcasted_iota(jnp.int32, (clumps, SLOT), 0)
            one_hot = jnp.where(column == ids_ref[:, here], 1.0, 0.0).astype(bf16)
            picked = jnp.dot(both, one_hot, preferred_element_type=f32)
            picked = picked[0:8] + picked[8:16]
            offset = offset_ref[:, here]
            turn = cross([picked[3 + i : 4 + i] for i in range(3)], [offset[i : i + 1] for i in range(3)])
            sphere_ref[:, here] = picked[0:3] + jnp.concatenate(turn, axis=0)

    clump_ref[...] = velocity_ref[lax.axis_index("space")]


def swap(value, axis, bit):
    size = lax.axis_size(axis)
    return lax.ppermute(value, axis, [(k, k ^ bit) for k in range(size)])


def per_device(
    fluid_state, sphere_state, sphere_offset, tile_list, tile_count, clump_ids, clump_state, clump_inverse
):
    owners = lax.axis_size("space")
    spheres = sphere_state.shape[1]
    fluid = fluid_state.shape[1]
    clumps = clump_state.shape[1]
    slots = tile_list.shape[0]
    rows = 3 * owners
    ids = clump_ids.reshape(1, spheres)
    vmem = pl.BlockSpec(memory_space=pltpu.VMEM)
    hbm = pl.BlockSpec(memory_space=pltpu.HBM)
    params = pltpu.CompilerParams(vmem_limit_bytes=48 * 1024 * 1024)

    keep, send = pl.pallas_call(
        loads_kernel,
        out_shape=(pltpu.VMEM((rows, clumps), f32), pltpu.VMEM((rows, clumps), f32)),
        in_specs=[pl.BlockSpec(memory_space=pltpu.SMEM)] + [hbm] * 7,
        out_specs=(vmem, vmem),
        scratch_shapes=[
            pltpu.SMEM((2, slots), jnp.int32),
            pltpu.VMEM((8, fluid), f32),
            pltpu.VMEM((7, spheres), f32),
            pltpu.VMEM((3, spheres), f32),
            pltpu.VMEM((1, spheres), jnp.int32),
            pltpu.VMEM((6, clumps), f32),
            pltpu.VMEM((4, clumps), f32),
            pltpu.SemaphoreType.DMA((7,)),
            pltpu.VMEM((3, spheres), f32),
            pltpu.VMEM((BLOCK, TILE, 3 * TILE), bf16),
            pltpu.VMEM((fluid // TILE, TILE, 3 * TILE), f32),
            pltpu.VMEM((fluid // TILE, 32, 2 * TILE), bf16),
            pltpu.VMEM((UNROLL, 2 * TILE, TILE), bf16),
            pltpu.VMEM((16, spheres), f32),
        ],
        compiler_params=params,
        name="clump_loads",
    )(tile_count, *(
        pltpu.with_memory_space_constraint(value, pltpu.HBM)
        for value in (
            tile_list.T, fluid_state, sphere_state, sphere_offset, ids, clump_state, clump_inverse
        )
    ))

    def small(kernel, height, name, *operands, scratch=()):
        return pl.pallas_call(
            kernel,
            out_shape=pltpu.VMEM((height, clumps), f32),
            in_specs=[vmem] * len(operands),
            out_specs=vmem,
            scratch_shapes=scratch,
            compiler_params=params,
            name=name,
        )(*operands)

    mine = small(first_kernel, rows + 3, "core_sum", keep, swap(send, "sub", 1), clump_inverse)
    holders = [0]
    stride = owners
    while stride > 1:
        count = math.gcd(stride, 4)
        stride //= count
        groups = [
            [first + k * stride for k in range(count)]
            for first in range(owners)
            if first // stride % count == 0
        ]
        parts = lax.all_gather(mine, "space", axis_index_groups=groups)
        holders = [owner + k * stride for k in range(count) for owner in holders]
        if stride > 1:
            height = rows + count * (mine.shape[0] - rows)
            mine = small(functools.partial(join_kernel, rows), height, "space_sum", parts)
    velocities = small(
        functools.partial(update_kernel, holders), rows, "clump_update", parts,
        scratch=[pltpu.VMEM((owners, 3, clumps), f32)],
    )

    return pl.pallas_call(
        velocity_kernel,
        out_shape=(
            jax.ShapeDtypeStruct((6, clumps), f32),
            jax.ShapeDtypeStruct((3, spheres), f32),
        ),
        in_specs=[vmem] * 4,
        out_specs=(vmem, vmem),
        scratch_shapes=[pltpu.VMEM((owners, 6, clumps), f32)],
        compiler_params=params,
        name="sphere_velocities",
    )(velocities, swap(velocities, "sub", 1), sphere_offset, ids)


def solution(mesh):
    in_specs = (
        P(None, "space"),
        P(None, "space"),
        P(None, "space"),
        P(("space", "sub"), None),
        P(("space", "sub")),
        P("space"),
        P(None, "space"),
        P(None, "space"),
    )
    out_specs = (P(None, "space"), P(None, "space"))
    return jax.shard_map(
        per_device, mesh=mesh, in_specs=in_specs, out_specs=out_specs, check_vma=False
    )
```

```python
import functools
import math

import jax
import jax.numpy as jnp
from jax import lax
from jax.experimental import pallas as pl
from jax.experimental.pallas import tpu as pltpu
from jax.sharding import PartitionSpec as P

TILE = 128
SLOT = 256
UNROLL = 4
LANES = 16
BLOCK = TILE // LANES

support_radius = 0.5
press_coef = 4.0
visc_coef = 1.0
gravity_step = 0.1

f32 = jnp.float32
bf16 = jnp.bfloat16


def split_two(value):
    high = value.astype(bf16)
    return high, (value - high.astype(f32)).astype(bf16)


def split_three(value):
    high = value.astype(bf16).astype(f32)
    middle = (value - high).astype(bf16).astype(f32)
    return high, middle, (value - high) - middle


def cross(left, right):
    return [
        left[1] * right[2] - left[2] * right[1],
        left[2] * right[0] - left[0] * right[2],
        left[0] * right[1] - left[1] * right[0],
    ]


def group_of(owners):
    return math.gcd(owners, 16)


def loads_kernel(
    count_ref, list_hbm, fluid_hbm, sphere_hbm, offset_hbm, ids_hbm, state_hbm, inverse_hbm,
    keep_ref, send_ref,
    list_ref, fluid_ref, sphere_ref, offset_ref, ids_ref, state_ref, inverse_ref, arrived,
    place_ref, choose_ref, wide_ref, terms_ref, weight_ref, acc_ref,
):
    fluid_tiles = fluid_ref.shape[1] // TILE
    clumps = keep_ref.shape[1]
    owners = keep_ref.shape[0] // 3
    core = lax.axis_index("sub")
    me = jnp.where(core == 0, lax.axis_index("space"), -1)

    pairs = (
        (fluid_hbm, fluid_ref),
        (sphere_hbm, sphere_ref),
        (list_hbm, list_ref),
        (offset_hbm, offset_ref),
        (ids_hbm, ids_ref),
        (state_hbm, state_ref),
        (inverse_hbm, inverse_ref),
    )
    copies = [
        pltpu.make_async_copy(source, target, arrived.at[k]) for k, (source, target) in enumerate(pairs)
    ]
    for copy in copies:
        copy.start()

    acc_ref[...] = jnp.zeros_like(acc_ref)

    lane = lax.broadcasted_iota(jnp.int32, (TILE, 3 * TILE), 0)
    target = lax.broadcasted_iota(jnp.int32, (TILE, 3 * TILE), 1) // TILE
    part = lane % LANES
    wanted = (part == target) | (part == target + 3) | (part == target + 6)
    for j in range(BLOCK):
        choose_ref[j] = jnp.where(wanted & (lane // LANES == j), 1.0, 0.0).astype(bf16)
    copies[0].wait()

    @pl.loop(0, fluid_tiles // BLOCK)
    def _(block):
        row = lax.broadcasted_iota(jnp.int32, (8, TILE), 0)
        lines = []
        for j in range(BLOCK):
            tile = block * BLOCK + j
            state = fluid_ref[:, pl.ds(pl.multiple_of(tile * TILE, TILE), TILE)]
            state = jnp.where(row < 3, state * (1.0 / support_radius) - 1.0, state)
            mass = state[7:8]
            first = jnp.where(row < 7, state * mass, state)
            second = jnp.where(row < 3, state * (mass * state[6:7]), 0.0)
            high, low = split_two(jnp.concatenate([first, second], axis=0))
            both = jnp.concatenate([high, low], axis=0)
            terms_ref[tile] = jnp.concatenate([both, both], axis=1)
            lines += [*split_three(state[0:3]), jnp.zeros((LANES - 9, TILE), f32)]
        turned = jnp.concatenate(lines, axis=0).T.astype(bf16)
        for j in range(BLOCK):
            wide_ref[block * BLOCK + j] = jnp.dot(turned, choose_ref[j], preferred_element_type=f32)

    copies[1].wait()
    place_ref[...] = sphere_ref[0:3, :] * (1.0 / support_radius) - 1.0
    copies[2].wait()

    def pair_weights(slot, part):
        a = list_ref[0, slot]
        b = list_ref[1, slot]
        cols = pl.ds(pl.multiple_of(a * TILE, TILE), TILE)
        dx, dy, dz = [
            place_ref[k : k + 1, cols] - wide_ref[b, :, k * TILE : (k + 1) * TILE] for k in range(3)
        ]
        square = jnp.maximum(dx * dx + dy * dy + dz * dz, 1e-30)
        falloff = jnp.maximum(1.0 - square * lax.rsqrt(square), 0.0)
        high, low = split_two(falloff * falloff * falloff)
        weight_ref[part, 0:TILE, :] = high
        weight_ref[part, TILE:, :] = low

    def add_sums(slot, part, live):
        a = list_ref[0, slot]
        b = list_ref[1, slot]
        cols = pl.ds(pl.multiple_of(a * TILE, TILE), TILE)
        sums = jnp.dot(terms_ref[b], weight_ref[part], preferred_element_type=f32)
        acc_ref[:, cols] += live * (sums[0:16] + sums[16:32])

    count = count_ref[0]
    trips = (count + UNROLL - 1) // UNROLL
    last = list_ref.shape[1] - 1

    for part in range(UNROLL):
        pair_weights(min(part, last), part)

    @pl.loop(1, trips)
    def _(trip):
        for part in range(UNROLL):
            add_sums((trip - 1) * UNROLL + part, part, 1.0)
        for part in range(UNROLL):
            pair_weights(jnp.minimum(trip * UNROLL + part, last), part)

    for part in range(UNROLL):
        slot = (trips - 1) * UNROLL + part
        live = jnp.where(slot < count, 1.0, 0.0).astype(f32)
        add_sums(jnp.clip(slot, 0, last), part, live)

    for copy in copies[3:]:
        copy.wait()
    group = group_of(owners)
    width = group * SLOT

    row = lax.broadcasted_iota(jnp.int32, state_ref.shape, 0)
    still = state_ref[...] + jnp.where(row == 2, -gravity_step, 0.0)
    still = still / jnp.concatenate([inverse_ref[0:1, :]] * 3 + [inverse_ref[1:4, :]], axis=0)

    @pl.loop(0, owners // group)
    def _(block):
        cols = pl.ds(pl.multiple_of(block * width, width), width)
        acc = acc_ref[:, cols]
        place = place_ref[:, cols]
        sphere = sphere_ref[:, cols]
        offset = offset_ref[:, cols]
        total = acc[7:8]
        pull = total * place - acc[0:3]
        press = acc[6:7] * place - acc[8:11]
        scale = press_coef * support_radius
        force = scale * (sphere[6:7] * pull + press) + visc_coef * (acc[3:6] - total * sphere[3:6])
        force = [force[k : k + 1] for k in range(3)]
        turn = cross([offset[k : k + 1] for k in range(3)], force)
        loads = jnp.concatenate(force + turn + [jnp.zeros_like(force[0])] * 2, axis=0)
        high, low = split_two(loads)
        both = jnp.concatenate([high, low], axis=0)
        column = lax.broadcasted_iota(jnp.int32, (clumps, SLOT), 0)
        keep, send = [], []
        for k in range(group):
            here = pl.ds(pl.multiple_of(block * width + k * SLOT, SLOT), SLOT)
            one_hot = jnp.where(column == ids_ref[:, here], 1.0, 0.0).astype(bf16)
            sums = lax.dot_general(
                both[:, k * SLOT : (k + 1) * SLOT], one_hot, (((1,), (1,)), ((), ())),
                preferred_element_type=f32,
            )
            own = jnp.where(block * group + k == me, 1.0, 0.0).astype(f32)
            sums = (sums[0:8] + sums[8:16])[0:6] + own * still
            keep.append(jnp.where(core == 0, sums[0:3], sums[3:6]))
            send.append(jnp.where(core == 0, sums[3:6], sums[0:3]))
        here = pl.ds(pl.multiple_of(block * (3 * group), math.gcd(3 * group, 8)), 3 * group)
        keep_ref[here, :] = jnp.concatenate(keep, axis=0)
        send_ref[here, :] = jnp.concatenate(send, axis=0)


def first_kernel(keep_ref, arrived_ref, inverse_ref, out_ref):
    rows = keep_ref.shape[0]
    out_ref[0:rows, :] = keep_ref[...] + arrived_ref[...]
    linear = jnp.concatenate([inverse_ref[0:1, :]] * 3, axis=0)
    out_ref[rows:, :] = jnp.where(lax.axis_index("sub") == 0, linear, inverse_ref[1:4, :])


def sum_rows(refs, rows):
    sums = [ref[0:rows, :] for ref in refs]
    while len(sums) > 1:
        sums = [left + right for left, right in zip(sums[0::2], sums[1::2])]
    return sums[0]


def join_kernel(rows, *refs):
    *parts, out_ref = refs
    more = parts[0].shape[0] - rows
    out_ref[0:rows, :] = sum_rows(parts, rows)
    for k, ref in enumerate(parts):
        out_ref[rows + k * more : rows + (k + 1) * more, :] = ref[rows:, :]


def update_kernel(partners, *refs):
    *parts, out_ref, inverse_ref = refs
    owners = len(partners[0])
    rows = 3 * owners
    held = owners // len(parts)
    me = lax.axis_index("space")
    first_core = lax.axis_index("sub") == 0
    for k in range(owners):
        partner = jnp.where(first_core, partners[0][k], partners[1][k])
        first = rows + 3 * (k % held)
        inverse_ref[me ^ partner] = parts[k // held][first : first + 3, :]
    out_ref[...] = sum_rows(parts, rows) * jnp.concatenate([inverse_ref[k] for k in range(owners)], axis=0)


def velocity_kernel(mine_ref, arrived_ref, offset_ref, ids_ref, clump_ref, sphere_ref, velocity_ref):
    owners, _, clumps = velocity_ref.shape
    group = group_of(owners)
    core = lax.axis_index("sub")

    @pl.loop(0, owners // group)
    def _(block):
        rows = pl.ds(pl.multiple_of(block * (3 * group), math.gcd(3 * group, 8)), 3 * group)
        mine = mine_ref[rows, :]
        arrived = arrived_ref[rows, :]
        linear = jnp.where(core == 0, mine, arrived)
        angular = jnp.where(core == 0, arrived, mine)
        for k in range(group):
            owner = block * group + k
            three = slice(3 * k, 3 * k + 3)
            velocity = jnp.concatenate([linear[three], angular[three]], axis=0)
            velocity_ref[owner] = velocity
            both = jnp.concatenate(
                split_two(jnp.concatenate([velocity, jnp.zeros((2, clumps), f32)], axis=0)), axis=0
            )
            here = pl.ds(pl.multiple_of(owner * SLOT, SLOT), SLOT)
            column = lax.broadcasted_iota(jnp.int32, (clumps, SLOT), 0)
            one_hot = jnp.where(column == ids_ref[:, here], 1.0, 0.0).astype(bf16)
            picked = jnp.dot(both, one_hot, preferred_element_type=f32)
            picked = picked[0:8] + picked[8:16]
            offset = offset_ref[:, here]
            turn = cross([picked[3 + i : 4 + i] for i in range(3)], [offset[i : i + 1] for i in range(3)])
            sphere_ref[:, here] = picked[0:3] + jnp.concatenate(turn, axis=0)

    clump_ref[...] = velocity_ref[lax.axis_index("space")]


def swap_cores(value):
    return lax.ppermute(value, "sub", [(0, 1), (1, 0)])


def swap(value, bits):
    chips = range(lax.axis_size("space"))
    pairs = [(2 * k + core, 2 * (k ^ bit) + core) for k in chips for core, bit in enumerate(bits)]
    return lax.ppermute(value, ("space", "sub"), pairs)


def steps_of(owners):
    pairs, left = [], owners
    while left > 2:
        pairs.append((left // 2, left // 4))
        left //= 4
    rest = [(1,)] * (left == 2)
    return pairs[1:] + pairs[:1] + rest, pairs + rest


def partners_of(steps):
    bits = [bit for step in steps for bit in step]
    return [sum(bit for n, bit in enumerate(bits) if k >> n & 1) for k in range(2 ** len(bits))]


def per_device(
    fluid_state, sphere_state, sphere_offset, tile_list, tile_count, clump_ids, clump_state, clump_inverse
):
    owners = lax.axis_size("space")
    spheres = sphere_state.shape[1]
    fluid = fluid_state.shape[1]
    clumps = clump_state.shape[1]
    slots = tile_list.shape[0]
    rows = 3 * owners
    ids = clump_ids.reshape(1, spheres)
    vmem = pl.BlockSpec(memory_space=pltpu.VMEM)
    hbm = pl.BlockSpec(memory_space=pltpu.HBM)
    params = pltpu.CompilerParams(vmem_limit_bytes=48 * 1024 * 1024)

    keep, send = pl.pallas_call(
        loads_kernel,
        out_shape=(pltpu.VMEM((rows, clumps), f32), pltpu.VMEM((rows, clumps), f32)),
        in_specs=[pl.BlockSpec(memory_space=pltpu.SMEM)] + [hbm] * 7,
        out_specs=(vmem, vmem),
        scratch_shapes=[
            pltpu.SMEM((2, slots), jnp.int32),
            pltpu.VMEM((8, fluid), f32),
            pltpu.VMEM((7, spheres), f32),
            pltpu.VMEM((3, spheres), f32),
            pltpu.VMEM((1, spheres), jnp.int32),
            pltpu.VMEM((6, clumps), f32),
            pltpu.VMEM((4, clumps), f32),
            pltpu.SemaphoreType.DMA((7,)),
            pltpu.VMEM((3, spheres), f32),
            pltpu.VMEM((BLOCK, TILE, 3 * TILE), bf16),
            pltpu.VMEM((fluid // TILE, TILE, 3 * TILE), f32),
            pltpu.VMEM((fluid // TILE, 32, 2 * TILE), bf16),
            pltpu.VMEM((UNROLL, 2 * TILE, TILE), bf16),
            pltpu.VMEM((16, spheres), f32),
        ],
        compiler_params=params,
        name="clump_loads",
    )(tile_count, *(
        pltpu.with_memory_space_constraint(value, pltpu.HBM)
        for value in (
            tile_list.T, fluid_state, sphere_state, sphere_offset, ids, clump_state, clump_inverse
        )
    ))

    def small(kernel, height, name, *operands, scratch=()):
        return pl.pallas_call(
            kernel,
            out_shape=pltpu.VMEM((height, clumps), f32),
            in_specs=[vmem] * len(operands),
            out_specs=vmem,
            scratch_shapes=scratch,
            compiler_params=params,
            name=name,
        )(*operands)

    mine = small(first_kernel, rows + 3, "core_sum", keep, swap_cores(send), clump_inverse)
    steps = steps_of(owners)
    for number, step in enumerate(zip(*steps)):
        both = [[*bits, sum(bits)] if len(bits) == 2 else bits for bits in step]
        parts = [mine] + [swap(mine, bits) for bits in zip(*both)]
        if number < len(steps[0]) - 1:
            height = rows + len(parts) * (mine.shape[0] - rows)
            mine = small(functools.partial(join_kernel, rows), height, "space_sum", *parts)
    partners = [partners_of(core_steps) for core_steps in steps]
    velocities = small(
        functools.partial(update_kernel, partners), rows, "clump_update", *parts,
        scratch=[pltpu.VMEM((owners, 3, clumps), f32)],
    )

    return pl.pallas_call(
        velocity_kernel,
        out_shape=(
            jax.ShapeDtypeStruct((6, clumps), f32),
            jax.ShapeDtypeStruct((3, spheres), f32),
        ),
        in_specs=[vmem] * 4,
        out_specs=(vmem, vmem),
        scratch_shapes=[pltpu.VMEM((owners, 6, clumps), f32)],
        compiler_params=params,
        name="sphere_velocities",
    )(velocities, swap_cores(velocities), sphere_offset, ids)


def solution(mesh):
    in_specs = (
        P(None, "space"),
        P(None, "space"),
        P(None, "space"),
        P(("space", "sub"), None),
        P(("space", "sub")),
        P("space"),
        P(None, "space"),
        P(None, "space"),
    )
    out_specs = (P(None, "space"), P(None, "space"))
    return jax.shard_map(
        per_device, mesh=mesh, in_specs=in_specs, out_specs=out_specs, check_vma=False
    )
```

```python
import functools
import math

import jax
import jax.numpy as jnp
from jax import lax
from jax.experimental import pallas as pl
from jax.experimental.pallas import tpu as pltpu
from jax.sharding import PartitionSpec as P

TILE = 128
SLOT = 256
UNROLL = 8
LANES = 16
BLOCK = TILE // LANES

support_radius = 0.5
press_coef = 4.0
visc_coef = 1.0
gravity_step = 0.1

f32 = jnp.float32
bf16 = jnp.bfloat16


def split_two(value):
    high = value.astype(bf16)
    return high, (value - high.astype(f32)).astype(bf16)


def split_three(value):
    high = value.astype(bf16).astype(f32)
    middle = (value - high).astype(bf16).astype(f32)
    return high, middle, (value - high) - middle


def cross(left, right):
    return [
        left[1] * right[2] - left[2] * right[1],
        left[2] * right[0] - left[0] * right[2],
        left[0] * right[1] - left[1] * right[0],
    ]


def group_of(owners):
    return math.gcd(owners, 16)


def loads_kernel(
    count_ref, list_hbm, fluid_hbm, sphere_hbm, offset_hbm, ids_hbm, state_hbm, inverse_hbm,
    keep_ref, send_ref,
    list_ref, fluid_ref, sphere_ref, offset_ref, ids_ref, state_ref, inverse_ref, arrived,
    place_ref, choose_ref, wide_ref, terms_ref, weight_ref, acc_ref,
):
    fluid_tiles = fluid_ref.shape[1] // TILE
    clumps = keep_ref.shape[1]
    owners = keep_ref.shape[0] // 3
    core = lax.axis_index("sub")
    me = jnp.where(core == 0, lax.axis_index("space"), -1)

    pairs = (
        (fluid_hbm, fluid_ref),
        (sphere_hbm, sphere_ref),
        (list_hbm, list_ref),
        (offset_hbm, offset_ref),
        (ids_hbm, ids_ref),
        (state_hbm, state_ref),
        (inverse_hbm, inverse_ref),
    )
    copies = [
        pltpu.make_async_copy(source, target, arrived.at[k]) for k, (source, target) in enumerate(pairs)
    ]
    for copy in copies:
        copy.start()

    acc_ref[...] = jnp.zeros_like(acc_ref)
    weight_ref[...] = jnp.zeros_like(weight_ref)

    lane = lax.broadcasted_iota(jnp.int32, (TILE, 3 * TILE), 0)
    target = lax.broadcasted_iota(jnp.int32, (TILE, 3 * TILE), 1) // TILE
    part = lane % LANES
    wanted = (part == target) | (part == target + 3) | (part == target + 6)
    for j in range(BLOCK):
        choose_ref[j] = jnp.where(wanted & (lane // LANES == j), 1.0, 0.0).astype(bf16)
    copies[0].wait()

    @pl.loop(0, fluid_tiles // BLOCK)
    def _(block):
        row = lax.broadcasted_iota(jnp.int32, (8, TILE), 0)
        lines = []
        for j in range(BLOCK):
            tile = block * BLOCK + j
            state = fluid_ref[:, pl.ds(pl.multiple_of(tile * TILE, TILE), TILE)]
            state = jnp.where(row < 3, state * (1.0 / support_radius) - 1.0, state)
            mass = state[7:8]
            first = jnp.where(row < 7, state * mass, state)
            second = jnp.where(row < 3, state * (mass * state[6:7]), 0.0)
            high, low = split_two(jnp.concatenate([first, second], axis=0))
            both = jnp.concatenate([high, low], axis=0)
            terms_ref[tile] = jnp.concatenate([both, both], axis=1)
            lines += [*split_three(state[0:3]), jnp.zeros((LANES - 9, TILE), f32)]
        turned = jnp.concatenate(lines, axis=0).T.astype(bf16)
        for j in range(BLOCK):
            wide_ref[block * BLOCK + j] = jnp.dot(turned, choose_ref[j], preferred_element_type=f32)

    copies[1].wait()
    place_ref[...] = sphere_ref[0:3, :] * (1.0 / support_radius) - 1.0
    copies[2].wait()

    def pair_weights(slot):
        a = list_ref[0, slot]
        b = list_ref[1, slot]
        cols = pl.ds(pl.multiple_of(a * TILE, TILE), TILE)
        dx, dy, dz = [
            place_ref[k : k + 1, cols] - wide_ref[b, :, k * TILE : (k + 1) * TILE] for k in range(3)
        ]
        square = jnp.maximum(dx * dx + dy * dy + dz * dz, 1e-30)
        falloff = jnp.maximum(1.0 - square * lax.rsqrt(square), 0.0)
        high, low = split_two(falloff * falloff * falloff)
        return jnp.concatenate([high, low], axis=0)

    count = count_ref[0]
    last = list_ref.shape[1] - 1

    def add_sums(slot, weights):
        here = jnp.clip(slot, 0, last)
        live = jnp.where((slot >= 0) & (slot < count), 1.0, 0.0).astype(f32)
        cols = pl.ds(pl.multiple_of(list_ref[0, here] * TILE, TILE), TILE)
        sums = jnp.dot(terms_ref[list_ref[1, here]], weights, preferred_element_type=f32)
        acc_ref[:, cols] += live * (sums[0:16] + sums[16:32])

    groups = (count + UNROLL - 1) // UNROLL

    @pl.loop(0, groups)
    def _(number):
        first = number * UNROLL
        add_sums(first - 1, weight_ref[...])
        for part in range(UNROLL - 1):
            add_sums(first + part, pair_weights(jnp.minimum(first + part, last)))
        weight_ref[...] = pair_weights(jnp.minimum(first + UNROLL - 1, last))

    add_sums(groups * UNROLL - 1, weight_ref[...])

    for copy in copies[3:]:
        copy.wait()
    group = group_of(owners)
    width = group * SLOT

    row = lax.broadcasted_iota(jnp.int32, state_ref.shape, 0)
    still = state_ref[...] + jnp.where(row == 2, -gravity_step, 0.0)
    still = still / jnp.concatenate([inverse_ref[0:1, :]] * 3 + [inverse_ref[1:4, :]], axis=0)

    @pl.loop(0, owners // group)
    def _(block):
        cols = pl.ds(pl.multiple_of(block * width, width), width)
        acc = acc_ref[:, cols]
        place = place_ref[:, cols]
        sphere = sphere_ref[:, cols]
        offset = offset_ref[:, cols]
        total = acc[7:8]
        pull = total * place - acc[0:3]
        press = acc[6:7] * place - acc[8:11]
        scale = press_coef * support_radius
        force = scale * (sphere[6:7] * pull + press) + visc_coef * (acc[3:6] - total * sphere[3:6])
        force = [force[k : k + 1] for k in range(3)]
        turn = cross([offset[k : k + 1] for k in range(3)], force)
        loads = jnp.concatenate(force + turn + [jnp.zeros_like(force[0])] * 2, axis=0)
        high, low = split_two(loads)
        both = jnp.concatenate([high, low], axis=0)
        column = lax.broadcasted_iota(jnp.int32, (clumps, SLOT), 0)
        keep, send = [], []
        for k in range(group):
            here = pl.ds(pl.multiple_of(block * width + k * SLOT, SLOT), SLOT)
            one_hot = jnp.where(column == ids_ref[:, here], 1.0, 0.0).astype(bf16)
            sums = lax.dot_general(
                both[:, k * SLOT : (k + 1) * SLOT], one_hot, (((1,), (1,)), ((), ())),
                preferred_element_type=f32,
            )
            own = jnp.where(block * group + k == me, 1.0, 0.0).astype(f32)
            sums = (sums[0:8] + sums[8:16])[0:6] + own * still
            keep.append(jnp.where(core == 0, sums[0:3], sums[3:6]))
            send.append(jnp.where(core == 0, sums[3:6], sums[0:3]))
        here = pl.ds(pl.multiple_of(block * (3 * group), math.gcd(3 * group, 8)), 3 * group)
        keep_ref[here, :] = jnp.concatenate(keep, axis=0)
        send_ref[here, :] = jnp.concatenate(send, axis=0)


def first_kernel(keep_ref, arrived_ref, inverse_ref, out_ref):
    rows = keep_ref.shape[0]
    out_ref[0:rows, :] = keep_ref[...] + arrived_ref[...]
    linear = jnp.concatenate([inverse_ref[0:1, :]] * 3, axis=0)
    out_ref[rows:, :] = jnp.where(lax.axis_index("sub") == 0, linear, inverse_ref[1:4, :])


def sum_rows(refs, rows):
    sums = [ref[0:rows, :] for ref in refs]
    while len(sums) > 1:
        sums = [left + right for left, right in zip(sums[0::2], sums[1::2])]
    return sums[0]


def join_kernel(rows, *refs):
    *parts, out_ref = refs
    more = parts[0].shape[0] - rows
    out_ref[0:rows, :] = sum_rows(parts, rows)
    for k, ref in enumerate(parts):
        out_ref[rows + k * more : rows + (k + 1) * more, :] = ref[rows:, :]


def update_kernel(partners, *refs):
    *parts, out_ref, inverse_ref = refs
    owners = len(partners)
    rows = 3 * owners
    held = owners // len(parts)
    me = lax.axis_index("space")
    for k, partner in enumerate(partners):
        first = rows + 3 * (k % held)
        inverse_ref[me ^ partner] = parts[k // held][first : first + 3, :]
    out_ref[...] = sum_rows(parts, rows) * jnp.concatenate([inverse_ref[k] for k in range(owners)], axis=0)


def velocity_kernel(
    mine_ref, arrived_ref, offset_ref, ids_ref, clump_ref, sphere_hbm, velocity_ref, sphere_ref, sent
):
    owners, _, clumps = velocity_ref.shape
    group = group_of(owners)
    core = lax.axis_index("sub")

    part = math.gcd(group, 4)

    @pl.loop(0, owners // group)
    def _(block):
        copies = []
        rows = pl.ds(pl.multiple_of(block * (3 * group), math.gcd(3 * group, 8)), 3 * group)
        mine = mine_ref[rows, :]
        arrived = arrived_ref[rows, :]
        linear = jnp.where(core == 0, mine, arrived)
        angular = jnp.where(core == 0, arrived, mine)
        for k in range(group):
            owner = block * group + k
            three = slice(3 * k, 3 * k + 3)
            velocity = jnp.concatenate([linear[three], angular[three]], axis=0)
            velocity_ref[owner] = velocity
            both = jnp.concatenate(
                split_two(jnp.concatenate([velocity, jnp.zeros((2, clumps), f32)], axis=0)), axis=0
            )
            here = pl.ds(pl.multiple_of(owner * SLOT, SLOT), SLOT)
            column = lax.broadcasted_iota(jnp.int32, (clumps, SLOT), 0)
            one_hot = jnp.where(column == ids_ref[:, here], 1.0, 0.0).astype(bf16)
            picked = jnp.dot(both, one_hot, preferred_element_type=f32)
            picked = picked[0:8] + picked[8:16]
            offset = offset_ref[:, here]
            turn = cross([picked[3 + i : 4 + i] for i in range(3)], [offset[i : i + 1] for i in range(3)])
            sphere_ref[:, here] = picked[0:3] + jnp.concatenate(turn, axis=0)
            if (k + 1) % part == 0:
                start = pl.multiple_of((owner + 1 - part) * SLOT, SLOT)
                done = pl.ds(start, part * SLOT)
                copies.append(
                    pltpu.make_async_copy(sphere_ref.at[:, done], sphere_hbm.at[:, done], sent.at[k // part])
                )
                copies[-1].start()
        for copy in copies:
            copy.wait()

    clump_ref[...] = velocity_ref[lax.axis_index("space")]


def swap(value, axis, bit):
    size = lax.axis_size(axis)
    return lax.ppermute(value, axis, [(k, k ^ bit) for k in range(size)])


def per_device(
    fluid_state, sphere_state, sphere_offset, tile_list, tile_count, clump_ids, clump_state, clump_inverse
):
    owners = lax.axis_size("space")
    spheres = sphere_state.shape[1]
    fluid = fluid_state.shape[1]
    clumps = clump_state.shape[1]
    slots = tile_list.shape[0]
    rows = 3 * owners
    ids = clump_ids.reshape(1, spheres)
    vmem = pl.BlockSpec(memory_space=pltpu.VMEM)
    hbm = pl.BlockSpec(memory_space=pltpu.HBM)
    params = pltpu.CompilerParams(vmem_limit_bytes=48 * 1024 * 1024)

    keep, send = pl.pallas_call(
        loads_kernel,
        out_shape=(pltpu.VMEM((rows, clumps), f32), pltpu.VMEM((rows, clumps), f32)),
        in_specs=[pl.BlockSpec(memory_space=pltpu.SMEM)] + [hbm] * 7,
        out_specs=(vmem, vmem),
        scratch_shapes=[
            pltpu.SMEM((2, slots), jnp.int32),
            pltpu.VMEM((8, fluid), f32),
            pltpu.VMEM((7, spheres), f32),
            pltpu.VMEM((3, spheres), f32),
            pltpu.VMEM((1, spheres), jnp.int32),
            pltpu.VMEM((6, clumps), f32),
            pltpu.VMEM((4, clumps), f32),
            pltpu.SemaphoreType.DMA((7,)),
            pltpu.VMEM((3, spheres), f32),
            pltpu.VMEM((BLOCK, TILE, 3 * TILE), bf16),
            pltpu.VMEM((fluid // TILE, TILE, 3 * TILE), f32),
            pltpu.VMEM((fluid // TILE, 32, 2 * TILE), bf16),
            pltpu.VMEM((2 * TILE, TILE), bf16),
            pltpu.VMEM((16, spheres), f32),
        ],
        compiler_params=params,
        name="clump_loads",
    )(tile_count, *(
        pltpu.with_memory_space_constraint(value, pltpu.HBM)
        for value in (
            tile_list.T, fluid_state, sphere_state, sphere_offset, ids, clump_state, clump_inverse
        )
    ))

    def small(kernel, height, name, *operands, scratch=()):
        return pl.pallas_call(
            kernel,
            out_shape=pltpu.VMEM((height, clumps), f32),
            in_specs=[vmem] * len(operands),
            out_specs=vmem,
            scratch_shapes=scratch,
            compiler_params=params,
            name=name,
        )(*operands)

    mine = small(first_kernel, rows + 3, "core_sum", keep, swap(send, "sub", 1), clump_inverse)
    bits = []
    left = owners
    while left > 1:
        step = [left // 2, left // 4] if left > 2 else [1]
        left //= 2 ** len(step)
        bits += step
        others = step if len(step) == 1 else [*step, sum(step)]
        parts = [mine] + [swap(mine, "space", bit) for bit in others]
        if left > 1:
            height = rows + len(parts) * (mine.shape[0] - rows)
            mine = small(functools.partial(join_kernel, rows), height, "space_sum", *parts)
    partners = [sum(bit for n, bit in enumerate(bits) if k >> n & 1) for k in range(owners)]
    velocities = small(
        functools.partial(update_kernel, partners), rows, "clump_update", *parts,
        scratch=[pltpu.VMEM((owners, 3, clumps), f32)],
    )

    return pl.pallas_call(
        velocity_kernel,
        out_shape=(
            jax.ShapeDtypeStruct((6, clumps), f32),
            jax.ShapeDtypeStruct((3, spheres), f32),
        ),
        in_specs=[vmem] * 4,
        out_specs=(vmem, hbm),
        scratch_shapes=[
            pltpu.VMEM((owners, 6, clumps), f32),
            pltpu.VMEM((3, spheres), f32),
            pltpu.SemaphoreType.DMA((group_of(owners),)),
        ],
        compiler_params=params,
        name="sphere_velocities",
    )(velocities, swap(velocities, "sub", 1), sphere_offset, ids)


def solution(mesh):
    in_specs = (
        P(None, "space"),
        P(None, "space"),
        P(None, "space"),
        P(("space", "sub"), None),
        P(("space", "sub")),
        P("space"),
        P(None, "space"),
        P(None, "space"),
    )
    out_specs = (P(None, "space"), P(None, "space"))
    return jax.shard_map(
        per_device, mesh=mesh, in_specs=in_specs, out_specs=out_specs, check_vma=False
    )
```

```python
import functools
import math

import jax
import jax.numpy as jnp
from jax import lax
from jax.experimental import pallas as pl
from jax.experimental.pallas import tpu as pltpu
from jax.sharding import PartitionSpec as P

TILE = 128
SLOT = 256
UNROLL = 8
LANES = 16
BLOCK = TILE // LANES

support_radius = 0.5
press_coef = 4.0
visc_coef = 1.0
gravity_step = 0.1

f32 = jnp.float32
bf16 = jnp.bfloat16


def split_two(value):
    high = value.astype(bf16)
    return high, (value - high.astype(f32)).astype(bf16)


def split_three(value):
    high = value.astype(bf16).astype(f32)
    middle = (value - high).astype(bf16).astype(f32)
    return high, middle, (value - high) - middle


def cross(left, right):
    return [
        left[1] * right[2] - left[2] * right[1],
        left[2] * right[0] - left[0] * right[2],
        left[0] * right[1] - left[1] * right[0],
    ]


def group_of(owners):
    return math.gcd(owners, 16)


def loads_kernel(
    count_ref, list_hbm, fluid_hbm, sphere_hbm, offset_hbm, ids_hbm, state_hbm, inverse_hbm,
    keep_ref, send_ref,
    list_ref, fluid_ref, sphere_ref, offset_ref, ids_ref, state_ref, inverse_ref, arrived,
    place_ref, choose_ref, wide_ref, terms_ref, weight_ref, acc_ref,
):
    fluid_tiles = fluid_ref.shape[1] // TILE
    clumps = keep_ref.shape[1]
    owners = keep_ref.shape[0] // 3
    core = lax.axis_index("sub")
    me = jnp.where(core == 0, lax.axis_index("space"), -1)

    pairs = (
        (fluid_hbm, fluid_ref),
        (sphere_hbm, sphere_ref),
        (list_hbm, list_ref),
        (offset_hbm, offset_ref),
        (ids_hbm, ids_ref),
        (state_hbm, state_ref),
        (inverse_hbm, inverse_ref),
    )
    copies = [
        pltpu.make_async_copy(source, target, arrived.at[k]) for k, (source, target) in enumerate(pairs)
    ]
    for copy in copies:
        copy.start()

    acc_ref[...] = jnp.zeros_like(acc_ref)

    lane = lax.broadcasted_iota(jnp.int32, (TILE, 3 * TILE), 0)
    target = lax.broadcasted_iota(jnp.int32, (TILE, 3 * TILE), 1) // TILE
    part = lane % LANES
    wanted = (part == target) | (part == target + 3) | (part == target + 6)
    for j in range(BLOCK):
        choose_ref[j] = jnp.where(wanted & (lane // LANES == j), 1.0, 0.0).astype(bf16)
    copies[0].wait()

    @pl.loop(0, fluid_tiles // BLOCK)
    def _(block):
        row = lax.broadcasted_iota(jnp.int32, (8, TILE), 0)
        lines = []
        for j in range(BLOCK):
            tile = block * BLOCK + j
            state = fluid_ref[:, pl.ds(pl.multiple_of(tile * TILE, TILE), TILE)]
            state = jnp.where(row < 3, state * (1.0 / support_radius) - 1.0, state)
            mass = state[7:8]
            first = jnp.where(row < 7, state * mass, state)
            second = jnp.where(row < 3, state * (mass * state[6:7]), 0.0)
            high, low = split_two(jnp.concatenate([first, second], axis=0))
            both = jnp.concatenate([high, low], axis=0)
            terms_ref[tile] = jnp.concatenate([both, both], axis=1)
            lines += [*split_three(state[0:3]), jnp.zeros((LANES - 9, TILE), f32)]
        turned = jnp.concatenate(lines, axis=0).T.astype(bf16)
        for j in range(BLOCK):
            wide_ref[block * BLOCK + j] = jnp.dot(turned, choose_ref[j], preferred_element_type=f32)

    copies[1].wait()
    place_ref[...] = sphere_ref[0:3, :] * (1.0 / support_radius) - 1.0
    copies[2].wait()

    def pair_weights(slot, part):
        a = list_ref[0, slot]
        b = list_ref[1, slot]
        cols = pl.ds(pl.multiple_of(a * TILE, TILE), TILE)
        dx, dy, dz = [
            place_ref[k : k + 1, cols] - wide_ref[b, :, k * TILE : (k + 1) * TILE] for k in range(3)
        ]
        square = jnp.maximum(dx * dx + dy * dy + dz * dz, 1e-30)
        falloff = jnp.maximum(1.0 - square * lax.rsqrt(square), 0.0)
        high, low = split_two(falloff * falloff * falloff)
        weight_ref[part, 0:TILE, :] = high
        weight_ref[part, TILE:, :] = low

    def add_sums(slot, part, live):
        a = list_ref[0, slot]
        b = list_ref[1, slot]
        cols = pl.ds(pl.multiple_of(a * TILE, TILE), TILE)
        sums = jnp.dot(terms_ref[b], weight_ref[part], preferred_element_type=f32)
        acc_ref[:, cols] += live * (sums[0:16] + sums[16:32])

    count = count_ref[0]
    trips = (count + UNROLL - 1) // UNROLL
    last = list_ref.shape[1] - 1

    for part in range(UNROLL):
        pair_weights(min(part, last), part)

    @pl.loop(1, trips)
    def _(trip):
        for part in range(UNROLL):
            add_sums((trip - 1) * UNROLL + part, part, 1.0)
        for part in range(UNROLL):
            pair_weights(jnp.minimum(trip * UNROLL + part, last), part)

    for part in range(UNROLL):
        slot = (trips - 1) * UNROLL + part
        live = jnp.where(slot < count, 1.0, 0.0).astype(f32)
        add_sums(jnp.clip(slot, 0, last), part, live)

    for copy in copies[3:]:
        copy.wait()
    group = group_of(owners)
    width = group * SLOT

    row = lax.broadcasted_iota(jnp.int32, state_ref.shape, 0)
    still = state_ref[...] + jnp.where(row == 2, -gravity_step, 0.0)
    still = still / jnp.concatenate([inverse_ref[0:1, :]] * 3 + [inverse_ref[1:4, :]], axis=0)

    @pl.loop(0, owners // group)
    def _(block):
        cols = pl.ds(pl.multiple_of(block * width, width), width)
        acc = acc_ref[:, cols]
        place = place_ref[:, cols]
        sphere = sphere_ref[:, cols]
        offset = offset_ref[:, cols]
        total = acc[7:8]
        pull = total * place - acc[0:3]
        press = acc[6:7] * place - acc[8:11]
        scale = press_coef * support_radius
        force = scale * (sphere[6:7] * pull + press) + visc_coef * (acc[3:6] - total * sphere[3:6])
        force = [force[k : k + 1] for k in range(3)]
        turn = cross([offset[k : k + 1] for k in range(3)], force)
        loads = jnp.concatenate(force + turn + [jnp.zeros_like(force[0])] * 2, axis=0)
        high, low = split_two(loads)
        both = jnp.concatenate([high, low], axis=0)
        column = lax.broadcasted_iota(jnp.int32, (clumps, SLOT), 0)
        keep, send = [], []
        for k in range(group):
            here = pl.ds(pl.multiple_of(block * width + k * SLOT, SLOT), SLOT)
            one_hot = jnp.where(column == ids_ref[:, here], 1.0, 0.0).astype(bf16)
            sums = lax.dot_general(
                both[:, k * SLOT : (k + 1) * SLOT], one_hot, (((1,), (1,)), ((), ())),
                preferred_element_type=f32,
            )
            own = jnp.where(block * group + k == me, 1.0, 0.0).astype(f32)
            sums = (sums[0:8] + sums[8:16])[0:6] + own * still
            keep.append(jnp.where(core == 0, sums[0:3], sums[3:6]))
            send.append(jnp.where(core == 0, sums[3:6], sums[0:3]))
        here = pl.ds(pl.multiple_of(block * (3 * group), math.gcd(3 * group, 8)), 3 * group)
        keep_ref[here, :] = jnp.concatenate(keep, axis=0)
        send_ref[here, :] = jnp.concatenate(send, axis=0)


def first_kernel(keep_ref, arrived_ref, inverse_ref, out_ref):
    rows = keep_ref.shape[0]
    out_ref[0:rows, :] = keep_ref[...] + arrived_ref[...]
    linear = jnp.concatenate([inverse_ref[0:1, :]] * 3, axis=0)
    out_ref[rows:, :] = jnp.where(lax.axis_index("sub") == 0, linear, inverse_ref[1:4, :])


def sum_rows(parts, rows):
    return functools.reduce(lambda total, part: total + part, [part[0:rows, :] for part in parts])


def join_kernel(rows, parts_ref, out_ref):
    parts = [parts_ref.at[k] for k in range(parts_ref.shape[0])]
    more = parts_ref.shape[1] - rows
    out_ref[0:rows, :] = sum_rows(parts, rows)
    for k, part in enumerate(parts):
        out_ref[rows + k * more : rows + (k + 1) * more, :] = part[rows:, :]


def update_kernel(holders, parts_ref, out_ref, inverse_ref):
    parts = [parts_ref.at[k] for k in range(parts_ref.shape[0])]
    owners = len(holders)
    rows = 3 * owners
    held = owners // len(parts)
    for k, owner in enumerate(holders):
        first = rows + 3 * (k % held)
        inverse_ref[owner] = parts[k // held][first : first + 3, :]
    out_ref[...] = sum_rows(parts, rows) * jnp.concatenate([inverse_ref[k] for k in range(owners)], axis=0)


def velocity_kernel(mine_ref, arrived_ref, offset_ref, ids_ref, clump_ref, sphere_ref, velocity_ref):
    owners, _, clumps = velocity_ref.shape
    group = group_of(owners)
    core = lax.axis_index("sub")

    @pl.loop(0, owners // group)
    def _(block):
        rows = pl.ds(pl.multiple_of(block * (3 * group), math.gcd(3 * group, 8)), 3 * group)
        mine = mine_ref[rows, :]
        arrived = arrived_ref[rows, :]
        linear = jnp.where(core == 0, mine, arrived)
        angular = jnp.where(core == 0, arrived, mine)
        for k in range(group):
            owner = block * group + k
            three = slice(3 * k, 3 * k + 3)
            velocity = jnp.concatenate([linear[three], angular[three]], axis=0)
            velocity_ref[owner] = velocity
            both = jnp.concatenate(
                split_two(jnp.concatenate([velocity, jnp.zeros((2, clumps), f32)], axis=0)), axis=0
            )
            here = pl.ds(pl.multiple_of(owner * SLOT, SLOT), SLOT)
            column = lax.broadcasted_iota(jnp.int32, (clumps, SLOT), 0)
            one_hot = jnp.where(column == ids_ref[:, here], 1.0, 0.0).astype(bf16)
            picked = jnp.dot(both, one_hot, preferred_element_type=f32)
            picked = picked[0:8] + picked[8:16]
            offset = offset_ref[:, here]
            turn = cross([picked[3 + i : 4 + i] for i in range(3)], [offset[i : i + 1] for i in range(3)])
            sphere_ref[:, here] = picked[0:3] + jnp.concatenate(turn, axis=0)

    clump_ref[...] = velocity_ref[lax.axis_index("space")]


def swap(value, axis, bit):
    size = lax.axis_size(axis)
    return lax.ppermute(value, axis, [(k, k ^ bit) for k in range(size)])


def per_device(
    fluid_state, sphere_state, sphere_offset, tile_list, tile_count, clump_ids, clump_state, clump_inverse
):
    owners = lax.axis_size("space")
    spheres = sphere_state.shape[1]
    fluid = fluid_state.shape[1]
    clumps = clump_state.shape[1]
    slots = tile_list.shape[0]
    rows = 3 * owners
    ids = clump_ids.reshape(1, spheres)
    vmem = pl.BlockSpec(memory_space=pltpu.VMEM)
    hbm = pl.BlockSpec(memory_space=pltpu.HBM)
    params = pltpu.CompilerParams(vmem_limit_bytes=48 * 1024 * 1024)

    keep, send = pl.pallas_call(
        loads_kernel,
        out_shape=(pltpu.VMEM((rows, clumps), f32), pltpu.VMEM((rows, clumps), f32)),
        in_specs=[pl.BlockSpec(memory_space=pltpu.SMEM)] + [hbm] * 7,
        out_specs=(vmem, vmem),
        scratch_shapes=[
            pltpu.SMEM((2, slots), jnp.int32),
            pltpu.VMEM((8, fluid), f32),
            pltpu.VMEM((7, spheres), f32),
            pltpu.VMEM((3, spheres), f32),
            pltpu.VMEM((1, spheres), jnp.int32),
            pltpu.VMEM((6, clumps), f32),
            pltpu.VMEM((4, clumps), f32),
            pltpu.SemaphoreType.DMA((7,)),
            pltpu.VMEM((3, spheres), f32),
            pltpu.VMEM((BLOCK, TILE, 3 * TILE), bf16),
            pltpu.VMEM((fluid // TILE, TILE, 3 * TILE), f32),
            pltpu.VMEM((fluid // TILE, 32, 2 * TILE), bf16),
            pltpu.VMEM((UNROLL, 2 * TILE, TILE), bf16),
            pltpu.VMEM((16, spheres), f32),
        ],
        compiler_params=params,
        name="clump_loads",
    )(tile_count, *(
        pltpu.with_memory_space_constraint(value, pltpu.HBM)
        for value in (
            tile_list.T, fluid_state, sphere_state, sphere_offset, ids, clump_state, clump_inverse
        )
    ))

    def small(kernel, height, name, *operands, scratch=()):
        return pl.pallas_call(
            kernel,
            out_shape=pltpu.VMEM((height, clumps), f32),
            in_specs=[vmem] * len(operands),
            out_specs=vmem,
            scratch_shapes=scratch,
            compiler_params=params,
            name=name,
        )(*operands)

    mine = small(first_kernel, rows + 3, "core_sum", keep, swap(send, "sub", 1), clump_inverse)
    holders = [0]
    stride = owners
    while stride > 1:
        count = math.gcd(stride, 4)
        stride //= count
        groups = [
            [first + k * stride for k in range(count)]
            for first in range(owners)
            if first // stride % count == 0
        ]
        copies = jnp.broadcast_to(mine[None], (count, *mine.shape))
        parts = lax.all_to_all(
            copies, "space", split_axis=0, concat_axis=0, axis_index_groups=groups, tiled=True
        )
        holders = [owner + k * stride for k in range(count) for owner in holders]
        if stride > 1:
            height = rows + count * (mine.shape[0] - rows)
            mine = small(functools.partial(join_kernel, rows), height, "space_sum", parts)
    velocities = small(
        functools.partial(update_kernel, holders), rows, "clump_update", parts,
        scratch=[pltpu.VMEM((owners, 3, clumps), f32)],
    )

    return pl.pallas_call(
        velocity_kernel,
        out_shape=(
            jax.ShapeDtypeStruct((6, clumps), f32),
            jax.ShapeDtypeStruct((3, spheres), f32),
        ),
        in_specs=[vmem] * 4,
        out_specs=(vmem, vmem),
        scratch_shapes=[pltpu.VMEM((owners, 6, clumps), f32)],
        compiler_params=params,
        name="sphere_velocities",
    )(velocities, swap(velocities, "sub", 1), sphere_offset, ids)


def solution(mesh):
    in_specs = (
        P(None, "space"),
        P(None, "space"),
        P(None, "space"),
        P(("space", "sub"), None),
        P(("space", "sub")),
        P("space"),
        P(None, "space"),
        P(None, "space"),
    )
    out_specs = (P(None, "space"), P(None, "space"))
    return jax.shard_map(
        per_device, mesh=mesh, in_specs=in_specs, out_specs=out_specs, check_vma=False
    )
```

```python
import functools
import math

import jax
import jax.numpy as jnp
from jax import lax
from jax.experimental import pallas as pl
from jax.experimental.pallas import tpu as pltpu
from jax.sharding import PartitionSpec as P

TILE = 128
SLOT = 256
UNROLL = 8
FIRST_MOVES = ((1, 0, 3, 2), (3, 2, 0, 1), (2, 3, 1, 0))
OTHER_MOVES = ((2, 3, 0, 1), (3, 0, 1, 2), (1, 2, 3, 0))
LANES = 16
BLOCK = TILE // LANES

support_radius = 0.5
press_coef = 4.0
visc_coef = 1.0
gravity_step = 0.1

f32 = jnp.float32
bf16 = jnp.bfloat16


def split_two(value):
    high = value.astype(bf16)
    return high, (value - high.astype(f32)).astype(bf16)


def split_three(value):
    high = value.astype(bf16).astype(f32)
    middle = (value - high).astype(bf16).astype(f32)
    return high, middle, (value - high) - middle


def cross(left, right):
    return [
        left[1] * right[2] - left[2] * right[1],
        left[2] * right[0] - left[0] * right[2],
        left[0] * right[1] - left[1] * right[0],
    ]


def group_of(owners):
    return math.gcd(owners, 16)


def loads_kernel(
    count_ref, list_hbm, fluid_hbm, sphere_hbm, offset_hbm, ids_hbm, state_hbm, inverse_hbm,
    keep_ref, send_ref,
    list_ref, fluid_ref, sphere_ref, offset_ref, ids_ref, state_ref, inverse_ref, arrived,
    place_ref, choose_ref, wide_ref, terms_ref, weight_ref, acc_ref,
):
    fluid_tiles = fluid_ref.shape[1] // TILE
    clumps = keep_ref.shape[1]
    owners = keep_ref.shape[0] // 3
    core = lax.axis_index("sub")
    me = jnp.where(core == 0, lax.axis_index("space"), -1)

    pairs = (
        (fluid_hbm, fluid_ref),
        (sphere_hbm, sphere_ref),
        (list_hbm, list_ref),
        (offset_hbm, offset_ref),
        (ids_hbm, ids_ref),
        (state_hbm, state_ref),
        (inverse_hbm, inverse_ref),
    )
    copies = [
        pltpu.make_async_copy(source, target, arrived.at[k]) for k, (source, target) in enumerate(pairs)
    ]
    for copy in copies:
        copy.start()

    acc_ref[...] = jnp.zeros_like(acc_ref)

    lane = lax.broadcasted_iota(jnp.int32, (TILE, 2 * TILE), 0)
    target = lax.broadcasted_iota(jnp.int32, (TILE, 2 * TILE), 1) // TILE
    part = lane % LANES
    wanted = (part == target) | (part == target + 3) | (part == target + 6)
    for j in range(BLOCK):
        choose_ref[j] = jnp.where(wanted & (lane // LANES == j), 1.0, 0.0).astype(bf16)
    copies[0].wait()

    @pl.loop(0, fluid_tiles // BLOCK)
    def _(block):
        row = lax.broadcasted_iota(jnp.int32, (8, TILE), 0)
        lines = []
        for j in range(BLOCK):
            tile = block * BLOCK + j
            state = fluid_ref[:, pl.ds(pl.multiple_of(tile * TILE, TILE), TILE)]
            state = jnp.where(row < 3, state * (1.0 / support_radius) - 1.0, state)
            mass = state[7:8]
            first = jnp.where(row < 7, state * mass, state)
            second = jnp.where(row < 3, state * (mass * state[6:7]), 0.0)
            high, low = split_two(jnp.concatenate([first, second], axis=0))
            both = jnp.concatenate([high, low], axis=0)
            terms_ref[tile] = jnp.concatenate([both, both], axis=1)
            lines += [*split_three(state[0:3]), state[0:3], jnp.zeros((LANES - 12, TILE), f32)]
        turned = jnp.concatenate(lines, axis=0).T
        parts = turned.astype(bf16)
        for j in range(BLOCK):
            tile = block * BLOCK + j
            z = j * LANES + 11
            wide_ref[tile, :, 0 : 2 * TILE] = jnp.dot(parts, choose_ref[j], preferred_element_type=f32)
            wide_ref[tile, :, 2 * TILE :] = jnp.broadcast_to(turned[:, z : z + 1], (TILE, TILE))

    copies[1].wait()
    place_ref[...] = sphere_ref[0:3, :] * (1.0 / support_radius) - 1.0
    copies[2].wait()

    def pair_weights(slot, part):
        a = list_ref[0, slot]
        b = list_ref[1, slot]
        cols = pl.ds(pl.multiple_of(a * TILE, TILE), TILE)
        dx, dy, dz = [
            place_ref[k : k + 1, cols] - wide_ref[b, :, k * TILE : (k + 1) * TILE] for k in range(3)
        ]
        square = jnp.maximum(dx * dx + dy * dy + dz * dz, 1e-30)
        falloff = jnp.maximum(1.0 - square * lax.rsqrt(square), 0.0)
        high, low = split_two(falloff * falloff * falloff)
        weight_ref[part, 0:TILE, :] = high
        weight_ref[part, TILE:, :] = low

    def add_sums(slot, part, live):
        a = list_ref[0, slot]
        b = list_ref[1, slot]
        cols = pl.ds(pl.multiple_of(a * TILE, TILE), TILE)
        sums = jnp.dot(terms_ref[b], weight_ref[part], preferred_element_type=f32)
        acc_ref[:, cols] += live * (sums[0:16] + sums[16:32])

    count = count_ref[0]
    trips = (count + UNROLL - 1) // UNROLL
    last = list_ref.shape[1] - 1

    for part in range(UNROLL):
        pair_weights(min(part, last), part)

    @pl.loop(1, trips)
    def _(trip):
        for part in range(UNROLL):
            add_sums((trip - 1) * UNROLL + part, part, 1.0)
        for part in range(UNROLL):
            pair_weights(jnp.minimum(trip * UNROLL + part, last), part)

    for part in range(UNROLL):
        slot = (trips - 1) * UNROLL + part
        live = jnp.where(slot < count, 1.0, 0.0).astype(f32)
        add_sums(jnp.clip(slot, 0, last), part, live)

    for copy in copies[3:]:
        copy.wait()
    group = group_of(owners)
    width = group * SLOT

    row = lax.broadcasted_iota(jnp.int32, state_ref.shape, 0)
    still = state_ref[...] + jnp.where(row == 2, -gravity_step, 0.0)
    still = still / jnp.concatenate([inverse_ref[0:1, :]] * 3 + [inverse_ref[1:4, :]], axis=0)

    @pl.loop(0, owners // group)
    def _(block):
        cols = pl.ds(pl.multiple_of(block * width, width), width)
        acc = acc_ref[:, cols]
        place = place_ref[:, cols]
        sphere = sphere_ref[:, cols]
        offset = offset_ref[:, cols]
        total = acc[7:8]
        pull = total * place - acc[0:3]
        press = acc[6:7] * place - acc[8:11]
        scale = press_coef * support_radius
        force = scale * (sphere[6:7] * pull + press) + visc_coef * (acc[3:6] - total * sphere[3:6])
        force = [force[k : k + 1] for k in range(3)]
        turn = cross([offset[k : k + 1] for k in range(3)], force)
        loads = jnp.concatenate(force + turn + [jnp.zeros_like(force[0])] * 2, axis=0)
        high, low = split_two(loads)
        both = jnp.concatenate([high, low], axis=0)
        column = lax.broadcasted_iota(jnp.int32, (clumps, SLOT), 0)
        keep, send = [], []
        for k in range(group):
            here = pl.ds(pl.multiple_of(block * width + k * SLOT, SLOT), SLOT)
            one_hot = jnp.where(column == ids_ref[:, here], 1.0, 0.0).astype(bf16)
            sums = lax.dot_general(
                both[:, k * SLOT : (k + 1) * SLOT], one_hot, (((1,), (1,)), ((), ())),
                preferred_element_type=f32,
            )
            own = jnp.where(block * group + k == me, 1.0, 0.0).astype(f32)
            sums = (sums[0:8] + sums[8:16])[0:6] + own * still
            keep.append(jnp.where(core == 0, sums[0:3], sums[3:6]))
            send.append(jnp.where(core == 0, sums[3:6], sums[0:3]))
        here = pl.ds(pl.multiple_of(block * (3 * group), math.gcd(3 * group, 8)), 3 * group)
        keep_ref[here, :] = jnp.concatenate(keep, axis=0)
        send_ref[here, :] = jnp.concatenate(send, axis=0)


def first_kernel(keep_ref, arrived_ref, inverse_ref, out_ref):
    rows = keep_ref.shape[0]
    out_ref[0:rows, :] = keep_ref[...] + arrived_ref[...]
    linear = jnp.concatenate([inverse_ref[0:1, :]] * 3, axis=0)
    out_ref[rows:, :] = jnp.where(lax.axis_index("sub") == 0, linear, inverse_ref[1:4, :])


def sum_rows(refs, rows):
    sums = [ref[0:rows, :] for ref in refs]
    while len(sums) > 1:
        sums = [left + right for left, right in zip(sums[0::2], sums[1::2])]
    return sums[0]


def join_kernel(rows, *refs):
    *parts, out_ref = refs
    more = parts[0].shape[0] - rows
    out_ref[0:rows, :] = sum_rows(parts, rows)
    for k, ref in enumerate(parts):
        out_ref[rows + k * more : rows + (k + 1) * more, :] = ref[rows:, :]


def update_kernel(steps, *refs):
    *parts, out_ref, inverse_ref = refs
    owners = inverse_ref.shape[0]
    rows = 3 * owners
    held = owners // len(parts)
    me = lax.axis_index("space")
    holders = [0]
    for stride, moves in steps:
        radix = len(moves[0])
        here = me // stride % radix
        sources = [here]
        for move in moves:
            sources.append(sum(jnp.where(here == at, move.index(at), 0) for at in range(radix)))
        holders = [holder + source * stride for source in sources for holder in holders]
    for k, holder in enumerate(holders):
        first = rows + 3 * (k % held)
        inverse_ref[holder] = parts[k // held][first : first + 3, :]
    out_ref[...] = sum_rows(parts, rows) * jnp.concatenate([inverse_ref[k] for k in range(owners)], axis=0)


def velocity_kernel(mine_ref, arrived_ref, offset_ref, ids_ref, clump_ref, sphere_ref, velocity_ref):
    owners, _, clumps = velocity_ref.shape
    group = group_of(owners)
    core = lax.axis_index("sub")

    @pl.loop(0, owners // group)
    def _(block):
        rows = pl.ds(pl.multiple_of(block * (3 * group), math.gcd(3 * group, 8)), 3 * group)
        mine = mine_ref[rows, :]
        arrived = arrived_ref[rows, :]
        linear = jnp.where(core == 0, mine, arrived)
        angular = jnp.where(core == 0, arrived, mine)
        for k in range(group):
            owner = block * group + k
            three = slice(3 * k, 3 * k + 3)
            velocity = jnp.concatenate([linear[three], angular[three]], axis=0)
            velocity_ref[owner] = velocity
            both = jnp.concatenate(
                split_two(jnp.concatenate([velocity, jnp.zeros((2, clumps), f32)], axis=0)), axis=0
            )
            here = pl.ds(pl.multiple_of(owner * SLOT, SLOT), SLOT)
            column = lax.broadcasted_iota(jnp.int32, (clumps, SLOT), 0)
            one_hot = jnp.where(column == ids_ref[:, here], 1.0, 0.0).astype(bf16)
            picked = jnp.dot(both, one_hot, preferred_element_type=f32)
            picked = picked[0:8] + picked[8:16]
            offset = offset_ref[:, here]
            turn = cross([picked[3 + i : 4 + i] for i in range(3)], [offset[i : i + 1] for i in range(3)])
            sphere_ref[:, here] = picked[0:3] + jnp.concatenate(turn, axis=0)

    clump_ref[...] = velocity_ref[lax.axis_index("space")]


def swap_cores(value):
    return lax.ppermute(value, "sub", [(0, 1), (1, 0)])


def send(value, stride, move):
    pairs = []
    for chip in range(lax.axis_size("space")):
        digit = chip // stride % len(move)
        pairs.append((chip, chip + (move[digit] - digit) * stride))
    return lax.ppermute(value, "space", pairs)


def steps_of(owners):
    steps, stride = [], owners
    while stride > 1:
        radix = math.gcd(stride, 4)
        stride //= radix
        steps.append((stride, ((1, 0),) if radix == 2 else OTHER_MOVES if steps else FIRST_MOVES))
    return steps


def per_device(
    fluid_state, sphere_state, sphere_offset, tile_list, tile_count, clump_ids, clump_state, clump_inverse
):
    owners = lax.axis_size("space")
    spheres = sphere_state.shape[1]
    fluid = fluid_state.shape[1]
    clumps = clump_state.shape[1]
    slots = tile_list.shape[0]
    rows = 3 * owners
    ids = clump_ids.reshape(1, spheres)
    vmem = pl.BlockSpec(memory_space=pltpu.VMEM)
    hbm = pl.BlockSpec(memory_space=pltpu.HBM)
    params = pltpu.CompilerParams(vmem_limit_bytes=48 * 1024 * 1024)

    keep, give = pl.pallas_call(
        loads_kernel,
        out_shape=(pltpu.VMEM((rows, clumps), f32), pltpu.VMEM((rows, clumps), f32)),
        in_specs=[pl.BlockSpec(memory_space=pltpu.SMEM)] + [hbm] * 7,
        out_specs=(vmem, vmem),
        scratch_shapes=[
            pltpu.SMEM((2, slots), jnp.int32),
            pltpu.VMEM((8, fluid), f32),
            pltpu.VMEM((7, spheres), f32),
            pltpu.VMEM((3, spheres), f32),
            pltpu.VMEM((1, spheres), jnp.int32),
            pltpu.VMEM((6, clumps), f32),
            pltpu.VMEM((4, clumps), f32),
            pltpu.SemaphoreType.DMA((7,)),
            pltpu.VMEM((3, spheres), f32),
            pltpu.VMEM((BLOCK, TILE, 2 * TILE), bf16),
            pltpu.VMEM((fluid // TILE, TILE, 3 * TILE), f32),
            pltpu.VMEM((fluid // TILE, 32, 2 * TILE), bf16),
            pltpu.VMEM((UNROLL, 2 * TILE, TILE), bf16),
            pltpu.VMEM((16, spheres), f32),
        ],
        compiler_params=params,
        name="clump_loads",
    )(tile_count, *(
        pltpu.with_memory_space_constraint(value, pltpu.HBM)
        for value in (
            tile_list.T, fluid_state, sphere_state, sphere_offset, ids, clump_state, clump_inverse
        )
    ))

    def small(kernel, height, name, *operands, scratch=()):
        return pl.pallas_call(
            kernel,
            out_shape=pltpu.VMEM((height, clumps), f32),
            in_specs=[vmem] * len(operands),
            out_specs=vmem,
            scratch_shapes=scratch,
            compiler_params=params,
            name=name,
        )(*operands)

    mine = small(first_kernel, rows + 3, "core_sum", keep, swap_cores(give), clump_inverse)
    steps = steps_of(owners)
    for stride, moves in steps:
        parts = [mine] + [send(mine, stride, move) for move in moves]
        if stride > 1:
            height = rows + len(parts) * (mine.shape[0] - rows)
            mine = small(functools.partial(join_kernel, rows), height, "space_sum", *parts)
    velocities = small(
        functools.partial(update_kernel, steps), rows, "clump_update", *parts,
        scratch=[pltpu.VMEM((owners, 3, clumps), f32)],
    )

    return pl.pallas_call(
        velocity_kernel,
        out_shape=(
            jax.ShapeDtypeStruct((6, clumps), f32),
            jax.ShapeDtypeStruct((3, spheres), f32),
        ),
        in_specs=[vmem] * 4,
        out_specs=(vmem, vmem),
        scratch_shapes=[pltpu.VMEM((owners, 6, clumps), f32)],
        compiler_params=params,
        name="sphere_velocities",
    )(velocities, swap_cores(velocities), sphere_offset, ids)


def solution(mesh):
    in_specs = (
        P(None, "space"),
        P(None, "space"),
        P(None, "space"),
        P(("space", "sub"), None),
        P(("space", "sub")),
        P("space"),
        P(None, "space"),
        P(None, "space"),
    )
    out_specs = (P(None, "space"), P(None, "space"))
    return jax.shard_map(
        per_device, mesh=mesh, in_specs=in_specs, out_specs=out_specs, check_vma=False
    )
```

```python
import functools
import math

import jax
import jax.numpy as jnp
from jax import lax
from jax.experimental import pallas as pl
from jax.experimental.pallas import tpu as pltpu
from jax.sharding import PartitionSpec as P

TILE = 128
SLOT = 256
UNROLL = 8
FIRST_MOVES = ((1, 0, 3, 2), (3, 2, 0, 1), (2, 3, 1, 0))
OTHER_MOVES = ((2, 3, 0, 1), (3, 0, 1, 2), (1, 2, 3, 0))
LANES = 16
BLOCK = TILE // LANES

support_radius = 0.5
press_coef = 4.0
visc_coef = 1.0
gravity_step = 0.1

f32 = jnp.float32
bf16 = jnp.bfloat16


def split_two(value):
    high = value.astype(bf16)
    return high, (value - high.astype(f32)).astype(bf16)


def split_three(value):
    high = value.astype(bf16).astype(f32)
    middle = (value - high).astype(bf16).astype(f32)
    return high, middle, (value - high) - middle


def cross(left, right):
    return [
        left[1] * right[2] - left[2] * right[1],
        left[2] * right[0] - left[0] * right[2],
        left[0] * right[1] - left[1] * right[0],
    ]


def group_of(owners):
    return math.gcd(owners, 8)


def loads_kernel(
    count_ref, list_hbm, fluid_hbm, sphere_hbm, offset_hbm, ids_hbm, state_hbm, inverse_hbm,
    keep_ref, send_ref,
    list_ref, fluid_ref, sphere_ref, offset_ref, ids_ref, state_ref, inverse_ref, arrived,
    place_ref, choose_ref, wide_ref, terms_ref, weight_ref, acc_ref,
):
    fluid_tiles = fluid_ref.shape[1] // TILE
    clumps = keep_ref.shape[1]
    owners = keep_ref.shape[0] // 3
    core = lax.axis_index("sub")
    me = jnp.where(core == 0, lax.axis_index("space"), -1)

    pairs = (
        (fluid_hbm, fluid_ref),
        (sphere_hbm, sphere_ref),
        (list_hbm, list_ref),
        (offset_hbm, offset_ref),
        (ids_hbm, ids_ref),
        (state_hbm, state_ref),
        (inverse_hbm, inverse_ref),
    )
    copies = [
        pltpu.make_async_copy(source, target, arrived.at[k]) for k, (source, target) in enumerate(pairs)
    ]
    for copy in copies:
        copy.start()

    acc_ref[...] = jnp.zeros_like(acc_ref)

    lane = lax.broadcasted_iota(jnp.int32, (TILE, 2 * TILE), 0)
    target = lax.broadcasted_iota(jnp.int32, (TILE, 2 * TILE), 1) // TILE
    part = lane % LANES
    wanted = (part == target) | (part == target + 3) | (part == target + 6)
    for j in range(BLOCK):
        choose_ref[j] = jnp.where(wanted & (lane // LANES == j), 1.0, 0.0).astype(bf16)
    copies[0].wait()

    @pl.loop(0, fluid_tiles // BLOCK)
    def _(block):
        row = lax.broadcasted_iota(jnp.int32, (8, TILE), 0)
        lines = []
        for j in range(BLOCK):
            tile = block * BLOCK + j
            state = fluid_ref[:, pl.ds(pl.multiple_of(tile * TILE, TILE), TILE)]
            state = jnp.where(row < 3, state * (1.0 / support_radius) - 1.0, state)
            mass = state[7:8]
            first = jnp.where(row < 7, state * mass, state)
            second = jnp.where(row < 3, state * (mass * state[6:7]), 0.0)
            high, low = split_two(jnp.concatenate([first, second], axis=0))
            both = jnp.concatenate([high, low], axis=0)
            terms_ref[tile] = jnp.concatenate([both, both], axis=1)
            lines += [*split_three(state[0:3]), state[0:3], jnp.zeros((LANES - 12, TILE), f32)]
        turned = jnp.concatenate(lines, axis=0).T
        parts = turned.astype(bf16)
        for j in range(BLOCK):
            tile = block * BLOCK + j
            z = j * LANES + 11
            wide_ref[tile, :, 0 : 2 * TILE] = jnp.dot(parts, choose_ref[j], preferred_element_type=f32)
            wide_ref[tile, :, 2 * TILE :] = jnp.broadcast_to(turned[:, z : z + 1], (TILE, TILE))

    copies[1].wait()
    place_ref[...] = sphere_ref[0:3, :] * (1.0 / support_radius) - 1.0
    copies[2].wait()

    def pair_weights(slot, part):
        a = list_ref[0, slot]
        b = list_ref[1, slot]
        cols = pl.ds(pl.multiple_of(a * TILE, TILE), TILE)
        dx, dy, dz = [
            place_ref[k : k + 1, cols] - wide_ref[b, :, k * TILE : (k + 1) * TILE] for k in range(3)
        ]
        square = jnp.maximum(dx * dx + dy * dy + dz * dz, 1e-30)
        falloff = jnp.maximum(1.0 - square * lax.rsqrt(square), 0.0)
        high, low = split_two(falloff * falloff * falloff)
        weight_ref[part, 0:TILE, :] = high
        weight_ref[part, TILE:, :] = low

    def add_sums(slot, part, live):
        a = list_ref[0, slot]
        b = list_ref[1, slot]
        cols = pl.ds(pl.multiple_of(a * TILE, TILE), TILE)
        sums = jnp.dot(terms_ref[b], weight_ref[part], preferred_element_type=f32)
        acc_ref[:, cols] += live * (sums[0:16] + sums[16:32])

    count = count_ref[0]
    trips = (count + UNROLL - 1) // UNROLL
    last = list_ref.shape[1] - 1

    for part in range(UNROLL):
        pair_weights(min(part, last), part)

    @pl.loop(1, trips)
    def _(trip):
        for part in range(UNROLL):
            add_sums((trip - 1) * UNROLL + part, part, 1.0)
        for part in range(UNROLL):
            pair_weights(jnp.minimum(trip * UNROLL + part, last), part)

    for part in range(UNROLL):
        slot = (trips - 1) * UNROLL + part
        live = jnp.where(slot < count, 1.0, 0.0).astype(f32)
        add_sums(jnp.clip(slot, 0, last), part, live)

    for copy in copies[3:]:
        copy.wait()
    group = group_of(owners)
    width = group * SLOT

    row = lax.broadcasted_iota(jnp.int32, state_ref.shape, 0)
    still = state_ref[...] + jnp.where(row == 2, -gravity_step, 0.0)
    still = still / jnp.concatenate([inverse_ref[0:1, :]] * 3 + [inverse_ref[1:4, :]], axis=0)

    @pl.loop(0, owners // group)
    def _(block):
        cols = pl.ds(pl.multiple_of(block * width, width), width)
        acc = acc_ref[:, cols]
        place = place_ref[:, cols]
        sphere = sphere_ref[:, cols]
        offset = offset_ref[:, cols]
        total = acc[7:8]
        pull = total * place - acc[0:3]
        press = acc[6:7] * place - acc[8:11]
        scale = press_coef * support_radius
        force = scale * (sphere[6:7] * pull + press) + visc_coef * (acc[3:6] - total * sphere[3:6])
        force = [force[k : k + 1] for k in range(3)]
        turn = cross([offset[k : k + 1] for k in range(3)], force)
        loads = jnp.concatenate(force + turn + [jnp.zeros_like(force[0])] * 2, axis=0)
        high, low = split_two(loads)
        both = jnp.concatenate([high, low], axis=0)
        column = lax.broadcasted_iota(jnp.int32, (clumps, SLOT), 0)
        keep, send = [], []
        for k in range(group):
            here = pl.ds(pl.multiple_of(block * width + k * SLOT, SLOT), SLOT)
            one_hot = jnp.where(column == ids_ref[:, here], 1.0, 0.0).astype(bf16)
            sums = lax.dot_general(
                both[:, k * SLOT : (k + 1) * SLOT], one_hot, (((1,), (1,)), ((), ())),
                preferred_element_type=f32,
            )
            own = jnp.where(block * group + k == me, 1.0, 0.0).astype(f32)
            sums = (sums[0:8] + sums[8:16])[0:6] + own * still
            keep.append(jnp.where(core == 0, sums[0:3], sums[3:6]))
            send.append(jnp.where(core == 0, sums[3:6], sums[0:3]))
        here = pl.ds(pl.multiple_of(block * (3 * group), math.gcd(3 * group, 8)), 3 * group)
        keep_ref[here, :] = jnp.concatenate(keep, axis=0)
        send_ref[here, :] = jnp.concatenate(send, axis=0)


def first_kernel(keep_ref, arrived_ref, inverse_ref, out_ref):
    rows = keep_ref.shape[0]
    out_ref[0:rows, :] = keep_ref[...] + arrived_ref[...]
    linear = jnp.concatenate([inverse_ref[0:1, :]] * 3, axis=0)
    out_ref[rows:, :] = jnp.where(lax.axis_index("sub") == 0, linear, inverse_ref[1:4, :])


def sum_rows(refs, rows):
    sums = [ref[0:rows, :] for ref in refs]
    while len(sums) > 1:
        sums = [left + right for left, right in zip(sums[0::2], sums[1::2])]
    return sums[0]


def join_kernel(rows, *refs):
    *parts, out_ref = refs
    more = parts[0].shape[0] - rows
    out_ref[0:rows, :] = sum_rows(parts, rows)
    for k, ref in enumerate(parts):
        out_ref[rows + k * more : rows + (k + 1) * more, :] = ref[rows:, :]


def update_kernel(steps, *refs):
    *parts, out_ref, inverse_ref = refs
    owners = inverse_ref.shape[0]
    rows = 3 * owners
    held = owners // len(parts)
    me = lax.axis_index("space")
    holders = [0]
    for stride, moves in steps:
        radix = len(moves[0])
        here = me // stride % radix
        sources = [here]
        for move in moves:
            sources.append(sum(jnp.where(here == at, move.index(at), 0) for at in range(radix)))
        holders = [holder + source * stride for source in sources for holder in holders]
    for k, holder in enumerate(holders):
        first = rows + 3 * (k % held)
        inverse_ref[holder] = parts[k // held][first : first + 3, :]
    out_ref[...] = sum_rows(parts, rows) * jnp.concatenate([inverse_ref[k] for k in range(owners)], axis=0)


def velocity_kernel(mine_ref, arrived_ref, offset_ref, ids_ref, clump_ref, sphere_ref, velocity_ref):
    owners, _, clumps = velocity_ref.shape
    group = group_of(owners)
    core = lax.axis_index("sub")

    @pl.loop(0, owners // group)
    def _(block):
        rows = pl.ds(pl.multiple_of(block * (3 * group), math.gcd(3 * group, 8)), 3 * group)
        mine = mine_ref[rows, :]
        arrived = arrived_ref[rows, :]
        linear = jnp.where(core == 0, mine, arrived)
        angular = jnp.where(core == 0, arrived, mine)
        for k in range(group):
            owner = block * group + k
            three = slice(3 * k, 3 * k + 3)
            velocity = jnp.concatenate([linear[three], angular[three]], axis=0)
            velocity_ref[owner] = velocity
            both = jnp.concatenate(
                split_two(jnp.concatenate([velocity, jnp.zeros((2, clumps), f32)], axis=0)), axis=0
            )
            here = pl.ds(pl.multiple_of(owner * SLOT, SLOT), SLOT)
            column = lax.broadcasted_iota(jnp.int32, (clumps, SLOT), 0)
            one_hot = jnp.where(column == ids_ref[:, here], 1.0, 0.0).astype(bf16)
            picked = jnp.dot(both, one_hot, preferred_element_type=f32)
            picked = picked[0:8] + picked[8:16]
            offset = offset_ref[:, here]
            turn = cross([picked[3 + i : 4 + i] for i in range(3)], [offset[i : i + 1] for i in range(3)])
            sphere_ref[:, here] = picked[0:3] + jnp.concatenate(turn, axis=0)

    clump_ref[...] = velocity_ref[lax.axis_index("space")]


def swap_cores(value):
    return lax.ppermute(value, "sub", [(0, 1), (1, 0)])


def send(value, stride, move):
    pairs = []
    for chip in range(lax.axis_size("space")):
        digit = chip // stride % len(move)
        pairs.append((chip, chip + (move[digit] - digit) * stride))
    return lax.ppermute(value, "space", pairs)


def steps_of(owners):
    steps, stride = [], owners
    while stride > 1:
        radix = math.gcd(stride, 4)
        stride //= radix
        steps.append((stride, ((1, 0),) if radix == 2 else OTHER_MOVES if steps else FIRST_MOVES))
    return steps


def per_device(
    fluid_state, sphere_state, sphere_offset, tile_list, tile_count, clump_ids, clump_state, clump_inverse
):
    owners = lax.axis_size("space")
    spheres = sphere_state.shape[1]
    fluid = fluid_state.shape[1]
    clumps = clump_state.shape[1]
    slots = tile_list.shape[0]
    rows = 3 * owners
    ids = clump_ids.reshape(1, spheres)
    vmem = pl.BlockSpec(memory_space=pltpu.VMEM)
    hbm = pl.BlockSpec(memory_space=pltpu.HBM)
    params = pltpu.CompilerParams(vmem_limit_bytes=48 * 1024 * 1024)

    keep, give = pl.pallas_call(
        loads_kernel,
        out_shape=(pltpu.VMEM((rows, clumps), f32), pltpu.VMEM((rows, clumps), f32)),
        in_specs=[pl.BlockSpec(memory_space=pltpu.SMEM)] + [hbm] * 7,
        out_specs=(vmem, vmem),
        scratch_shapes=[
            pltpu.SMEM((2, slots), jnp.int32),
            pltpu.VMEM((8, fluid), f32),
            pltpu.VMEM((7, spheres), f32),
            pltpu.VMEM((3, spheres), f32),
            pltpu.VMEM((1, spheres), jnp.int32),
            pltpu.VMEM((6, clumps), f32),
            pltpu.VMEM((4, clumps), f32),
            pltpu.SemaphoreType.DMA((7,)),
            pltpu.VMEM((3, spheres), f32),
            pltpu.VMEM((BLOCK, TILE, 2 * TILE), bf16),
            pltpu.VMEM((fluid // TILE, TILE, 3 * TILE), f32),
            pltpu.VMEM((fluid // TILE, 32, 2 * TILE), bf16),
            pltpu.VMEM((UNROLL, 2 * TILE, TILE), bf16),
            pltpu.VMEM((16, spheres), f32),
        ],
        compiler_params=params,
        name="clump_loads",
    )(tile_count, *(
        pltpu.with_memory_space_constraint(value, pltpu.HBM)
        for value in (
            tile_list.T, fluid_state, sphere_state, sphere_offset, ids, clump_state, clump_inverse
        )
    ))

    def small(kernel, height, name, *operands, scratch=()):
        return pl.pallas_call(
            kernel,
            out_shape=pltpu.VMEM((height, clumps), f32),
            in_specs=[vmem] * len(operands),
            out_specs=vmem,
            scratch_shapes=scratch,
            compiler_params=params,
            name=name,
        )(*operands)

    mine = small(first_kernel, rows + 3, "core_sum", keep, swap_cores(give), clump_inverse)
    steps = steps_of(owners)
    for stride, moves in steps:
        parts = [mine] + [send(mine, stride, move) for move in moves]
        if stride > 1:
            height = rows + len(parts) * (mine.shape[0] - rows)
            mine = small(functools.partial(join_kernel, rows), height, "space_sum", *parts)
    velocities = small(
        functools.partial(update_kernel, steps), rows, "clump_update", *parts,
        scratch=[pltpu.VMEM((owners, 3, clumps), f32)],
    )

    return pl.pallas_call(
        velocity_kernel,
        out_shape=(
            jax.ShapeDtypeStruct((6, clumps), f32),
            jax.ShapeDtypeStruct((3, spheres), f32),
        ),
        in_specs=[vmem] * 4,
        out_specs=(vmem, vmem),
        scratch_shapes=[pltpu.VMEM((owners, 6, clumps), f32)],
        compiler_params=params,
        name="sphere_velocities",
    )(velocities, swap_cores(velocities), sphere_offset, ids)


def solution(mesh):
    in_specs = (
        P(None, "space"),
        P(None, "space"),
        P(None, "space"),
        P(("space", "sub"), None),
        P(("space", "sub")),
        P("space"),
        P(None, "space"),
        P(None, "space"),
    )
    out_specs = (P(None, "space"), P(None, "space"))
    return jax.shard_map(
        per_device, mesh=mesh, in_specs=in_specs, out_specs=out_specs, check_vma=False
    )
```

```python
import functools
import math

import jax
import jax.numpy as jnp
from jax import lax
from jax.experimental import pallas as pl
from jax.experimental.pallas import tpu as pltpu
from jax.sharding import PartitionSpec as P

TILE = 128
SLOT = 256
UNROLL = 8
FIRST_MOVES = ((1, 0, 3, 2), (3, 2, 0, 1), (2, 3, 1, 0))
OTHER_MOVES = ((2, 3, 0, 1), (3, 0, 1, 2), (1, 2, 3, 0))
LANES = 16
BLOCK = TILE // LANES

support_radius = 0.5
press_coef = 4.0
visc_coef = 1.0
gravity_step = 0.1

f32 = jnp.float32
bf16 = jnp.bfloat16


def split_two(value):
    high = value.astype(bf16)
    return high, (value - high.astype(f32)).astype(bf16)


def split_three(value):
    high = value.astype(bf16).astype(f32)
    middle = (value - high).astype(bf16).astype(f32)
    return high, middle, (value - high) - middle


def cross(left, right):
    return [
        left[1] * right[2] - left[2] * right[1],
        left[2] * right[0] - left[0] * right[2],
        left[0] * right[1] - left[1] * right[0],
    ]


def group_of(owners):
    return math.gcd(owners, 16)


def loads_kernel(
    count_ref, list_hbm, fluid_hbm, sphere_hbm, offset_hbm, ids_hbm, state_hbm, inverse_hbm,
    keep_ref, send_ref,
    list_ref, fluid_ref, sphere_ref, offset_ref, ids_ref, state_ref, inverse_ref, arrived,
    place_ref, choose_ref, wide_ref, terms_ref, weight_ref, acc_ref,
):
    fluid_tiles = fluid_ref.shape[1] // TILE
    clumps = keep_ref.shape[1]
    owners = keep_ref.shape[0] // 3
    core = lax.axis_index("sub")
    me = jnp.where(core == 0, lax.axis_index("space"), -1)

    pairs = (
        (fluid_hbm, fluid_ref),
        (sphere_hbm, sphere_ref),
        (list_hbm, list_ref),
        (offset_hbm, offset_ref),
        (ids_hbm, ids_ref),
        (state_hbm, state_ref),
        (inverse_hbm, inverse_ref),
    )
    copies = [
        pltpu.make_async_copy(source, target, arrived.at[k]) for k, (source, target) in enumerate(pairs)
    ]
    for copy in copies:
        copy.start()

    acc_ref[...] = jnp.zeros_like(acc_ref)

    lane = lax.broadcasted_iota(jnp.int32, (TILE, 2 * TILE), 0)
    target = lax.broadcasted_iota(jnp.int32, (TILE, 2 * TILE), 1) // TILE
    part = lane % LANES
    wanted = (part == target) | (part == target + 3) | (part == target + 6)
    for j in range(BLOCK):
        choose_ref[j] = jnp.where(wanted & (lane // LANES == j), 1.0, 0.0).astype(bf16)
    copies[0].wait()

    @pl.loop(0, fluid_tiles // BLOCK, unroll=2)
    def _(block):
        row = lax.broadcasted_iota(jnp.int32, (8, TILE), 0)
        lines = []
        for j in range(BLOCK):
            tile = block * BLOCK + j
            state = fluid_ref[:, pl.ds(pl.multiple_of(tile * TILE, TILE), TILE)]
            state = jnp.where(row < 3, state * (1.0 / support_radius) - 1.0, state)
            mass = state[7:8]
            first = jnp.where(row < 7, state * mass, state)
            second = jnp.where(row < 3, state * (mass * state[6:7]), 0.0)
            high, low = split_two(jnp.concatenate([first, second], axis=0))
            both = jnp.concatenate([high, low], axis=0)
            terms_ref[tile] = jnp.concatenate([both, both], axis=1)
            lines += [*split_three(state[0:3]), state[0:3], jnp.zeros((LANES - 12, TILE), f32)]
        turned = jnp.concatenate(lines, axis=0).T
        parts = turned.astype(bf16)
        for j in range(BLOCK):
            tile = block * BLOCK + j
            z = j * LANES + 11
            wide_ref[tile, :, 0 : 2 * TILE] = jnp.dot(parts, choose_ref[j], preferred_element_type=f32)
            wide_ref[tile, :, 2 * TILE :] = jnp.broadcast_to(turned[:, z : z + 1], (TILE, TILE))

    copies[1].wait()
    place_ref[...] = sphere_ref[0:3, :] * (1.0 / support_radius) - 1.0
    copies[2].wait()

    def pair_weights(slot, part):
        a = list_ref[0, slot]
        b = list_ref[1, slot]
        cols = pl.ds(pl.multiple_of(a * TILE, TILE), TILE)
        dx, dy, dz = [
            place_ref[k : k + 1, cols] - wide_ref[b, :, k * TILE : (k + 1) * TILE] for k in range(3)
        ]
        square = jnp.maximum(dx * dx + dy * dy + dz * dz, 1e-30)
        falloff = jnp.maximum(1.0 - square * lax.rsqrt(square), 0.0)
        high, low = split_two(falloff * falloff * falloff)
        weight_ref[part, 0:TILE, :] = high
        weight_ref[part, TILE:, :] = low

    def add_sums(slot, part, live):
        a = list_ref[0, slot]
        b = list_ref[1, slot]
        cols = pl.ds(pl.multiple_of(a * TILE, TILE), TILE)
        sums = jnp.dot(terms_ref[b], weight_ref[part], preferred_element_type=f32)
        acc_ref[:, cols] += live * (sums[0:16] + sums[16:32])

    count = count_ref[0]
    trips = (count + UNROLL - 1) // UNROLL
    last = list_ref.shape[1] - 1

    for part in range(UNROLL):
        pair_weights(min(part, last), part)

    @pl.loop(1, trips)
    def _(trip):
        for part in range(UNROLL):
            add_sums((trip - 1) * UNROLL + part, part, 1.0)
        for part in range(UNROLL):
            pair_weights(jnp.minimum(trip * UNROLL + part, last), part)

    for part in range(UNROLL):
        slot = (trips - 1) * UNROLL + part
        live = jnp.where(slot < count, 1.0, 0.0).astype(f32)
        add_sums(jnp.clip(slot, 0, last), part, live)

    for copy in copies[3:]:
        copy.wait()
    group = group_of(owners)
    width = group * SLOT

    row = lax.broadcasted_iota(jnp.int32, state_ref.shape, 0)
    still = state_ref[...] + jnp.where(row == 2, -gravity_step, 0.0)
    still = still / jnp.concatenate([inverse_ref[0:1, :]] * 3 + [inverse_ref[1:4, :]], axis=0)

    @pl.loop(0, owners // group)
    def _(block):
        cols = pl.ds(pl.multiple_of(block * width, width), width)
        acc = acc_ref[:, cols]
        place = place_ref[:, cols]
        sphere = sphere_ref[:, cols]
        offset = offset_ref[:, cols]
        total = acc[7:8]
        pull = total * place - acc[0:3]
        press = acc[6:7] * place - acc[8:11]
        scale = press_coef * support_radius
        force = scale * (sphere[6:7] * pull + press) + visc_coef * (acc[3:6] - total * sphere[3:6])
        force = [force[k : k + 1] for k in range(3)]
        turn = cross([offset[k : k + 1] for k in range(3)], force)
        loads = jnp.concatenate(force + turn + [jnp.zeros_like(force[0])] * 2, axis=0)
        high, low = split_two(loads)
        both = jnp.concatenate([high, low], axis=0)
        column = lax.broadcasted_iota(jnp.int32, (clumps, SLOT), 0)
        keep, send = [], []
        for k in range(group):
            here = pl.ds(pl.multiple_of(block * width + k * SLOT, SLOT), SLOT)
            one_hot = jnp.where(column == ids_ref[:, here], 1.0, 0.0).astype(bf16)
            sums = lax.dot_general(
                both[:, k * SLOT : (k + 1) * SLOT], one_hot, (((1,), (1,)), ((), ())),
                preferred_element_type=f32,
            )
            own = jnp.where(block * group + k == me, 1.0, 0.0).astype(f32)
            sums = (sums[0:8] + sums[8:16])[0:6] + own * still
            keep.append(jnp.where(core == 0, sums[0:3], sums[3:6]))
            send.append(jnp.where(core == 0, sums[3:6], sums[0:3]))
        here = pl.ds(pl.multiple_of(block * (3 * group), math.gcd(3 * group, 8)), 3 * group)
        keep_ref[here, :] = jnp.concatenate(keep, axis=0)
        send_ref[here, :] = jnp.concatenate(send, axis=0)


def first_kernel(keep_ref, arrived_ref, inverse_ref, out_ref):
    rows = keep_ref.shape[0]
    out_ref[0:rows, :] = keep_ref[...] + arrived_ref[...]
    linear = jnp.concatenate([inverse_ref[0:1, :]] * 3, axis=0)
    out_ref[rows:, :] = jnp.where(lax.axis_index("sub") == 0, linear, inverse_ref[1:4, :])


def sum_rows(refs, rows):
    sums = [ref[0:rows, :] for ref in refs]
    while len(sums) > 1:
        sums = [left + right for left, right in zip(sums[0::2], sums[1::2])]
    return sums[0]


def join_kernel(rows, *refs):
    *parts, out_ref = refs
    more = parts[0].shape[0] - rows
    out_ref[0:rows, :] = sum_rows(parts, rows)
    for k, ref in enumerate(parts):
        out_ref[rows + k * more : rows + (k + 1) * more, :] = ref[rows:, :]


def update_kernel(steps, *refs):
    *parts, out_ref, inverse_ref = refs
    owners = inverse_ref.shape[0]
    rows = 3 * owners
    held = owners // len(parts)
    me = lax.axis_index("space")
    holders = [0]
    for stride, moves in steps:
        radix = len(moves[0])
        here = me // stride % radix
        sources = [here]
        for move in moves:
            sources.append(sum(jnp.where(here == at, move.index(at), 0) for at in range(radix)))
        holders = [holder + source * stride for source in sources for holder in holders]
    for k, holder in enumerate(holders):
        first = rows + 3 * (k % held)
        inverse_ref[holder] = parts[k // held][first : first + 3, :]
    out_ref[...] = sum_rows(parts, rows) * jnp.concatenate([inverse_ref[k] for k in range(owners)], axis=0)


def velocity_kernel(mine_ref, arrived_ref, offset_ref, ids_ref, clump_ref, sphere_ref, velocity_ref):
    owners, _, clumps = velocity_ref.shape
    group = group_of(owners)
    core = lax.axis_index("sub")

    @pl.loop(0, owners // group)
    def _(block):
        rows = pl.ds(pl.multiple_of(block * (3 * group), math.gcd(3 * group, 8)), 3 * group)
        mine = mine_ref[rows, :]
        arrived = arrived_ref[rows, :]
        linear = jnp.where(core == 0, mine, arrived)
        angular = jnp.where(core == 0, arrived, mine)
        for k in range(group):
            owner = block * group + k
            three = slice(3 * k, 3 * k + 3)
            velocity = jnp.concatenate([linear[three], angular[three]], axis=0)
            velocity_ref[owner] = velocity
            both = jnp.concatenate(
                split_two(jnp.concatenate([velocity, jnp.zeros((2, clumps), f32)], axis=0)), axis=0
            )
            here = pl.ds(pl.multiple_of(owner * SLOT, SLOT), SLOT)
            column = lax.broadcasted_iota(jnp.int32, (clumps, SLOT), 0)
            one_hot = jnp.where(column == ids_ref[:, here], 1.0, 0.0).astype(bf16)
            picked = jnp.dot(both, one_hot, preferred_element_type=f32)
            picked = picked[0:8] + picked[8:16]
            offset = offset_ref[:, here]
            turn = cross([picked[3 + i : 4 + i] for i in range(3)], [offset[i : i + 1] for i in range(3)])
            sphere_ref[:, here] = picked[0:3] + jnp.concatenate(turn, axis=0)

    clump_ref[...] = velocity_ref[lax.axis_index("space")]


def swap_cores(value):
    return lax.ppermute(value, "sub", [(0, 1), (1, 0)])


def send(value, stride, move):
    pairs = []
    for chip in range(lax.axis_size("space")):
        digit = chip // stride % len(move)
        pairs.append((chip, chip + (move[digit] - digit) * stride))
    return lax.ppermute(value, "space", pairs)


def steps_of(owners):
    steps, stride = [], owners
    while stride > 1:
        radix = math.gcd(stride, 4)
        stride //= radix
        steps.append((stride, ((1, 0),) if radix == 2 else OTHER_MOVES if steps else FIRST_MOVES))
    return steps


def per_device(
    fluid_state, sphere_state, sphere_offset, tile_list, tile_count, clump_ids, clump_state, clump_inverse
):
    owners = lax.axis_size("space")
    spheres = sphere_state.shape[1]
    fluid = fluid_state.shape[1]
    clumps = clump_state.shape[1]
    slots = tile_list.shape[0]
    rows = 3 * owners
    ids = clump_ids.reshape(1, spheres)
    vmem = pl.BlockSpec(memory_space=pltpu.VMEM)
    hbm = pl.BlockSpec(memory_space=pltpu.HBM)
    params = pltpu.CompilerParams(vmem_limit_bytes=48 * 1024 * 1024)

    keep, give = pl.pallas_call(
        loads_kernel,
        out_shape=(pltpu.VMEM((rows, clumps), f32), pltpu.VMEM((rows, clumps), f32)),
        in_specs=[pl.BlockSpec(memory_space=pltpu.SMEM)] + [hbm] * 7,
        out_specs=(vmem, vmem),
        scratch_shapes=[
            pltpu.SMEM((2, slots), jnp.int32),
            pltpu.VMEM((8, fluid), f32),
            pltpu.VMEM((7, spheres), f32),
            pltpu.VMEM((3, spheres), f32),
            pltpu.VMEM((1, spheres), jnp.int32),
            pltpu.VMEM((6, clumps), f32),
            pltpu.VMEM((4, clumps), f32),
            pltpu.SemaphoreType.DMA((7,)),
            pltpu.VMEM((3, spheres), f32),
            pltpu.VMEM((BLOCK, TILE, 2 * TILE), bf16),
            pltpu.VMEM((fluid // TILE, TILE, 3 * TILE), f32),
            pltpu.VMEM((fluid // TILE, 32, 2 * TILE), bf16),
            pltpu.VMEM((UNROLL, 2 * TILE, TILE), bf16),
            pltpu.VMEM((16, spheres), f32),
        ],
        compiler_params=params,
        name="clump_loads",
    )(tile_count, *(
        pltpu.with_memory_space_constraint(value, pltpu.HBM)
        for value in (
            tile_list.T, fluid_state, sphere_state, sphere_offset, ids, clump_state, clump_inverse
        )
    ))

    def small(kernel, height, name, *operands, scratch=()):
        return pl.pallas_call(
            kernel,
            out_shape=pltpu.VMEM((height, clumps), f32),
            in_specs=[vmem] * len(operands),
            out_specs=vmem,
            scratch_shapes=scratch,
            compiler_params=params,
            name=name,
        )(*operands)

    mine = small(first_kernel, rows + 3, "core_sum", keep, swap_cores(give), clump_inverse)
    steps = steps_of(owners)
    for stride, moves in steps:
        parts = [mine] + [send(mine, stride, move) for move in moves]
        if stride > 1:
            height = rows + len(parts) * (mine.shape[0] - rows)
            mine = small(functools.partial(join_kernel, rows), height, "space_sum", *parts)
    velocities = small(
        functools.partial(update_kernel, steps), rows, "clump_update", *parts,
        scratch=[pltpu.VMEM((owners, 3, clumps), f32)],
    )

    return pl.pallas_call(
        velocity_kernel,
        out_shape=(
            jax.ShapeDtypeStruct((6, clumps), f32),
            jax.ShapeDtypeStruct((3, spheres), f32),
        ),
        in_specs=[vmem] * 4,
        out_specs=(vmem, vmem),
        scratch_shapes=[pltpu.VMEM((owners, 6, clumps), f32)],
        compiler_params=params,
        name="sphere_velocities",
    )(velocities, swap_cores(velocities), sphere_offset, ids)


def solution(mesh):
    in_specs = (
        P(None, "space"),
        P(None, "space"),
        P(None, "space"),
        P(("space", "sub"), None),
        P(("space", "sub")),
        P("space"),
        P(None, "space"),
        P(None, "space"),
    )
    out_specs = (P(None, "space"), P(None, "space"))
    return jax.shard_map(
        per_device, mesh=mesh, in_specs=in_specs, out_specs=out_specs, check_vma=False
    )
```

```python
import functools
import math

import jax
import jax.numpy as jnp
from jax import lax
from jax.experimental import pallas as pl
from jax.experimental.pallas import tpu as pltpu
from jax.sharding import PartitionSpec as P

TILE = 128
SLOT = 256
UNROLL = 8
FIRST_MOVES = ((1, 0, 3, 2), (3, 2, 0, 1), (2, 3, 1, 0))
OTHER_MOVES = ((2, 3, 0, 1), (3, 0, 1, 2), (1, 2, 3, 0))
LANES = 16
BLOCK = TILE // LANES

support_radius = 0.5
press_coef = 4.0
visc_coef = 1.0
gravity_step = 0.1

f32 = jnp.float32
bf16 = jnp.bfloat16


def split_two(value):
    high = value.astype(bf16)
    return high, (value - high.astype(f32)).astype(bf16)


def split_three(value):
    high = value.astype(bf16).astype(f32)
    middle = (value - high).astype(bf16).astype(f32)
    return high, middle, (value - high) - middle


def cross(left, right):
    return [
        left[1] * right[2] - left[2] * right[1],
        left[2] * right[0] - left[0] * right[2],
        left[0] * right[1] - left[1] * right[0],
    ]


def group_of(owners):
    return math.gcd(owners, 16)


def loads_kernel(
    count_ref, list_hbm, fluid_hbm, sphere_hbm, offset_hbm, ids_hbm, state_hbm, inverse_hbm,
    keep_ref, send_ref,
    list_ref, fluid_ref, sphere_ref, offset_ref, ids_ref, state_ref, inverse_ref, arrived,
    place_ref, choose_ref, wide_ref, terms_ref, weight_ref, acc_ref,
):
    fluid_tiles = fluid_ref.shape[1] // TILE
    clumps = keep_ref.shape[1]
    owners = keep_ref.shape[0] // 3
    core = lax.axis_index("sub")
    me = jnp.where(core == 0, lax.axis_index("space"), -1)

    pairs = (
        (fluid_hbm, fluid_ref),
        (sphere_hbm, sphere_ref),
        (list_hbm, list_ref),
        (offset_hbm, offset_ref),
        (ids_hbm, ids_ref),
        (state_hbm, state_ref),
        (inverse_hbm, inverse_ref),
    )
    copies = [
        pltpu.make_async_copy(source, target, arrived.at[k]) for k, (source, target) in enumerate(pairs)
    ]
    for copy in copies:
        copy.start()

    acc_ref[...] = jnp.zeros_like(acc_ref)

    lane = lax.broadcasted_iota(jnp.int32, (TILE, 2 * TILE), 0)
    target = lax.broadcasted_iota(jnp.int32, (TILE, 2 * TILE), 1) // TILE
    part = lane % LANES
    wanted = (part == target) | (part == target + 3) | (part == target + 6)
    for j in range(BLOCK):
        choose_ref[j] = jnp.where(wanted & (lane // LANES == j), 1.0, 0.0).astype(bf16)
    copies[0].wait()

    @pl.loop(0, fluid_tiles // BLOCK, unroll=4)
    def _(block):
        row = lax.broadcasted_iota(jnp.int32, (8, TILE), 0)
        lines = []
        for j in range(BLOCK):
            tile = block * BLOCK + j
            state = fluid_ref[:, pl.ds(pl.multiple_of(tile * TILE, TILE), TILE)]
            state = jnp.where(row < 3, state * (1.0 / support_radius) - 1.0, state)
            mass = state[7:8]
            first = jnp.where(row < 7, state * mass, state)
            second = jnp.where(row < 3, state * (mass * state[6:7]), 0.0)
            high, low = split_two(jnp.concatenate([first, second], axis=0))
            both = jnp.concatenate([high, low], axis=0)
            terms_ref[tile] = jnp.concatenate([both, both], axis=1)
            lines += [*split_three(state[0:3]), state[0:3], jnp.zeros((LANES - 12, TILE), f32)]
        turned = jnp.concatenate(lines, axis=0).T
        parts = turned.astype(bf16)
        for j in range(BLOCK):
            tile = block * BLOCK + j
            z = j * LANES + 11
            wide_ref[tile, :, 0 : 2 * TILE] = jnp.dot(parts, choose_ref[j], preferred_element_type=f32)
            wide_ref[tile, :, 2 * TILE :] = jnp.broadcast_to(turned[:, z : z + 1], (TILE, TILE))

    copies[1].wait()
    place_ref[...] = sphere_ref[0:3, :] * (1.0 / support_radius) - 1.0
    copies[2].wait()

    def pair_weights(slot, part):
        a = list_ref[0, slot]
        b = list_ref[1, slot]
        cols = pl.ds(pl.multiple_of(a * TILE, TILE), TILE)
        dx, dy, dz = [
            place_ref[k : k + 1, cols] - wide_ref[b, :, k * TILE : (k + 1) * TILE] for k in range(3)
        ]
        square = jnp.maximum(dx * dx + dy * dy + dz * dz, 1e-30)
        falloff = jnp.maximum(1.0 - square * lax.rsqrt(square), 0.0)
        high, low = split_two(falloff * falloff * falloff)
        weight_ref[part, 0:TILE, :] = high
        weight_ref[part, TILE:, :] = low

    def add_sums(slot, part, live):
        a = list_ref[0, slot]
        b = list_ref[1, slot]
        cols = pl.ds(pl.multiple_of(a * TILE, TILE), TILE)
        sums = jnp.dot(terms_ref[b], weight_ref[part], preferred_element_type=f32)
        acc_ref[:, cols] += live * (sums[0:16] + sums[16:32])

    count = count_ref[0]
    trips = (count + UNROLL - 1) // UNROLL
    last = list_ref.shape[1] - 1

    for part in range(UNROLL):
        pair_weights(min(part, last), part)

    @pl.loop(1, trips)
    def _(trip):
        for part in range(UNROLL):
            add_sums((trip - 1) * UNROLL + part, part, 1.0)
        for part in range(UNROLL):
            pair_weights(jnp.minimum(trip * UNROLL + part, last), part)

    for part in range(UNROLL):
        slot = (trips - 1) * UNROLL + part
        live = jnp.where(slot < count, 1.0, 0.0).astype(f32)
        add_sums(jnp.clip(slot, 0, last), part, live)

    for copy in copies[3:]:
        copy.wait()
    group = group_of(owners)
    width = group * SLOT

    row = lax.broadcasted_iota(jnp.int32, state_ref.shape, 0)
    still = state_ref[...] + jnp.where(row == 2, -gravity_step, 0.0)
    still = still / jnp.concatenate([inverse_ref[0:1, :]] * 3 + [inverse_ref[1:4, :]], axis=0)

    @pl.loop(0, owners // group)
    def _(block):
        cols = pl.ds(pl.multiple_of(block * width, width), width)
        acc = acc_ref[:, cols]
        place = place_ref[:, cols]
        sphere = sphere_ref[:, cols]
        offset = offset_ref[:, cols]
        total = acc[7:8]
        pull = total * place - acc[0:3]
        press = acc[6:7] * place - acc[8:11]
        scale = press_coef * support_radius
        force = scale * (sphere[6:7] * pull + press) + visc_coef * (acc[3:6] - total * sphere[3:6])
        force = [force[k : k + 1] for k in range(3)]
        turn = cross([offset[k : k + 1] for k in range(3)], force)
        loads = jnp.concatenate(force + turn + [jnp.zeros_like(force[0])] * 2, axis=0)
        high, low = split_two(loads)
        both = jnp.concatenate([high, low], axis=0)
        column = lax.broadcasted_iota(jnp.int32, (clumps, SLOT), 0)
        keep, send = [], []
        for k in range(group):
            here = pl.ds(pl.multiple_of(block * width + k * SLOT, SLOT), SLOT)
            one_hot = jnp.where(column == ids_ref[:, here], 1.0, 0.0).astype(bf16)
            sums = lax.dot_general(
                both[:, k * SLOT : (k + 1) * SLOT], one_hot, (((1,), (1,)), ((), ())),
                preferred_element_type=f32,
            )
            own = jnp.where(block * group + k == me, 1.0, 0.0).astype(f32)
            sums = (sums[0:8] + sums[8:16])[0:6] + own * still
            keep.append(jnp.where(core == 0, sums[0:3], sums[3:6]))
            send.append(jnp.where(core == 0, sums[3:6], sums[0:3]))
        here = pl.ds(pl.multiple_of(block * (3 * group), math.gcd(3 * group, 8)), 3 * group)
        keep_ref[here, :] = jnp.concatenate(keep, axis=0)
        send_ref[here, :] = jnp.concatenate(send, axis=0)


def first_kernel(keep_ref, arrived_ref, inverse_ref, out_ref):
    rows = keep_ref.shape[0]
    out_ref[0:rows, :] = keep_ref[...] + arrived_ref[...]
    linear = jnp.concatenate([inverse_ref[0:1, :]] * 3, axis=0)
    out_ref[rows:, :] = jnp.where(lax.axis_index("sub") == 0, linear, inverse_ref[1:4, :])


def sum_rows(refs, rows):
    sums = [ref[0:rows, :] for ref in refs]
    while len(sums) > 1:
        sums = [left + right for left, right in zip(sums[0::2], sums[1::2])]
    return sums[0]


def join_kernel(rows, *refs):
    *parts, out_ref = refs
    more = parts[0].shape[0] - rows
    out_ref[0:rows, :] = sum_rows(parts, rows)
    for k, ref in enumerate(parts):
        out_ref[rows + k * more : rows + (k + 1) * more, :] = ref[rows:, :]


def update_kernel(steps, *refs):
    *parts, out_ref, inverse_ref = refs
    owners = inverse_ref.shape[0]
    rows = 3 * owners
    held = owners // len(parts)
    me = lax.axis_index("space")
    holders = [0]
    for stride, moves in steps:
        radix = len(moves[0])
        here = me // stride % radix
        sources = [here]
        for move in moves:
            sources.append(sum(jnp.where(here == at, move.index(at), 0) for at in range(radix)))
        holders = [holder + source * stride for source in sources for holder in holders]
    for k, holder in enumerate(holders):
        first = rows + 3 * (k % held)
        inverse_ref[holder] = parts[k // held][first : first + 3, :]
    out_ref[...] = sum_rows(parts, rows) * jnp.concatenate([inverse_ref[k] for k in range(owners)], axis=0)


def velocity_kernel(mine_ref, arrived_ref, offset_ref, ids_ref, clump_ref, sphere_ref, velocity_ref):
    owners, _, clumps = velocity_ref.shape
    group = group_of(owners)
    core = lax.axis_index("sub")

    @pl.loop(0, owners // group)
    def _(block):
        rows = pl.ds(pl.multiple_of(block * (3 * group), math.gcd(3 * group, 8)), 3 * group)
        mine = mine_ref[rows, :]
        arrived = arrived_ref[rows, :]
        linear = jnp.where(core == 0, mine, arrived)
        angular = jnp.where(core == 0, arrived, mine)
        for k in range(group):
            owner = block * group + k
            three = slice(3 * k, 3 * k + 3)
            velocity = jnp.concatenate([linear[three], angular[three]], axis=0)
            velocity_ref[owner] = velocity
            both = jnp.concatenate(
                split_two(jnp.concatenate([velocity, jnp.zeros((2, clumps), f32)], axis=0)), axis=0
            )
            here = pl.ds(pl.multiple_of(owner * SLOT, SLOT), SLOT)
            column = lax.broadcasted_iota(jnp.int32, (clumps, SLOT), 0)
            one_hot = jnp.where(column == ids_ref[:, here], 1.0, 0.0).astype(bf16)
            picked = jnp.dot(both, one_hot, preferred_element_type=f32)
            picked = picked[0:8] + picked[8:16]
            offset = offset_ref[:, here]
            turn = cross([picked[3 + i : 4 + i] for i in range(3)], [offset[i : i + 1] for i in range(3)])
            sphere_ref[:, here] = picked[0:3] + jnp.concatenate(turn, axis=0)

    clump_ref[...] = velocity_ref[lax.axis_index("space")]


def swap_cores(value):
    return lax.ppermute(value, "sub", [(0, 1), (1, 0)])


def send(value, stride, move):
    pairs = []
    for chip in range(lax.axis_size("space")):
        digit = chip // stride % len(move)
        pairs.append((chip, chip + (move[digit] - digit) * stride))
    return lax.ppermute(value, "space", pairs)


def steps_of(owners):
    steps, stride = [], owners
    while stride > 1:
        radix = math.gcd(stride, 4)
        stride //= radix
        steps.append((stride, ((1, 0),) if radix == 2 else OTHER_MOVES if steps else FIRST_MOVES))
    return steps


def per_device(
    fluid_state, sphere_state, sphere_offset, tile_list, tile_count, clump_ids, clump_state, clump_inverse
):
    owners = lax.axis_size("space")
    spheres = sphere_state.shape[1]
    fluid = fluid_state.shape[1]
    clumps = clump_state.shape[1]
    slots = tile_list.shape[0]
    rows = 3 * owners
    ids = clump_ids.reshape(1, spheres)
    vmem = pl.BlockSpec(memory_space=pltpu.VMEM)
    hbm = pl.BlockSpec(memory_space=pltpu.HBM)
    params = pltpu.CompilerParams(vmem_limit_bytes=48 * 1024 * 1024)

    keep, give = pl.pallas_call(
        loads_kernel,
        out_shape=(pltpu.VMEM((rows, clumps), f32), pltpu.VMEM((rows, clumps), f32)),
        in_specs=[pl.BlockSpec(memory_space=pltpu.SMEM)] + [hbm] * 7,
        out_specs=(vmem, vmem),
        scratch_shapes=[
            pltpu.SMEM((2, slots), jnp.int32),
            pltpu.VMEM((8, fluid), f32),
            pltpu.VMEM((7, spheres), f32),
            pltpu.VMEM((3, spheres), f32),
            pltpu.VMEM((1, spheres), jnp.int32),
            pltpu.VMEM((6, clumps), f32),
            pltpu.VMEM((4, clumps), f32),
            pltpu.SemaphoreType.DMA((7,)),
            pltpu.VMEM((3, spheres), f32),
            pltpu.VMEM((BLOCK, TILE, 2 * TILE), bf16),
            pltpu.VMEM((fluid // TILE, TILE, 3 * TILE), f32),
            pltpu.VMEM((fluid // TILE, 32, 2 * TILE), bf16),
            pltpu.VMEM((UNROLL, 2 * TILE, TILE), bf16),
            pltpu.VMEM((16, spheres), f32),
        ],
        compiler_params=params,
        name="clump_loads",
    )(tile_count, *(
        pltpu.with_memory_space_constraint(value, pltpu.HBM)
        for value in (
            tile_list.T, fluid_state, sphere_state, sphere_offset, ids, clump_state, clump_inverse
        )
    ))

    def small(kernel, height, name, *operands, scratch=()):
        return pl.pallas_call(
            kernel,
            out_shape=pltpu.VMEM((height, clumps), f32),
            in_specs=[vmem] * len(operands),
            out_specs=vmem,
            scratch_shapes=scratch,
            compiler_params=params,
            name=name,
        )(*operands)

    mine = small(first_kernel, rows + 3, "core_sum", keep, swap_cores(give), clump_inverse)
    steps = steps_of(owners)
    for stride, moves in steps:
        parts = [mine] + [send(mine, stride, move) for move in moves]
        if stride > 1:
            height = rows + len(parts) * (mine.shape[0] - rows)
            mine = small(functools.partial(join_kernel, rows), height, "space_sum", *parts)
    velocities = small(
        functools.partial(update_kernel, steps), rows, "clump_update", *parts,
        scratch=[pltpu.VMEM((owners, 3, clumps), f32)],
    )

    return pl.pallas_call(
        velocity_kernel,
        out_shape=(
            jax.ShapeDtypeStruct((6, clumps), f32),
            jax.ShapeDtypeStruct((3, spheres), f32),
        ),
        in_specs=[vmem] * 4,
        out_specs=(vmem, vmem),
        scratch_shapes=[pltpu.VMEM((owners, 6, clumps), f32)],
        compiler_params=params,
        name="sphere_velocities",
    )(velocities, swap_cores(velocities), sphere_offset, ids)


def solution(mesh):
    in_specs = (
        P(None, "space"),
        P(None, "space"),
        P(None, "space"),
        P(("space", "sub"), None),
        P(("space", "sub")),
        P("space"),
        P(None, "space"),
        P(None, "space"),
    )
    out_specs = (P(None, "space"), P(None, "space"))
    return jax.shard_map(
        per_device, mesh=mesh, in_specs=in_specs, out_specs=out_specs, check_vma=False
    )
```

```python
import functools
import math

import jax
import jax.numpy as jnp
from jax import lax
from jax.experimental import pallas as pl
from jax.experimental.pallas import tpu as pltpu
from jax.sharding import PartitionSpec as P

TILE = 128
SLOT = 256
UNROLL = 8
FIRST_MOVES = ((1, 0, 3, 2), (3, 2, 0, 1), (2, 3, 1, 0))
OTHER_MOVES = ((2, 3, 0, 1), (1, 0, 3, 2), (3, 2, 1, 0))
LANES = 16
BLOCK = TILE // LANES

support_radius = 0.5
press_coef = 4.0
visc_coef = 1.0
gravity_step = 0.1

f32 = jnp.float32
bf16 = jnp.bfloat16


def split_two(value):
    high = value.astype(bf16)
    return high, (value - high.astype(f32)).astype(bf16)


def split_three(value):
    high = value.astype(bf16).astype(f32)
    middle = (value - high).astype(bf16).astype(f32)
    return high, middle, (value - high) - middle


def cross(left, right):
    return [
        left[1] * right[2] - left[2] * right[1],
        left[2] * right[0] - left[0] * right[2],
        left[0] * right[1] - left[1] * right[0],
    ]


def group_of(owners):
    return math.gcd(owners, 16)


def loads_kernel(
    count_ref, list_hbm, fluid_hbm, sphere_hbm, offset_hbm, ids_hbm, state_hbm, inverse_hbm,
    keep_ref, send_ref,
    list_ref, fluid_ref, sphere_ref, offset_ref, ids_ref, state_ref, inverse_ref, arrived,
    place_ref, choose_ref, wide_ref, terms_ref, weight_ref, acc_ref,
):
    fluid_tiles = fluid_ref.shape[1] // TILE
    clumps = keep_ref.shape[1]
    owners = keep_ref.shape[0] // 3
    core = lax.axis_index("sub")
    me = jnp.where(core == 0, lax.axis_index("space"), -1)

    pairs = (
        (fluid_hbm, fluid_ref),
        (sphere_hbm, sphere_ref),
        (list_hbm, list_ref),
        (offset_hbm, offset_ref),
        (ids_hbm, ids_ref),
        (state_hbm, state_ref),
        (inverse_hbm, inverse_ref),
    )
    copies = [
        pltpu.make_async_copy(source, target, arrived.at[k]) for k, (source, target) in enumerate(pairs)
    ]
    for copy in copies:
        copy.start()

    acc_ref[...] = jnp.zeros_like(acc_ref)

    lane = lax.broadcasted_iota(jnp.int32, (TILE, 2 * TILE), 0)
    target = lax.broadcasted_iota(jnp.int32, (TILE, 2 * TILE), 1) // TILE
    part = lane % LANES
    wanted = (part == target) | (part == target + 3) | (part == target + 6)
    for j in range(BLOCK):
        choose_ref[j] = jnp.where(wanted & (lane // LANES == j), 1.0, 0.0).astype(bf16)
    copies[0].wait()

    @pl.loop(0, fluid_tiles // BLOCK, unroll=4)
    def _(block):
        row = lax.broadcasted_iota(jnp.int32, (8, TILE), 0)
        lines = []
        for j in range(BLOCK):
            tile = block * BLOCK + j
            state = fluid_ref[:, pl.ds(pl.multiple_of(tile * TILE, TILE), TILE)]
            state = jnp.where(row < 3, state * (1.0 / support_radius) - 1.0, state)
            mass = state[7:8]
            first = jnp.where(row < 7, state * mass, state)
            second = jnp.where(row < 3, state * (mass * state[6:7]), 0.0)
            high, low = split_two(jnp.concatenate([first, second], axis=0))
            both = jnp.concatenate([high, low], axis=0)
            terms_ref[tile] = jnp.concatenate([both, both], axis=1)
            lines += [*split_three(state[0:3]), state[0:3], jnp.zeros((LANES - 12, TILE), f32)]
        turned = jnp.concatenate(lines, axis=0).T
        parts = turned.astype(bf16)
        for j in range(BLOCK):
            tile = block * BLOCK + j
            z = j * LANES + 11
            wide_ref[tile, :, 0 : 2 * TILE] = jnp.dot(parts, choose_ref[j], preferred_element_type=f32)
            wide_ref[tile, :, 2 * TILE :] = jnp.broadcast_to(turned[:, z : z + 1], (TILE, TILE))

    copies[1].wait()
    place_ref[...] = sphere_ref[0:3, :] * (1.0 / support_radius) - 1.0
    copies[2].wait()

    def pair_weights(slot, part):
        a = list_ref[0, slot]
        b = list_ref[1, slot]
        cols = pl.ds(pl.multiple_of(a * TILE, TILE), TILE)
        dx, dy, dz = [
            place_ref[k : k + 1, cols] - wide_ref[b, :, k * TILE : (k + 1) * TILE] for k in range(3)
        ]
        square = jnp.maximum(dx * dx + dy * dy + dz * dz, 1e-30)
        falloff = jnp.maximum(1.0 - square * lax.rsqrt(square), 0.0)
        high, low = split_two(falloff * falloff * falloff)
        weight_ref[part, 0:TILE, :] = high
        weight_ref[part, TILE:, :] = low

    def add_sums(slot, part, live):
        a = list_ref[0, slot]
        b = list_ref[1, slot]
        cols = pl.ds(pl.multiple_of(a * TILE, TILE), TILE)
        sums = jnp.dot(terms_ref[b], weight_ref[part], preferred_element_type=f32)
        acc_ref[:, cols] += live * (sums[0:16] + sums[16:32])

    count = count_ref[0]
    trips = (count + UNROLL - 1) // UNROLL
    last = list_ref.shape[1] - 1

    for part in range(UNROLL):
        pair_weights(min(part, last), part)

    @pl.loop(1, trips)
    def _(trip):
        for part in range(UNROLL):
            add_sums((trip - 1) * UNROLL + part, part, 1.0)
        for part in range(UNROLL):
            pair_weights(jnp.minimum(trip * UNROLL + part, last), part)

    for part in range(UNROLL):
        slot = (trips - 1) * UNROLL + part
        live = jnp.where(slot < count, 1.0, 0.0).astype(f32)
        add_sums(jnp.clip(slot, 0, last), part, live)

    for copy in copies[3:]:
        copy.wait()
    group = group_of(owners)
    width = group * SLOT

    row = lax.broadcasted_iota(jnp.int32, state_ref.shape, 0)
    still = state_ref[...] + jnp.where(row == 2, -gravity_step, 0.0)
    still = still / jnp.concatenate([inverse_ref[0:1, :]] * 3 + [inverse_ref[1:4, :]], axis=0)

    @pl.loop(0, owners // group)
    def _(block):
        cols = pl.ds(pl.multiple_of(block * width, width), width)
        acc = acc_ref[:, cols]
        place = place_ref[:, cols]
        sphere = sphere_ref[:, cols]
        offset = offset_ref[:, cols]
        total = acc[7:8]
        pull = total * place - acc[0:3]
        press = acc[6:7] * place - acc[8:11]
        scale = press_coef * support_radius
        force = scale * (sphere[6:7] * pull + press) + visc_coef * (acc[3:6] - total * sphere[3:6])
        force = [force[k : k + 1] for k in range(3)]
        turn = cross([offset[k : k + 1] for k in range(3)], force)
        loads = jnp.concatenate(force + turn + [jnp.zeros_like(force[0])] * 2, axis=0)
        high, low = split_two(loads)
        both = jnp.concatenate([high, low], axis=0)
        column = lax.broadcasted_iota(jnp.int32, (clumps, SLOT), 0)
        keep, send = [], []
        for k in range(group):
            here = pl.ds(pl.multiple_of(block * width + k * SLOT, SLOT), SLOT)
            one_hot = jnp.where(column == ids_ref[:, here], 1.0, 0.0).astype(bf16)
            sums = lax.dot_general(
                both[:, k * SLOT : (k + 1) * SLOT], one_hot, (((1,), (1,)), ((), ())),
                preferred_element_type=f32,
            )
            own = jnp.where(block * group + k == me, 1.0, 0.0).astype(f32)
            sums = (sums[0:8] + sums[8:16])[0:6] + own * still
            keep.append(jnp.where(core == 0, sums[0:3], sums[3:6]))
            send.append(jnp.where(core == 0, sums[3:6], sums[0:3]))
        here = pl.ds(pl.multiple_of(block * (3 * group), math.gcd(3 * group, 8)), 3 * group)
        keep_ref[here, :] = jnp.concatenate(keep, axis=0)
        send_ref[here, :] = jnp.concatenate(send, axis=0)


def first_kernel(keep_ref, arrived_ref, inverse_ref, out_ref):
    rows = keep_ref.shape[0]
    out_ref[0:rows, :] = keep_ref[...] + arrived_ref[...]
    linear = jnp.concatenate([inverse_ref[0:1, :]] * 3, axis=0)
    out_ref[rows:, :] = jnp.where(lax.axis_index("sub") == 0, linear, inverse_ref[1:4, :])


def sum_rows(refs, rows):
    sums = [ref[0:rows, :] for ref in refs]
    while len(sums) > 1:
        sums = [left + right for left, right in zip(sums[0::2], sums[1::2])]
    return sums[0]


def join_kernel(rows, *refs):
    *parts, out_ref = refs
    more = parts[0].shape[0] - rows
    out_ref[0:rows, :] = sum_rows(parts, rows)
    for k, ref in enumerate(parts):
        out_ref[rows + k * more : rows + (k + 1) * more, :] = ref[rows:, :]


def update_kernel(steps, *refs):
    *parts, out_ref, inverse_ref = refs
    owners = inverse_ref.shape[0]
    rows = 3 * owners
    held = owners // len(parts)
    me = lax.axis_index("space")
    holders = [0]
    for stride, moves in steps:
        radix = len(moves[0])
        here = me // stride % radix
        sources = [here]
        for move in moves:
            sources.append(sum(jnp.where(here == at, move.index(at), 0) for at in range(radix)))
        holders = [holder + source * stride for source in sources for holder in holders]
    for k, holder in enumerate(holders):
        first = rows + 3 * (k % held)
        inverse_ref[holder] = parts[k // held][first : first + 3, :]
    out_ref[...] = sum_rows(parts, rows) * jnp.concatenate([inverse_ref[k] for k in range(owners)], axis=0)


def velocity_kernel(mine_ref, arrived_ref, offset_ref, ids_ref, clump_ref, sphere_ref, velocity_ref):
    owners, _, clumps = velocity_ref.shape
    group = group_of(owners)
    core = lax.axis_index("sub")

    @pl.loop(0, owners // group)
    def _(block):
        rows = pl.ds(pl.multiple_of(block * (3 * group), math.gcd(3 * group, 8)), 3 * group)
        mine = mine_ref[rows, :]
        arrived = arrived_ref[rows, :]
        linear = jnp.where(core == 0, mine, arrived)
        angular = jnp.where(core == 0, arrived, mine)
        for k in range(group):
            owner = block * group + k
            three = slice(3 * k, 3 * k + 3)
            velocity = jnp.concatenate([linear[three], angular[three]], axis=0)
            velocity_ref[owner] = velocity
            both = jnp.concatenate(
                split_two(jnp.concatenate([velocity, jnp.zeros((2, clumps), f32)], axis=0)), axis=0
            )
            here = pl.ds(pl.multiple_of(owner * SLOT, SLOT), SLOT)
            column = lax.broadcasted_iota(jnp.int32, (clumps, SLOT), 0)
            one_hot = jnp.where(column == ids_ref[:, here], 1.0, 0.0).astype(bf16)
            picked = jnp.dot(both, one_hot, preferred_element_type=f32)
            picked = picked[0:8] + picked[8:16]
            offset = offset_ref[:, here]
            turn = cross([picked[3 + i : 4 + i] for i in range(3)], [offset[i : i + 1] for i in range(3)])
            sphere_ref[:, here] = picked[0:3] + jnp.concatenate(turn, axis=0)

    clump_ref[...] = velocity_ref[lax.axis_index("space")]


def swap_cores(value):
    return lax.ppermute(value, "sub", [(0, 1), (1, 0)])


def send(value, stride, move):
    pairs = []
    for chip in range(lax.axis_size("space")):
        digit = chip // stride % len(move)
        pairs.append((chip, chip + (move[digit] - digit) * stride))
    return lax.ppermute(value, "space", pairs)


def steps_of(owners):
    steps, stride = [], owners
    while stride > 1:
        radix = math.gcd(stride, 4)
        stride //= radix
        steps.append((stride, ((1, 0),) if radix == 2 else OTHER_MOVES if steps else FIRST_MOVES))
    return steps


def per_device(
    fluid_state, sphere_state, sphere_offset, tile_list, tile_count, clump_ids, clump_state, clump_inverse
):
    owners = lax.axis_size("space")
    spheres = sphere_state.shape[1]
    fluid = fluid_state.shape[1]
    clumps = clump_state.shape[1]
    slots = tile_list.shape[0]
    rows = 3 * owners
    ids = clump_ids.reshape(1, spheres)
    vmem = pl.BlockSpec(memory_space=pltpu.VMEM)
    hbm = pl.BlockSpec(memory_space=pltpu.HBM)
    params = pltpu.CompilerParams(vmem_limit_bytes=48 * 1024 * 1024)

    keep, give = pl.pallas_call(
        loads_kernel,
        out_shape=(pltpu.VMEM((rows, clumps), f32), pltpu.VMEM((rows, clumps), f32)),
        in_specs=[pl.BlockSpec(memory_space=pltpu.SMEM)] + [hbm] * 7,
        out_specs=(vmem, vmem),
        scratch_shapes=[
            pltpu.SMEM((2, slots), jnp.int32),
            pltpu.VMEM((8, fluid), f32),
            pltpu.VMEM((7, spheres), f32),
            pltpu.VMEM((3, spheres), f32),
            pltpu.VMEM((1, spheres), jnp.int32),
            pltpu.VMEM((6, clumps), f32),
            pltpu.VMEM((4, clumps), f32),
            pltpu.SemaphoreType.DMA((7,)),
            pltpu.VMEM((3, spheres), f32),
            pltpu.VMEM((BLOCK, TILE, 2 * TILE), bf16),
            pltpu.VMEM((fluid // TILE, TILE, 3 * TILE), f32),
            pltpu.VMEM((fluid // TILE, 32, 2 * TILE), bf16),
            pltpu.VMEM((UNROLL, 2 * TILE, TILE), bf16),
            pltpu.VMEM((16, spheres), f32),
        ],
        compiler_params=params,
        name="clump_loads",
    )(tile_count, *(
        pltpu.with_memory_space_constraint(value, pltpu.HBM)
        for value in (
            tile_list.T, fluid_state, sphere_state, sphere_offset, ids, clump_state, clump_inverse
        )
    ))

    def small(kernel, height, name, *operands, scratch=()):
        return pl.pallas_call(
            kernel,
            out_shape=pltpu.VMEM((height, clumps), f32),
            in_specs=[vmem] * len(operands),
            out_specs=vmem,
            scratch_shapes=scratch,
            compiler_params=params,
            name=name,
        )(*operands)

    mine = small(first_kernel, rows + 3, "core_sum", keep, swap_cores(give), clump_inverse)
    steps = steps_of(owners)
    for stride, moves in steps:
        parts = [mine] + [send(mine, stride, move) for move in moves]
        if stride > 1:
            height = rows + len(parts) * (mine.shape[0] - rows)
            mine = small(functools.partial(join_kernel, rows), height, "space_sum", *parts)
    velocities = small(
        functools.partial(update_kernel, steps), rows, "clump_update", *parts,
        scratch=[pltpu.VMEM((owners, 3, clumps), f32)],
    )

    return pl.pallas_call(
        velocity_kernel,
        out_shape=(
            jax.ShapeDtypeStruct((6, clumps), f32),
            jax.ShapeDtypeStruct((3, spheres), f32),
        ),
        in_specs=[vmem] * 4,
        out_specs=(vmem, vmem),
        scratch_shapes=[pltpu.VMEM((owners, 6, clumps), f32)],
        compiler_params=params,
        name="sphere_velocities",
    )(velocities, swap_cores(velocities), sphere_offset, ids)


def solution(mesh):
    in_specs = (
        P(None, "space"),
        P(None, "space"),
        P(None, "space"),
        P(("space", "sub"), None),
        P(("space", "sub")),
        P("space"),
        P(None, "space"),
        P(None, "space"),
    )
    out_specs = (P(None, "space"), P(None, "space"))
    return jax.shard_map(
        per_device, mesh=mesh, in_specs=in_specs, out_specs=out_specs, check_vma=False
    )
```

```python
import functools
import math

import jax
import jax.numpy as jnp
from jax import lax
from jax.experimental import pallas as pl
from jax.experimental.pallas import tpu as pltpu
from jax.sharding import PartitionSpec as P

TILE = 128
SLOT = 256
UNROLL = 8
FIRST_MOVES = ((1, 0, 3, 2), (3, 2, 0, 1), (2, 3, 1, 0))
OTHER_MOVES = ((2, 3, 0, 1), (3, 0, 1, 2), (1, 2, 3, 0))
LANES = 16
BLOCK = TILE // LANES

support_radius = 0.5
press_coef = 4.0
visc_coef = 1.0
gravity_step = 0.1

f32 = jnp.float32
bf16 = jnp.bfloat16


def split_two(value):
    high = value.astype(bf16)
    return high, (value - high.astype(f32)).astype(bf16)


def split_three(value):
    high = value.astype(bf16).astype(f32)
    middle = (value - high).astype(bf16).astype(f32)
    return high, middle, (value - high) - middle


def cross(left, right):
    return [
        left[1] * right[2] - left[2] * right[1],
        left[2] * right[0] - left[0] * right[2],
        left[0] * right[1] - left[1] * right[0],
    ]


def group_of(owners):
    return math.gcd(owners, 16)


def loads_kernel(
    count_ref, list_hbm, fluid_hbm, sphere_hbm, offset_hbm, ids_hbm, state_hbm, inverse_hbm,
    keep_ref, send_ref,
    list_ref, fluid_ref, sphere_ref, offset_ref, ids_ref, state_ref, inverse_ref, arrived,
    place_ref, choose_ref, wide_ref, terms_ref, weight_ref, acc_ref,
):
    fluid_tiles = fluid_ref.shape[1] // TILE
    clumps = keep_ref.shape[1]
    owners = keep_ref.shape[0] // 3
    core = lax.axis_index("sub")
    me = jnp.where(core == 0, lax.axis_index("space"), -1)

    pairs = (
        (sphere_hbm, sphere_ref),
        (list_hbm, list_ref),
        (offset_hbm, offset_ref),
        (ids_hbm, ids_ref),
        (state_hbm, state_ref),
        (inverse_hbm, inverse_ref),
    )
    copies = [
        pltpu.make_async_copy(source, target, arrived.at[k]) for k, (source, target) in enumerate(pairs)
    ]
    blocks = fluid_tiles // BLOCK
    fluid_copies = []
    for block in range(blocks):
        cols = pl.ds(block * BLOCK * TILE, BLOCK * TILE)
        fluid_copies.append(
            pltpu.make_async_copy(fluid_hbm.at[:, cols], fluid_ref.at[:, cols], arrived.at[len(pairs) + block])
        )
    for copy in fluid_copies + copies:
        copy.start()

    acc_ref[...] = jnp.zeros_like(acc_ref)

    lane = lax.broadcasted_iota(jnp.int32, (TILE, 2 * TILE), 0)
    target = lax.broadcasted_iota(jnp.int32, (TILE, 2 * TILE), 1) // TILE
    part = lane % LANES
    wanted = (part == target) | (part == target + 3) | (part == target + 6)
    for j in range(BLOCK):
        choose_ref[j] = jnp.where(wanted & (lane // LANES == j), 1.0, 0.0).astype(bf16)

    for block in range(blocks):
        fluid_copies[block].wait()
        row = lax.broadcasted_iota(jnp.int32, (8, TILE), 0)
        lines = []
        for j in range(BLOCK):
            tile = block * BLOCK + j
            state = fluid_ref[:, pl.ds(tile * TILE, TILE)]
            state = jnp.where(row < 3, state * (1.0 / support_radius) - 1.0, state)
            mass = state[7:8]
            first = jnp.where(row < 7, state * mass, state)
            second = jnp.where(row < 3, state * (mass * state[6:7]), 0.0)
            high, low = split_two(jnp.concatenate([first, second], axis=0))
            both = jnp.concatenate([high, low], axis=0)
            terms_ref[tile] = jnp.concatenate([both, both], axis=1)
            lines += [*split_three(state[0:3]), state[0:3], jnp.zeros((LANES - 12, TILE), f32)]
        turned = jnp.concatenate(lines, axis=0).T
        parts = turned.astype(bf16)
        for j in range(BLOCK):
            tile = block * BLOCK + j
            z = j * LANES + 11
            wide_ref[tile, :, 0 : 2 * TILE] = jnp.dot(parts, choose_ref[j], preferred_element_type=f32)
            wide_ref[tile, :, 2 * TILE :] = jnp.broadcast_to(turned[:, z : z + 1], (TILE, TILE))

    copies[0].wait()
    place_ref[...] = sphere_ref[0:3, :] * (1.0 / support_radius) - 1.0
    copies[1].wait()

    def pair_weights(slot, part):
        a = list_ref[0, slot]
        b = list_ref[1, slot]
        cols = pl.ds(pl.multiple_of(a * TILE, TILE), TILE)
        dx, dy, dz = [
            place_ref[k : k + 1, cols] - wide_ref[b, :, k * TILE : (k + 1) * TILE] for k in range(3)
        ]
        square = jnp.maximum(dx * dx + dy * dy + dz * dz, 1e-30)
        falloff = jnp.maximum(1.0 - square * lax.rsqrt(square), 0.0)
        high, low = split_two(falloff * falloff * falloff)
        weight_ref[part, 0:TILE, :] = high
        weight_ref[part, TILE:, :] = low

    def add_sums(slot, part, live):
        a = list_ref[0, slot]
        b = list_ref[1, slot]
        cols = pl.ds(pl.multiple_of(a * TILE, TILE), TILE)
        sums = jnp.dot(terms_ref[b], weight_ref[part], preferred_element_type=f32)
        acc_ref[:, cols] += live * (sums[0:16] + sums[16:32])

    count = count_ref[0]
    trips = (count + UNROLL - 1) // UNROLL
    last = list_ref.shape[1] - 1

    for part in range(UNROLL):
        pair_weights(min(part, last), part)

    @pl.loop(1, trips)
    def _(trip):
        for part in range(UNROLL):
            add_sums((trip - 1) * UNROLL + part, part, 1.0)
        for part in range(UNROLL):
            pair_weights(jnp.minimum(trip * UNROLL + part, last), part)

    for part in range(UNROLL):
        slot = (trips - 1) * UNROLL + part
        live = jnp.where(slot < count, 1.0, 0.0).astype(f32)
        add_sums(jnp.clip(slot, 0, last), part, live)

    for copy in copies[2:]:
        copy.wait()
    group = group_of(owners)
    width = group * SLOT

    row = lax.broadcasted_iota(jnp.int32, state_ref.shape, 0)
    still = state_ref[...] + jnp.where(row == 2, -gravity_step, 0.0)
    still = still / jnp.concatenate([inverse_ref[0:1, :]] * 3 + [inverse_ref[1:4, :]], axis=0)

    @pl.loop(0, owners // group)
    def _(block):
        cols = pl.ds(pl.multiple_of(block * width, width), width)
        acc = acc_ref[:, cols]
        place = place_ref[:, cols]
        sphere = sphere_ref[:, cols]
        offset = offset_ref[:, cols]
        total = acc[7:8]
        pull = total * place - acc[0:3]
        press = acc[6:7] * place - acc[8:11]
        scale = press_coef * support_radius
        force = scale * (sphere[6:7] * pull + press) + visc_coef * (acc[3:6] - total * sphere[3:6])
        force = [force[k : k + 1] for k in range(3)]
        turn = cross([offset[k : k + 1] for k in range(3)], force)
        loads = jnp.concatenate(force + turn + [jnp.zeros_like(force[0])] * 2, axis=0)
        high, low = split_two(loads)
        both = jnp.concatenate([high, low], axis=0)
        column = lax.broadcasted_iota(jnp.int32, (clumps, SLOT), 0)
        keep, send = [], []
        for k in range(group):
            here = pl.ds(pl.multiple_of(block * width + k * SLOT, SLOT), SLOT)
            one_hot = jnp.where(column == ids_ref[:, here], 1.0, 0.0).astype(bf16)
            sums = lax.dot_general(
                both[:, k * SLOT : (k + 1) * SLOT], one_hot, (((1,), (1,)), ((), ())),
                preferred_element_type=f32,
            )
            own = jnp.where(block * group + k == me, 1.0, 0.0).astype(f32)
            sums = (sums[0:8] + sums[8:16])[0:6] + own * still
            keep.append(jnp.where(core == 0, sums[0:3], sums[3:6]))
            send.append(jnp.where(core == 0, sums[3:6], sums[0:3]))
        here = pl.ds(pl.multiple_of(block * (3 * group), math.gcd(3 * group, 8)), 3 * group)
        keep_ref[here, :] = jnp.concatenate(keep, axis=0)
        send_ref[here, :] = jnp.concatenate(send, axis=0)


def first_kernel(keep_ref, arrived_ref, inverse_ref, out_ref):
    rows = keep_ref.shape[0]
    out_ref[0:rows, :] = keep_ref[...] + arrived_ref[...]
    linear = jnp.concatenate([inverse_ref[0:1, :]] * 3, axis=0)
    out_ref[rows:, :] = jnp.where(lax.axis_index("sub") == 0, linear, inverse_ref[1:4, :])


def sum_rows(refs, rows):
    sums = [ref[0:rows, :] for ref in refs]
    while len(sums) > 1:
        sums = [left + right for left, right in zip(sums[0::2], sums[1::2])]
    return sums[0]


def join_kernel(rows, *refs):
    *parts, out_ref = refs
    more = parts[0].shape[0] - rows
    out_ref[0:rows, :] = sum_rows(parts, rows)
    for k, ref in enumerate(parts):
        out_ref[rows + k * more : rows + (k + 1) * more, :] = ref[rows:, :]


def update_kernel(steps, *refs):
    *parts, out_ref, inverse_ref = refs
    owners = inverse_ref.shape[0]
    rows = 3 * owners
    held = owners // len(parts)
    me = lax.axis_index("space")
    holders = [0]
    for stride, moves in steps:
        radix = len(moves[0])
        here = me // stride % radix
        sources = [here]
        for move in moves:
            sources.append(sum(jnp.where(here == at, move.index(at), 0) for at in range(radix)))
        holders = [holder + source * stride for source in sources for holder in holders]
    for k, holder in enumerate(holders):
        first = rows + 3 * (k % held)
        inverse_ref[holder] = parts[k // held][first : first + 3, :]
    out_ref[...] = sum_rows(parts, rows) * jnp.concatenate([inverse_ref[k] for k in range(owners)], axis=0)


def velocity_kernel(mine_ref, arrived_ref, offset_ref, ids_ref, clump_ref, sphere_ref, velocity_ref):
    owners, _, clumps = velocity_ref.shape
    group = group_of(owners)
    core = lax.axis_index("sub")

    @pl.loop(0, owners // group)
    def _(block):
        rows = pl.ds(pl.multiple_of(block * (3 * group), math.gcd(3 * group, 8)), 3 * group)
        mine = mine_ref[rows, :]
        arrived = arrived_ref[rows, :]
        linear = jnp.where(core == 0, mine, arrived)
        angular = jnp.where(core == 0, arrived, mine)
        for k in range(group):
            owner = block * group + k
            three = slice(3 * k, 3 * k + 3)
            velocity = jnp.concatenate([linear[three], angular[three]], axis=0)
            velocity_ref[owner] = velocity
            both = jnp.concatenate(
                split_two(jnp.concatenate([velocity, jnp.zeros((2, clumps), f32)], axis=0)), axis=0
            )
            here = pl.ds(pl.multiple_of(owner * SLOT, SLOT), SLOT)
            column = lax.broadcasted_iota(jnp.int32, (clumps, SLOT), 0)
            one_hot = jnp.where(column == ids_ref[:, here], 1.0, 0.0).astype(bf16)
            picked = jnp.dot(both, one_hot, preferred_element_type=f32)
            picked = picked[0:8] + picked[8:16]
            offset = offset_ref[:, here]
            turn = cross([picked[3 + i : 4 + i] for i in range(3)], [offset[i : i + 1] for i in range(3)])
            sphere_ref[:, here] = picked[0:3] + jnp.concatenate(turn, axis=0)

    clump_ref[...] = velocity_ref[lax.axis_index("space")]


def swap_cores(value):
    return lax.ppermute(value, "sub", [(0, 1), (1, 0)])


def send(value, stride, move):
    pairs = []
    for chip in range(lax.axis_size("space")):
        digit = chip // stride % len(move)
        pairs.append((chip, chip + (move[digit] - digit) * stride))
    return lax.ppermute(value, "space", pairs)


def steps_of(owners):
    steps, stride = [], owners
    while stride > 1:
        radix = math.gcd(stride, 4)
        stride //= radix
        steps.append((stride, ((1, 0),) if radix == 2 else OTHER_MOVES if steps else FIRST_MOVES))
    return steps


def per_device(
    fluid_state, sphere_state, sphere_offset, tile_list, tile_count, clump_ids, clump_state, clump_inverse
):
    owners = lax.axis_size("space")
    spheres = sphere_state.shape[1]
    fluid = fluid_state.shape[1]
    clumps = clump_state.shape[1]
    slots = tile_list.shape[0]
    rows = 3 * owners
    ids = clump_ids.reshape(1, spheres)
    vmem = pl.BlockSpec(memory_space=pltpu.VMEM)
    hbm = pl.BlockSpec(memory_space=pltpu.HBM)
    params = pltpu.CompilerParams(vmem_limit_bytes=48 * 1024 * 1024)

    keep, give = pl.pallas_call(
        loads_kernel,
        out_shape=(pltpu.VMEM((rows, clumps), f32), pltpu.VMEM((rows, clumps), f32)),
        in_specs=[pl.BlockSpec(memory_space=pltpu.SMEM)] + [hbm] * 7,
        out_specs=(vmem, vmem),
        scratch_shapes=[
            pltpu.SMEM((2, slots), jnp.int32),
            pltpu.VMEM((8, fluid), f32),
            pltpu.VMEM((7, spheres), f32),
            pltpu.VMEM((3, spheres), f32),
            pltpu.VMEM((1, spheres), jnp.int32),
            pltpu.VMEM((6, clumps), f32),
            pltpu.VMEM((4, clumps), f32),
            pltpu.SemaphoreType.DMA((6 + fluid // (BLOCK * TILE),)),
            pltpu.VMEM((3, spheres), f32),
            pltpu.VMEM((BLOCK, TILE, 2 * TILE), bf16),
            pltpu.VMEM((fluid // TILE, TILE, 3 * TILE), f32),
            pltpu.VMEM((fluid // TILE, 32, 2 * TILE), bf16),
            pltpu.VMEM((UNROLL, 2 * TILE, TILE), bf16),
            pltpu.VMEM((16, spheres), f32),
        ],
        compiler_params=params,
        name="clump_loads",
    )(tile_count, *(
        pltpu.with_memory_space_constraint(value, pltpu.HBM)
        for value in (
            tile_list.T, fluid_state, sphere_state, sphere_offset, ids, clump_state, clump_inverse
        )
    ))

    def small(kernel, height, name, *operands, scratch=()):
        return pl.pallas_call(
            kernel,
            out_shape=pltpu.VMEM((height, clumps), f32),
            in_specs=[vmem] * len(operands),
            out_specs=vmem,
            scratch_shapes=scratch,
            compiler_params=params,
            name=name,
        )(*operands)

    mine = small(first_kernel, rows + 3, "core_sum", keep, swap_cores(give), clump_inverse)
    steps = steps_of(owners)
    for stride, moves in steps:
        parts = [mine] + [send(mine, stride, move) for move in moves]
        if stride > 1:
            height = rows + len(parts) * (mine.shape[0] - rows)
            mine = small(functools.partial(join_kernel, rows), height, "space_sum", *parts)
    velocities = small(
        functools.partial(update_kernel, steps), rows, "clump_update", *parts,
        scratch=[pltpu.VMEM((owners, 3, clumps), f32)],
    )

    return pl.pallas_call(
        velocity_kernel,
        out_shape=(
            jax.ShapeDtypeStruct((6, clumps), f32),
            jax.ShapeDtypeStruct((3, spheres), f32),
        ),
        in_specs=[vmem] * 4,
        out_specs=(vmem, vmem),
        scratch_shapes=[pltpu.VMEM((owners, 6, clumps), f32)],
        compiler_params=params,
        name="sphere_velocities",
    )(velocities, swap_cores(velocities), sphere_offset, ids)


def solution(mesh):
    in_specs = (
        P(None, "space"),
        P(None, "space"),
        P(None, "space"),
        P(("space", "sub"), None),
        P(("space", "sub")),
        P("space"),
        P(None, "space"),
        P(None, "space"),
    )
    out_specs = (P(None, "space"), P(None, "space"))
    return jax.shard_map(
        per_device, mesh=mesh, in_specs=in_specs, out_specs=out_specs, check_vma=False
    )
```

```python
import functools
import math

import jax
import jax.numpy as jnp
from jax import lax
from jax.experimental import pallas as pl
from jax.experimental.pallas import tpu as pltpu
from jax.sharding import PartitionSpec as P

TILE = 128
SLOT = 256
UNROLL = 8
FIRST_MOVES = ((1, 0, 3, 2), (3, 2, 0, 1), (2, 3, 1, 0))
OTHER_MOVES = ((2, 3, 0, 1), (3, 0, 1, 2), (1, 2, 3, 0))
LANES = 16
BLOCK = TILE // LANES

support_radius = 0.5
press_coef = 4.0
visc_coef = 1.0
gravity_step = 0.1

f32 = jnp.float32
bf16 = jnp.bfloat16


def split_two(value):
    high = value.astype(bf16)
    return high, (value - high.astype(f32)).astype(bf16)


def split_three(value):
    high = value.astype(bf16).astype(f32)
    middle = (value - high).astype(bf16).astype(f32)
    return high, middle, (value - high) - middle


def cross(left, right):
    return [
        left[1] * right[2] - left[2] * right[1],
        left[2] * right[0] - left[0] * right[2],
        left[0] * right[1] - left[1] * right[0],
    ]


def group_of(owners):
    return math.gcd(owners, 16)


def loads_kernel(
    count_ref, list_hbm, fluid_hbm, sphere_hbm, offset_hbm, ids_hbm, state_hbm, inverse_hbm,
    keep_ref, send_ref,
    list_ref, fluid_ref, sphere_ref, offset_ref, ids_ref, state_ref, inverse_ref, arrived,
    place_ref, choose_ref, wide_ref, terms_ref, weight_ref, acc_ref,
):
    fluid_tiles = fluid_ref.shape[1] // TILE
    clumps = keep_ref.shape[1]
    owners = keep_ref.shape[0] // 3
    core = lax.axis_index("sub")
    me = jnp.where(core == 0, lax.axis_index("space"), -1)

    pairs = (
        (sphere_hbm, sphere_ref),
        (list_hbm, list_ref),
        (offset_hbm, offset_ref),
        (ids_hbm, ids_ref),
        (state_hbm, state_ref),
        (inverse_hbm, inverse_ref),
    )
    copies = [
        pltpu.make_async_copy(source, target, arrived.at[k]) for k, (source, target) in enumerate(pairs)
    ]
    blocks = fluid_tiles // BLOCK
    fluid_copies = []
    for block in range(blocks):
        cols = pl.ds(block * BLOCK * TILE, BLOCK * TILE)
        fluid_copies.append(
            pltpu.make_async_copy(fluid_hbm.at[:, cols], fluid_ref.at[:, cols], arrived.at[len(pairs) + block])
        )
    for copy in fluid_copies + copies:
        copy.start()

    acc_ref[...] = jnp.zeros_like(acc_ref)

    lane = lax.broadcasted_iota(jnp.int32, (TILE, 2 * TILE), 0)
    target = lax.broadcasted_iota(jnp.int32, (TILE, 2 * TILE), 1) // TILE
    part = lane % LANES
    wanted = (part == target) | (part == target + 3) | (part == target + 6)
    for j in range(BLOCK):
        choose_ref[j] = jnp.where(wanted & (lane // LANES == j), 1.0, 0.0).astype(bf16)

    for copy in fluid_copies:
        copy.wait()
    for block in range(blocks):
        row = lax.broadcasted_iota(jnp.int32, (8, TILE), 0)
        lines = []
        for j in range(BLOCK):
            tile = block * BLOCK + j
            state = fluid_ref[:, pl.ds(tile * TILE, TILE)]
            state = jnp.where(row < 3, state * (1.0 / support_radius) - 1.0, state)
            mass = state[7:8]
            first = jnp.where(row < 7, state * mass, state)
            second = jnp.where(row < 3, state * (mass * state[6:7]), 0.0)
            high, low = split_two(jnp.concatenate([first, second], axis=0))
            both = jnp.concatenate([high, low], axis=0)
            terms_ref[tile] = jnp.concatenate([both, both], axis=1)
            lines += [*split_three(state[0:3]), state[0:3], jnp.zeros((LANES - 12, TILE), f32)]
        turned = jnp.concatenate(lines, axis=0).T
        parts = turned.astype(bf16)
        for j in range(BLOCK):
            tile = block * BLOCK + j
            z = j * LANES + 11
            wide_ref[tile, :, 0 : 2 * TILE] = jnp.dot(parts, choose_ref[j], preferred_element_type=f32)
            wide_ref[tile, :, 2 * TILE :] = jnp.broadcast_to(turned[:, z : z + 1], (TILE, TILE))

    copies[0].wait()
    place_ref[...] = sphere_ref[0:3, :] * (1.0 / support_radius) - 1.0
    copies[1].wait()

    def pair_weights(slot, part):
        a = list_ref[0, slot]
        b = list_ref[1, slot]
        cols = pl.ds(pl.multiple_of(a * TILE, TILE), TILE)
        dx, dy, dz = [
            place_ref[k : k + 1, cols] - wide_ref[b, :, k * TILE : (k + 1) * TILE] for k in range(3)
        ]
        square = jnp.maximum(dx * dx + dy * dy + dz * dz, 1e-30)
        falloff = jnp.maximum(1.0 - square * lax.rsqrt(square), 0.0)
        high, low = split_two(falloff * falloff * falloff)
        weight_ref[part, 0:TILE, :] = high
        weight_ref[part, TILE:, :] = low

    def add_sums(slot, part, live):
        a = list_ref[0, slot]
        b = list_ref[1, slot]
        cols = pl.ds(pl.multiple_of(a * TILE, TILE), TILE)
        sums = jnp.dot(terms_ref[b], weight_ref[part], preferred_element_type=f32)
        acc_ref[:, cols] += live * (sums[0:16] + sums[16:32])

    count = count_ref[0]
    trips = (count + UNROLL - 1) // UNROLL
    last = list_ref.shape[1] - 1

    for part in range(UNROLL):
        pair_weights(min(part, last), part)

    @pl.loop(1, trips)
    def _(trip):
        for part in range(UNROLL):
            add_sums((trip - 1) * UNROLL + part, part, 1.0)
        for part in range(UNROLL):
            pair_weights(jnp.minimum(trip * UNROLL + part, last), part)

    for part in range(UNROLL):
        slot = (trips - 1) * UNROLL + part
        live = jnp.where(slot < count, 1.0, 0.0).astype(f32)
        add_sums(jnp.clip(slot, 0, last), part, live)

    for copy in copies[2:]:
        copy.wait()
    group = group_of(owners)
    width = group * SLOT

    row = lax.broadcasted_iota(jnp.int32, state_ref.shape, 0)
    still = state_ref[...] + jnp.where(row == 2, -gravity_step, 0.0)
    still = still / jnp.concatenate([inverse_ref[0:1, :]] * 3 + [inverse_ref[1:4, :]], axis=0)

    @pl.loop(0, owners // group)
    def _(block):
        cols = pl.ds(pl.multiple_of(block * width, width), width)
        acc = acc_ref[:, cols]
        place = place_ref[:, cols]
        sphere = sphere_ref[:, cols]
        offset = offset_ref[:, cols]
        total = acc[7:8]
        pull = total * place - acc[0:3]
        press = acc[6:7] * place - acc[8:11]
        scale = press_coef * support_radius
        force = scale * (sphere[6:7] * pull + press) + visc_coef * (acc[3:6] - total * sphere[3:6])
        force = [force[k : k + 1] for k in range(3)]
        turn = cross([offset[k : k + 1] for k in range(3)], force)
        loads = jnp.concatenate(force + turn + [jnp.zeros_like(force[0])] * 2, axis=0)
        high, low = split_two(loads)
        both = jnp.concatenate([high, low], axis=0)
        column = lax.broadcasted_iota(jnp.int32, (clumps, SLOT), 0)
        keep, send = [], []
        for k in range(group):
            here = pl.ds(pl.multiple_of(block * width + k * SLOT, SLOT), SLOT)
            one_hot = jnp.where(column == ids_ref[:, here], 1.0, 0.0).astype(bf16)
            sums = lax.dot_general(
                both[:, k * SLOT : (k + 1) * SLOT], one_hot, (((1,), (1,)), ((), ())),
                preferred_element_type=f32,
            )
            own = jnp.where(block * group + k == me, 1.0, 0.0).astype(f32)
            sums = (sums[0:8] + sums[8:16])[0:6] + own * still
            keep.append(jnp.where(core == 0, sums[0:3], sums[3:6]))
            send.append(jnp.where(core == 0, sums[3:6], sums[0:3]))
        here = pl.ds(pl.multiple_of(block * (3 * group), math.gcd(3 * group, 8)), 3 * group)
        keep_ref[here, :] = jnp.concatenate(keep, axis=0)
        send_ref[here, :] = jnp.concatenate(send, axis=0)


def first_kernel(keep_ref, arrived_ref, inverse_ref, out_ref):
    rows = keep_ref.shape[0]
    out_ref[0:rows, :] = keep_ref[...] + arrived_ref[...]
    linear = jnp.concatenate([inverse_ref[0:1, :]] * 3, axis=0)
    out_ref[rows:, :] = jnp.where(lax.axis_index("sub") == 0, linear, inverse_ref[1:4, :])


def sum_rows(refs, rows):
    sums = [ref[0:rows, :] for ref in refs]
    while len(sums) > 1:
        sums = [left + right for left, right in zip(sums[0::2], sums[1::2])]
    return sums[0]


def join_kernel(rows, *refs):
    *parts, out_ref = refs
    more = parts[0].shape[0] - rows
    out_ref[0:rows, :] = sum_rows(parts, rows)
    for k, ref in enumerate(parts):
        out_ref[rows + k * more : rows + (k + 1) * more, :] = ref[rows:, :]


def update_kernel(steps, *refs):
    *parts, out_ref, inverse_ref = refs
    owners = inverse_ref.shape[0]
    rows = 3 * owners
    held = owners // len(parts)
    me = lax.axis_index("space")
    holders = [0]
    for stride, moves in steps:
        radix = len(moves[0])
        here = me // stride % radix
        sources = [here]
        for move in moves:
            sources.append(sum(jnp.where(here == at, move.index(at), 0) for at in range(radix)))
        holders = [holder + source * stride for source in sources for holder in holders]
    for k, holder in enumerate(holders):
        first = rows + 3 * (k % held)
        inverse_ref[holder] = parts[k // held][first : first + 3, :]
    out_ref[...] = sum_rows(parts, rows) * jnp.concatenate([inverse_ref[k] for k in range(owners)], axis=0)


def velocity_kernel(mine_ref, arrived_ref, offset_ref, ids_ref, clump_ref, sphere_ref, velocity_ref):
    owners, _, clumps = velocity_ref.shape
    group = group_of(owners)
    core = lax.axis_index("sub")

    @pl.loop(0, owners // group)
    def _(block):
        rows = pl.ds(pl.multiple_of(block * (3 * group), math.gcd(3 * group, 8)), 3 * group)
        mine = mine_ref[rows, :]
        arrived = arrived_ref[rows, :]
        linear = jnp.where(core == 0, mine, arrived)
        angular = jnp.where(core == 0, arrived, mine)
        for k in range(group):
            owner = block * group + k
            three = slice(3 * k, 3 * k + 3)
            velocity = jnp.concatenate([linear[three], angular[three]], axis=0)
            velocity_ref[owner] = velocity
            both = jnp.concatenate(
                split_two(jnp.concatenate([velocity, jnp.zeros((2, clumps), f32)], axis=0)), axis=0
            )
            here = pl.ds(pl.multiple_of(owner * SLOT, SLOT), SLOT)
            column = lax.broadcasted_iota(jnp.int32, (clumps, SLOT), 0)
            one_hot = jnp.where(column == ids_ref[:, here], 1.0, 0.0).astype(bf16)
            picked = jnp.dot(both, one_hot, preferred_element_type=f32)
            picked = picked[0:8] + picked[8:16]
            offset = offset_ref[:, here]
            turn = cross([picked[3 + i : 4 + i] for i in range(3)], [offset[i : i + 1] for i in range(3)])
            sphere_ref[:, here] = picked[0:3] + jnp.concatenate(turn, axis=0)

    clump_ref[...] = velocity_ref[lax.axis_index("space")]


def swap_cores(value):
    return lax.ppermute(value, "sub", [(0, 1), (1, 0)])


def send(value, stride, move):
    pairs = []
    for chip in range(lax.axis_size("space")):
        digit = chip // stride % len(move)
        pairs.append((chip, chip + (move[digit] - digit) * stride))
    return lax.ppermute(value, "space", pairs)


def steps_of(owners):
    steps, stride = [], owners
    while stride > 1:
        radix = math.gcd(stride, 4)
        stride //= radix
        steps.append((stride, ((1, 0),) if radix == 2 else OTHER_MOVES if steps else FIRST_MOVES))
    return steps


def per_device(
    fluid_state, sphere_state, sphere_offset, tile_list, tile_count, clump_ids, clump_state, clump_inverse
):
    owners = lax.axis_size("space")
    spheres = sphere_state.shape[1]
    fluid = fluid_state.shape[1]
    clumps = clump_state.shape[1]
    slots = tile_list.shape[0]
    rows = 3 * owners
    ids = clump_ids.reshape(1, spheres)
    vmem = pl.BlockSpec(memory_space=pltpu.VMEM)
    hbm = pl.BlockSpec(memory_space=pltpu.HBM)
    params = pltpu.CompilerParams(vmem_limit_bytes=48 * 1024 * 1024)

    keep, give = pl.pallas_call(
        loads_kernel,
        out_shape=(pltpu.VMEM((rows, clumps), f32), pltpu.VMEM((rows, clumps), f32)),
        in_specs=[pl.BlockSpec(memory_space=pltpu.SMEM)] + [hbm] * 7,
        out_specs=(vmem, vmem),
        scratch_shapes=[
            pltpu.SMEM((2, slots), jnp.int32),
            pltpu.VMEM((8, fluid), f32),
            pltpu.VMEM((7, spheres), f32),
            pltpu.VMEM((3, spheres), f32),
            pltpu.VMEM((1, spheres), jnp.int32),
            pltpu.VMEM((6, clumps), f32),
            pltpu.VMEM((4, clumps), f32),
            pltpu.SemaphoreType.DMA((6 + fluid // (BLOCK * TILE),)),
            pltpu.VMEM((3, spheres), f32),
            pltpu.VMEM((BLOCK, TILE, 2 * TILE), bf16),
            pltpu.VMEM((fluid // TILE, TILE, 3 * TILE), f32),
            pltpu.VMEM((fluid // TILE, 32, 2 * TILE), bf16),
            pltpu.VMEM((UNROLL, 2 * TILE, TILE), bf16),
            pltpu.VMEM((16, spheres), f32),
        ],
        compiler_params=params,
        name="clump_loads",
    )(tile_count, *(
        pltpu.with_memory_space_constraint(value, pltpu.HBM)
        for value in (
            tile_list.T, fluid_state, sphere_state, sphere_offset, ids, clump_state, clump_inverse
        )
    ))

    def small(kernel, height, name, *operands, scratch=()):
        return pl.pallas_call(
            kernel,
            out_shape=pltpu.VMEM((height, clumps), f32),
            in_specs=[vmem] * len(operands),
            out_specs=vmem,
            scratch_shapes=scratch,
            compiler_params=params,
            name=name,
        )(*operands)

    mine = small(first_kernel, rows + 3, "core_sum", keep, swap_cores(give), clump_inverse)
    steps = steps_of(owners)
    for stride, moves in steps:
        parts = [mine] + [send(mine, stride, move) for move in moves]
        if stride > 1:
            height = rows + len(parts) * (mine.shape[0] - rows)
            mine = small(functools.partial(join_kernel, rows), height, "space_sum", *parts)
    velocities = small(
        functools.partial(update_kernel, steps), rows, "clump_update", *parts,
        scratch=[pltpu.VMEM((owners, 3, clumps), f32)],
    )

    return pl.pallas_call(
        velocity_kernel,
        out_shape=(
            jax.ShapeDtypeStruct((6, clumps), f32),
            jax.ShapeDtypeStruct((3, spheres), f32),
        ),
        in_specs=[vmem] * 4,
        out_specs=(vmem, vmem),
        scratch_shapes=[pltpu.VMEM((owners, 6, clumps), f32)],
        compiler_params=params,
        name="sphere_velocities",
    )(velocities, swap_cores(velocities), sphere_offset, ids)


def solution(mesh):
    in_specs = (
        P(None, "space"),
        P(None, "space"),
        P(None, "space"),
        P(("space", "sub"), None),
        P(("space", "sub")),
        P("space"),
        P(None, "space"),
        P(None, "space"),
    )
    out_specs = (P(None, "space"), P(None, "space"))
    return jax.shard_map(
        per_device, mesh=mesh, in_specs=in_specs, out_specs=out_specs, check_vma=False
    )
```
